32 devices in a mesh: pairs: 4 (over z), hours: 8 (over y, x, core).
Axes of the slice: x: 2, y: 2, z: 4, core: 2. Of those that a mesh axis runs over, the one named last changes fastest.
Arguments:
- spectra: bfloat16 [32, 16, 8, 2, 1024], P('pairs', 'hours'), may hold values from -6 to 6
- masks: int32 [32, 16, 8], P('pairs', 'hours'), may hold values 0 or 1
- pair_rows: int32 [48, 2], P('pairs'), may hold values from 0 to 31, as said below
- start_basis: float32 [4, 2048], replicated, may hold values from -6 to 6
Outputs:
- window_stacks: float32 [48, 16, 2048], P('pairs', 'hours')
- stack: float32 [48, 2048], P('pairs', 'hours')
- basis: float32 [48, 4, 2048], P('pairs', None, 'hours')
The draws below stay inside these ranges and needn't reach their ends.
Inputs may be any that keep to these rules, and one draw needn't show every extreme that they name: pair_rows[p, 0] is a station of group p // 12, the group being stations 8 * i to 8 * i + 7 for group i; pair_rows[p, 1] is another station of that group or a station of the group just before or just after it, counted around all groups; each block of 12 rows has pairs with all three of these groups, and its pairs reach exactly 4 distinct stations of the group just before and exactly 4 of the group just after.
All inputs are finite; a program needn't handle non-finite values. No bound on the sum of `masks` on one device may be relied on, other than what follows from the above.
Results may differ from the reference program's by a relative error of at most 0.0064.
Values may be sent and summed in bfloat16 or wider, within the bound.
No kernel may reach another device: no remote copies, remote signals or barrier semaphores. Data moves between devices by JAX's collectives and lax.ppermute only.
A program may use at most 64 MiB of HBM per device.

```python
import math
import jax
import jax.numpy as jnp
from jax import lax

STA_DEV = 8
PAIR_DEV = 12
SEG = 8
FREQ = 1024
LAGS = 2048
BAND = 64
RANK = 4
TURNS = 2
STATIONS = 32
PAIRS = 48
WINDOWS = 16


def draw_pair_rows(key, part):
    groups = STATIONS // STA_DEV
    near = STA_DEV // 2
    row = jnp.arange(PAIRS, dtype=jnp.int32)
    block = row // PAIR_DEV
    within = row % PAIR_DEV
    keys = jax.random.split(key, 7)
    role_perm = jax.vmap(lambda k: jax.random.permutation(k, PAIR_DEV))(jax.random.split(keys[0], groups)).astype(jnp.int32)
    left_perm = jax.vmap(lambda k: jax.random.permutation(k, STA_DEV))(jax.random.split(keys[1], groups)).astype(jnp.int32)
    right_perm = jax.vmap(lambda k: jax.random.permutation(k, STA_DEV))(jax.random.split(keys[2], groups)).astype(jnp.int32)
    role = role_perm[block, within]
    first_local = jax.random.randint(keys[3], (PAIRS,), 0, STA_DEV, dtype=jnp.int32)
    drawn = jax.random.randint(keys[4], (PAIRS,), -1, 2, dtype=jnp.int32)
    pick = jax.random.randint(keys[5], (PAIRS,), 0, near, dtype=jnp.int32)
    stride = jax.random.randint(keys[6], (PAIRS,), 1, STA_DEV, dtype=jnp.int32)
    offset = jnp.where(role < near, -1, jnp.where(role < 2 * near, 1, jnp.where(role == 2 * near, 0, drawn)))
    slot = jnp.where(role < near, role, jnp.where(role < 2 * near, role - near, pick))
    slot = jnp.clip(slot, 0, near - 1)
    neighbour_local = jnp.where(offset < 0, left_perm[block, slot], right_perm[block, slot])
    second_local = jnp.where(offset == 0, jnp.mod(first_local + stride, STA_DEV), neighbour_local)
    second_group = jnp.mod(block + offset, groups)
    first = block * STA_DEV + first_local
    second = second_group * STA_DEV + second_local
    return jnp.stack([first, second], 1).astype(jnp.int32)


def touch_ends(array, rng, low, largest):
    dims = array.shape
    spot = [jax.random.randint(jax.random.fold_in(rng, axis), (), 0, dims[axis]) for axis in range(len(dims))]
    array = array.at[tuple(spot)].set(low)
    longest = dims.index(max(dims))
    spot[longest] = (spot[longest] + 1) % dims[longest]
    return array.at[tuple(spot)].set(largest)


def steps_of(own_key, extent, shards, low, top_value):
    gain, own = 1.0, jax.random.fold_in(own_key, 6)
    for position, shards_of in shards:
        steps = jnp.exp(jax.random.uniform(jax.random.fold_in(own, position), (shards_of,), jnp.float32, low / len(shards), top_value / len(shards)))
        gain = gain * jnp.repeat(steps, extent[position] // shards_of).reshape([-1 if axis == position else 1 for axis in range(len(extent))])
    return gain


def normal_values(own_key, dims, deviation, most, pieces=(), held_as=jnp.bfloat16):
    values = deviation * jax.random.normal(own_key, dims, jnp.float32)
    if pieces:
        values = values * steps_of(own_key, dims, pieces, -0.22, 0.18)
    return jnp.clip(values, -most, most).astype(held_as)


def setup_inputs(seed: int = 0) -> dict:
    splits = jax.random.split(jax.random.key(seed), 5)
    return {
        "spectra": normal_values(splits[0], (STATIONS, WINDOWS, SEG, 2, FREQ), 1.0, 6.0, ((0, 4), (1, 8))),
        "masks": touch_ends((jax.random.randint(splits[1], (STATIONS, WINDOWS, SEG), 0, 8) < 7).astype(jnp.int32), jax.random.fold_in(splits[1], 1), 0, 1),
        "pair_rows": draw_pair_rows(jax.random.fold_in(splits[4], 71), 0),
        "start_basis": normal_values(splits[3], (RANK, LAGS), 1.0, 6.0, (), jnp.float32),
    }


HIGH = lax.Precision.HIGHEST

def whiten(spectra, masks):
    values = spectra.astype(jnp.float32)
    shape = values.shape
    banded = values.reshape(shape[:-1] + (shape[-1] // BAND, BAND))
    power = lax.optimization_barrier(jnp.mean(banded * banded, axis=(3, 5), keepdims=True))
    scaled = banded * lax.rsqrt(power + 1e-06) * masks.astype(jnp.float32)[:, :, :, None, None, None]
    return scaled.reshape(shape).astype(jnp.bfloat16)

def kernel_table(freq, lags):
    nfft = 2 * lags
    bins = jnp.arange(1, freq + 1, dtype=jnp.int32)[:, None]
    shifts = jnp.arange(lags, dtype=jnp.int32)[None, :] - lags // 2
    phase = jnp.mod(bins * shifts, nfft).astype(jnp.float32) * (2.0 * math.pi / nfft)
    scale = freq ** (-0.5)
    return jnp.concatenate([jnp.cos(phase) * scale, -jnp.sin(phase) * scale], 0).astype(jnp.bfloat16)

def cross_spectra(first, second):
    a_re = first[..., 0, :].astype(jnp.float32)
    a_im = first[..., 1, :].astype(jnp.float32)
    b_re = second[..., 0, :].astype(jnp.float32)
    b_im = second[..., 1, :].astype(jnp.float32)
    real_part = a_re * b_re + a_im * b_im
    imag_part = a_im * b_re - a_re * b_im
    return jnp.concatenate([real_part, imag_part], -1).astype(jnp.bfloat16)

def from_gram(vectors, gram):
    rank = vectors.shape[-2]
    lower = [[None] * rank for index in range(rank)]
    for row in range(rank):
        for col in range(row + 1):
            total = gram[..., row, col]
            for inner in range(col):
                total = total - lower[row][inner] * lower[col][inner]
            if row == col:
                lower[row][row] = jnp.sqrt(total)
            else:
                lower[row][col] = total / lower[col][col]
    result = []
    for row in range(rank):
        current = vectors[..., row, :]
        for inner in range(row):
            current = current - lower[row][inner][..., None] * result[inner]
        result.append(current / lower[row][row][..., None])
    return jnp.stack(result, -2)

def orthonormal(vectors):
    gram = jnp.einsum('...il,...jl->...ij', vectors, vectors, precision=HIGH)
    return from_gram(vectors, gram)

def power_step(basis, corr):
    proj = jnp.einsum('wrl,wgl->wrg', basis, corr, precision=HIGH)
    back = jnp.einsum('wrg,wgl->wrl', proj, corr, precision=HIGH)
    return back + float(LAGS) * basis

def reference(spectra, masks, pair_rows, start_basis):
    whitened = whiten(spectra, masks)
    table = kernel_table(FREQ, LAGS).astype(jnp.float32)

    def per_pair(rows):
        first = whitened[rows[0]]
        second = whitened[rows[1]]
        cross = cross_spectra(first, second).astype(jnp.float32)
        corr = jnp.dot(cross.reshape(WINDOWS * SEG, 2 * FREQ), table, precision=HIGH)
        corr = corr.reshape(WINDOWS, SEG, LAGS)
        basis_now = jnp.broadcast_to(start_basis, (WINDOWS, RANK, LAGS)).astype(jnp.float32)
        for turn in range(TURNS):
            basis_now = orthonormal(power_step(basis_now, corr))
        final_terms = power_step(basis_now, corr)
        summed = lax.optimization_barrier(jnp.sum(corr, axis=1))
        coef = jnp.einsum('wl,wrl->wr', summed, basis_now, precision=HIGH)
        windows = jnp.einsum('wr,wrl->wl', coef, basis_now, precision=HIGH) / math.sqrt(SEG)
        merged = lax.optimization_barrier(jnp.sum(final_terms, axis=0))
        stack = lax.optimization_barrier(jnp.sum(windows, axis=0)) / math.sqrt(WINDOWS)
        basis = math.sqrt(LAGS) * orthonormal(merged)
        return (windows, stack, basis)
    window_stacks, stack, basis = lax.map(per_pair, pair_rows)
    return (window_stacks, stack, basis)
```

```python
import functools
import math

import jax
import jax.numpy as jnp
import numpy as np
from jax import lax
from jax.experimental import pallas as pl
from jax.experimental.pallas import tpu as pltpu
from jax.sharding import PartitionSpec as P

BAND = 64
TURNS = 2
NEAR = 4
F32 = jnp.float32
BF16 = jnp.bfloat16
VMEM = pl.BlockSpec(memory_space=pltpu.VMEM)
SMEM = pl.BlockSpec(memory_space=pltpu.SMEM)
HEAD = 128
LANE = 16


def kernel_table(freq, lags):
    nfft = 2 * lags
    bins = np.arange(1, freq + 1, dtype=np.int64)[:, None]
    shifts = np.arange(lags, dtype=np.int64)[None, :] - lags // 2
    phase = np.mod(bins * shifts, nfft).astype(np.float64) * (2.0 * math.pi / nfft)
    scale = freq ** (-0.5)
    table = np.concatenate([np.cos(phase) * scale, -np.sin(phase) * scale], 0)
    return table.astype(np.float32).astype(jnp.bfloat16)


def pick_matrix(pairs, seg, rank):
    pick = np.zeros((HEAD, 2 * HEAD), np.float32)
    side = (seg + rank) * LANE
    for pair in range(pairs):
        for part in range(seg):
            pick[pair * seg + part, part * LANE + pair] = 1
            pick[pair * seg + part, side + pair] = 1
    for row in range(rank):
        pick[pairs * seg + row, (seg + row) * LANE : (seg + row + 1) * LANE] = 1
    return pick.astype(jnp.bfloat16)


def spread_matrix(pairs, seg, rank):
    spread = np.zeros((HEAD, (rank + 1) * HEAD), np.float32)
    for row in range(rank + 1):
        for part in range(seg):
            for pair in range(pairs):
                spread[row * LANE + part, row * HEAD + pair * seg + part] = 1
        for other in range(rank):
            spread[row * LANE + seg + other, row * HEAD + pairs * seg + other] = 1
    return spread.astype(jnp.bfloat16)


def two_parts(values):
    high = values.astype(BF16)
    return high, (values - high.astype(F32)).astype(BF16)


def three_parts(values):
    high = values.astype(BF16)
    rest = values - high.astype(F32)
    mid = rest.astype(BF16)
    return high, mid, (rest - mid.astype(F32)).astype(BF16)


def dot(left, right):
    return jnp.dot(left, right, preferred_element_type=F32)


def dot_rows(left, right):
    return lax.dot_general(left, right, (((1,), (1,)), ((), ())), preferred_element_type=F32)


def lower_factor(gram, rank):
    lower = [[None] * rank for _ in range(rank)]
    inverse = [None] * rank
    for row in range(rank):
        for col in range(row + 1):
            total = gram[row][col]
            for inner in range(col):
                total = total - lower[row][inner] * lower[col][inner]
            if row == col:
                inverse[row] = lax.rsqrt(total)
                lower[row][row] = total * inverse[row]
            else:
                lower[row][col] = total * inverse[col]
    return lower, inverse


def solve_rows(rows, lower, inverse):
    result = []
    for row, current in enumerate(rows):
        for inner in range(row):
            current = current - lower[row][inner] * result[inner]
        result.append(current * inverse[row])
    return result


def select_kernel(stations, place, before, after, *refs):
    windows = len(refs) // 3
    whitened, to_next, to_last = refs[:windows], refs[windows : 2 * windows], refs[2 * windows :]
    low = place[0] * stations
    for rows, outs in ((after, to_next), (before, to_last)):
        needed = jnp.int32(0)
        for row in range(rows.shape[0]):
            local = rows[row, 1] - low
            here = jnp.logical_and(local >= 0, local < stations)
            bit = jnp.left_shift(jnp.int32(1), jnp.clip(local, 0, stations - 1))
            needed = jnp.where(here, jnp.bitwise_or(needed, bit), needed)
        slot = jnp.int32(0)
        for station in range(stations):
            wanted = jnp.bitwise_and(jnp.right_shift(needed, station), 1)
            spot = jnp.minimum(slot, NEAR - 1)

            @pl.when(wanted == 1)
            def _():
                for source, target in zip(whitened, outs):
                    target[spot] = source[station]

            slot = slot + wanted


def window_kernel(sizes, index, own, low, high, table, start, pick, spread, *refs):
    pairs, seg, rank, lags, freq, total_windows, slices, first_window = sizes
    rows = pairs * seg
    if first_window:
        win_out, merged_out, near, cross, vectors, high_part, low_part = refs
    else:
        (core, partial, win_out, send_out, keep_out, near, cross, vectors, high_part, low_part, pieces) = refs
    stations = own.shape[0]
    near[0:NEAR] = low[...]
    near[NEAR : NEAR + stations] = own[...]
    near[NEAR + stations :] = high[...]
    for pair in range(0, pairs, 2):
        real, imag = [], []
        for one in (pair, pair + 1):
            a = near[NEAR + index[0, one]].astype(F32)
            b = near[index[1, one]].astype(F32)
            a_re, a_im, b_re, b_im = a[:seg], a[seg:], b[:seg], b[seg:]
            real.append(a_re * b_re + a_im * b_im)
            imag.append(a_im * b_re - a_re * b_im)
        block = pl.ds(pair * seg, 2 * seg)
        cross[block, 0:freq] = jnp.concatenate(real, 0).astype(BF16)
        cross[block, freq:] = jnp.concatenate(imag, 0).astype(BF16)
    vectors[rows : rows + rank] = start[...]
    vectors[rows + rank :] = jnp.zeros((HEAD - rows - rank, lags), F32)
    step = 512
    for at in range(0, lags, step):
        vectors[0:rows, at : at + step] = dot(cross[...], table[:, at : at + step])
    every = vectors[...]
    high_part[...] = every.astype(BF16)
    low_part[...] = (every - high_part[...].astype(F32)).astype(BF16)
    gram = dot_rows(high_part[...], high_part[...])
    side = dot_rows(low_part[...], high_part[...])
    gram = gram + side + side.T
    lane = lax.broadcasted_iota(jnp.int32, (seg, HEAD), 1)
    sub = lax.broadcasted_iota(jnp.int32, (seg, HEAD), 0)
    blocks = jnp.zeros((seg, HEAD), F32)
    for pair in range(pairs):
        blocks = blocks + jnp.where(lane // seg == pair, gram[pair * seg : (pair + 1) * seg], 0.0)
    basis_rows = gram[rows : rows + 8]
    turned = [
        jnp.where(lane % seg == sub, jnp.broadcast_to(basis_rows[row : row + 1], (seg, HEAD)), 0.0)
        for row in range(rank)
    ]
    stacked = jnp.concatenate([blocks, basis_rows] + turned, 0)
    count = stacked.shape[0]
    moved = dot(jnp.concatenate(three_parts(stacked), 0), pick[...])
    moved = moved[0:count] + moved[count : 2 * count] + moved[2 * count :]
    products = [moved[0:16, k * LANE : (k + 1) * LANE] for k in range(seg)]
    side_at = (seg + rank) * LANE
    for row in range(rank):
        upper = moved[16 + row * seg : 16 + (row + 1) * seg, side_at : side_at + LANE]
        under = moved[8:16, (seg + row) * LANE : (seg + row + 1) * LANE]
        products.append(jnp.concatenate([upper, under], 0))
    level = lax.broadcasted_iota(jnp.int32, (16, LANE), 0)
    of_corr = level < seg
    known = [jnp.where(level == seg + row, 1.0, 0.0) for row in range(rank)]
    reach = [jnp.where(of_corr, products[seg + row], 0.0) for row in range(rank)]
    for turn in range(TURNS):
        known = [known[r] + reach[r] * (1.0 / lags) for r in range(rank)]
        images = []
        for r in range(rank):
            image = known[r][0:1] * products[0]
            for k in range(1, seg + rank):
                image = image + known[r][k : k + 1] * products[k]
            images.append(image)
        inner = [
            [jnp.sum(images[r] * known[s], 0, keepdims=True) for s in range(r + 1)] for r in range(rank)
        ]
        lower, inverse = lower_factor(inner, rank)
        known = solve_rows(known, lower, inverse)
        reach = [jnp.where(of_corr, v, 0.0) for v in solve_rows(images, lower, inverse)]
    outs = [reach[r] + float(lags) * known[r] for r in range(rank)]
    window = jnp.zeros_like(known[0])
    for r in range(rank):
        window = window + jnp.sum(reach[r], 0, keepdims=True) * known[r]
    outs.append(window * (1.0 / math.sqrt(seg)))
    coefs = jnp.concatenate(outs + [jnp.zeros((HEAD - (rank + 1) * 16, LANE), F32)], 0)
    coefs = jnp.concatenate([coefs, jnp.zeros((HEAD, HEAD - LANE), F32)], 1).T[0:LANE]
    wide = dot(jnp.concatenate(two_parts(coefs), 0), spread[...])
    wide = wide[0:LANE] + wide[LANE:]
    row_of = lax.broadcasted_iota(jnp.int32, (LANE, HEAD), 0)
    lane_of = lax.broadcasted_iota(jnp.int32, (LANE, HEAD), 1)
    mine = jnp.logical_or(lane_of // seg == row_of, lane_of >= rows)
    weights = [
        jnp.where(mine, wide[:, r * HEAD : (r + 1) * HEAD], 0.0)[0:pairs] for r in range(rank + 1)
    ]
    filled = (rank + 1) * pairs
    height = -(-filled // 16) * 16
    weights = jnp.concatenate(weights + [jnp.zeros((height - filled, HEAD), F32)], 0)
    w_high, w_low = two_parts(weights)
    both = jnp.concatenate([w_high, w_low], 0)
    scale = 1.0 / math.sqrt(total_windows)
    width = lags // slices
    top = rank * pairs
    for at in range(0, lags, step):
        part = dot(both, high_part[:, at : at + step])
        result = part[0:height] + part[height:] + dot(w_high, low_part[:, at : at + step])
        win_out[:, at : at + step] = result[top:filled]
        result = jnp.concatenate([result[0:top], result[top:] * scale], 0)
        if first_window:
            merged_out[:, at : at + step] = result
        else:
            result = result + partial[:, at : at + step]
            for piece in range(at // width, (at + step) // width):
                pieces[piece] = result[:, piece * width - at : (piece + 1) * width - at]
    if not first_window:
        for piece in range(slices // 2):
            send_out[piece] = pieces[2 * piece + 1 - core[0]].astype(BF16)
            keep_out[piece] = pieces[2 * piece + core[0]]


def add_kernel(chip, keep, got, mine_out, *sends):
    mine_out[...] = keep[chip[0]] + got[chip[0]].astype(F32)
    for step, out in enumerate(sends):
        other = jnp.bitwise_xor(chip[0], step + 1)
        out[...] = (keep[other] + got[other].astype(F32)).astype(BF16)


def gram_kernel(pairs, rank, mine, *refs):
    got, (total_out, gram_out) = refs[:-2], refs[-2:]
    total = mine[...]
    for one in got:
        total = total + one[...].astype(F32)
    total_out[...] = total
    rows = [total[r * pairs : (r + 1) * pairs] for r in range(rank)]
    lane = lax.broadcasted_iota(jnp.int32, (pairs, 128), 1)
    gram = jnp.zeros((pairs, 128), F32)
    for r in range(rank):
        for s in range(r + 1):
            gram = jnp.where(lane == r * rank + s, jnp.sum(rows[r] * rows[s], 1, keepdims=True), gram)
    gram_out[...] = gram


def finish_kernel(pairs, rank, lags, total, *refs):
    grams, (stack_out, basis_out) = refs[:-2], refs[-2:]
    gram = grams[0][...]
    for one in grams[1:]:
        gram = gram + one[...]
    entries = [[gram[:, r * rank + s : r * rank + s + 1] for s in range(r + 1)] for r in range(rank)]
    lower, inverse = lower_factor(entries, rank)
    rows = [total[r * pairs : (r + 1) * pairs] for r in range(rank)]
    for r, row in enumerate(solve_rows(rows, lower, inverse)):
        basis_out[:, r, :] = row * math.sqrt(lags)
    stack_out[...] = total[rank * pairs : (rank + 1) * pairs]


def call(kernel, out_shape, in_specs, out_specs, scratch=(), flops=0, moved=0):
    return pl.pallas_call(
        kernel,
        out_shape=out_shape,
        in_specs=in_specs,
        out_specs=out_specs,
        scratch_shapes=list(scratch),
        compiler_params=pltpu.CompilerParams(vmem_limit_bytes=32 * 1024 * 1024),
        cost_estimate=pl.CostEstimate(flops=flops, bytes_accessed=moved, transcendentals=0),
    )


def struct(shape, dtype=F32):
    return jax.ShapeDtypeStruct(shape, dtype)


def whiten(spectra, masks):
    values = spectra.astype(F32)
    shape = values.shape
    banded = values.reshape(shape[:-1] + (shape[-1] // BAND, BAND))
    power = jnp.mean(banded * banded, axis=(3, 5), keepdims=True)
    scaled = banded * lax.rsqrt(power + 1e-06) * masks.astype(F32)[:, :, :, None, None, None]
    whitened = scaled.reshape(shape).astype(BF16).transpose(0, 1, 3, 2, 4)
    shape = whitened.shape
    whitened = whitened.reshape(shape[0], shape[1], shape[2] * shape[3], shape[4])
    return [whitened[:, w] for w in range(shape[1])]


def pair_index(pair_rows, stations, group_index, groups):
    first, second = pair_rows[:, 0], pair_rows[:, 1]
    local = jnp.mod(second, stations)
    relative = jnp.mod(second // stations - group_index + 1, groups)
    number = jnp.arange(stations, dtype=jnp.int32)

    def slot(side):
        used = jnp.logical_and(relative[:, None] == side, local[:, None] == number[None, :])
        used = jnp.any(used, 0)
        return jnp.sum(jnp.where(jnp.logical_and(used[None, :], number[None, :] < local[:, None]), 1, 0), 1)

    spot = jnp.where(
        relative == 0, slot(0), jnp.where(relative == 1, NEAR + local, NEAR + stations + slot(2))
    )
    return jnp.stack([jnp.mod(first, stations), spot]).astype(jnp.int32)


def on_device(spectra, masks, pair_rows, start_basis):
    stations, windows, seg, parts, freq = spectra.shape
    rank, lags = start_basis.shape
    pairs = pair_rows.shape[0]
    groups = lax.axis_size("pairs")
    group_index = lax.axis_index("pairs")
    slices = lax.axis_size("hours")
    hour = lax.axis_index("hours")
    width = lags // slices
    chips = slices // 2
    forward = [(i, (i + 1) % groups) for i in range(groups)]
    backward = [(target, source) for source, target in forward]
    before = lax.ppermute(pair_rows, "pairs", forward)
    after = lax.ppermute(pair_rows, "pairs", backward)
    whitened = whiten(spectra, masks)
    index = pair_index(pair_rows, stations, group_index, groups)
    block = struct((NEAR, parts * seg, freq), BF16)
    sends = call(
        functools.partial(select_kernel, stations),
        [block] * (2 * windows),
        [SMEM] * 3 + [VMEM] * windows,
        [VMEM] * (2 * windows),
    )(group_index.reshape(1).astype(jnp.int32), before, after, *whitened)
    lows = [lax.ppermute(sends[w], "pairs", forward) for w in range(windows)]
    highs = [lax.ppermute(sends[windows + w], "pairs", backward) for w in range(windows)]
    table = jnp.asarray(kernel_table(freq, lags))
    pick = jnp.asarray(pick_matrix(pairs, seg, rank))
    spread = jnp.asarray(spread_matrix(pairs, seg, rank))
    core = jnp.mod(hour, 2).reshape(1).astype(jnp.int32)
    chip = (hour // 2).reshape(1).astype(jnp.int32)
    height = -(-(rank + 1) * pairs // 16) * 16
    total_windows = windows * slices
    partial, stacks = None, []
    for w in range(windows):
        last = w == windows - 1
        sizes = (pairs, seg, rank, lags, freq, total_windows, slices, w == 0)
        scratch = [
            pltpu.VMEM((stations + 2 * NEAR, parts * seg, freq), BF16),
            pltpu.VMEM((pairs * seg, parts * freq), BF16),
            pltpu.VMEM((HEAD, lags), F32),
            pltpu.VMEM((HEAD, lags), BF16),
            pltpu.VMEM((HEAD, lags), BF16),
        ]
        args = [index, whitened[w], lows[w], highs[w], table, start_basis, pick, spread]
        specs = [SMEM] + [VMEM] * 7
        outs = [struct((pairs, lags))]
        if w == 0:
            outs.append(struct((height, lags)))
        else:
            args += [core, partial]
            specs += [SMEM, VMEM]
            outs += [struct((chips, height, width), BF16), struct((chips, height, width))]
            scratch.append(pltpu.VMEM((slices, height, width), F32))
        result = call(
            functools.partial(window_kernel, sizes),
            outs,
            specs,
            [VMEM] * len(outs),
            scratch,
            flops=2 * pairs * seg * parts * freq * lags,
            moved=parts * freq * lags * 2,
        )(*args)
        stacks.append(result[0])
        if w == 0:
            partial = result[1]
        else:
            send, keep = result[1:]
    window_stacks = jnp.stack(stacks, 1)
    swap = lambda value, step: lax.ppermute(value, "hours", [(k, k ^ step) for k in range(slices)])
    got = swap(send, 1)
    piece = struct((height, width))
    pieces = call(
        add_kernel,
        [piece] + [struct((height, width), BF16)] * (chips - 1),
        [SMEM, VMEM, VMEM],
        [VMEM] * chips,
    )(chip, keep, got)
    arrived = [swap(one, 2 * (step + 1)) for step, one in enumerate(pieces[1:])]
    total, gram = call(
        functools.partial(gram_kernel, pairs, rank),
        [piece, struct((pairs, 128))],
        [VMEM] * chips,
        [VMEM] * 2,
    )(pieces[0], *arrived)
    gram = gram + swap(gram, 1)
    grams = [gram] + [swap(gram, 2 * (step + 1)) for step in range(chips - 1)]
    stack, basis = call(
        functools.partial(finish_kernel, pairs, rank, lags),
        [struct((pairs, width)), struct((pairs, rank, width))],
        [VMEM] * (chips + 1),
        [VMEM] * 2,
    )(total, *grams)
    return (window_stacks, stack, basis)


def solution(mesh):
    in_specs = (
        P("pairs", "hours", None, None, None),
        P("pairs", "hours", None),
        P("pairs", None),
        P(),
    )
    out_specs = (P("pairs", "hours", None), P("pairs", "hours"), P("pairs", None, "hours"))
    return jax.shard_map(
        on_device, mesh=mesh, in_specs=in_specs, out_specs=out_specs, check_vma=False
    )
```

```python
import functools
import math

import jax
import jax.numpy as jnp
import numpy as np
from jax import lax
from jax.experimental import pallas as pl
from jax.experimental.pallas import tpu as pltpu
from jax.sharding import PartitionSpec as P

BAND = 64
TURNS = 2
NEAR = 4
F32 = jnp.float32
BF16 = jnp.bfloat16
VMEM = pl.BlockSpec(memory_space=pltpu.VMEM)
SMEM = pl.BlockSpec(memory_space=pltpu.SMEM)
HBM = pl.BlockSpec(memory_space=pltpu.HBM)
HEAD = 128
LANE = 16


def kernel_table(freq, lags):
    nfft = 2 * lags
    bins = np.arange(1, freq + 1, dtype=np.int64)[:, None]
    shifts = np.arange(lags, dtype=np.int64)[None, :] - lags // 2
    phase = np.mod(bins * shifts, nfft).astype(np.float64) * (2.0 * math.pi / nfft)
    scale = freq ** (-0.5)
    table = np.concatenate([np.cos(phase) * scale, -np.sin(phase) * scale], 0)
    return table.astype(np.float32).astype(jnp.bfloat16)


def pick_matrix(pairs, seg, rank):
    pick = np.zeros((HEAD, 2 * HEAD), np.float32)
    side = (seg + rank) * LANE
    for pair in range(pairs):
        for part in range(seg):
            pick[pair * seg + part, part * LANE + pair] = 1
            pick[pair * seg + part, side + pair] = 1
    for row in range(rank):
        pick[pairs * seg + row, (seg + row) * LANE : (seg + row + 1) * LANE] = 1
    return pick.astype(jnp.bfloat16)


def spread_matrix(pairs, seg, rank):
    spread = np.zeros((HEAD, (rank + 1) * HEAD), np.float32)
    for row in range(rank + 1):
        for part in range(seg):
            for pair in range(pairs):
                spread[row * LANE + part, row * HEAD + pair * seg + part] = 1
        for other in range(rank):
            spread[row * LANE + seg + other, row * HEAD + pairs * seg + other] = 1
    return spread.astype(jnp.bfloat16)


def two_parts(values):
    high = values.astype(BF16)
    return high, (values - high.astype(F32)).astype(BF16)


def three_parts(values):
    high = values.astype(BF16)
    rest = values - high.astype(F32)
    mid = rest.astype(BF16)
    return high, mid, (rest - mid.astype(F32)).astype(BF16)


def dot(left, right):
    return jnp.dot(left, right, preferred_element_type=F32)


def dot_rows(left, right):
    return lax.dot_general(left, right, (((1,), (1,)), ((), ())), preferred_element_type=F32)


def lower_factor(gram, rank):
    lower = [[None] * rank for _ in range(rank)]
    inverse = [None] * rank
    for row in range(rank):
        for col in range(row + 1):
            total = gram[row][col]
            for inner in range(col):
                total = total - lower[row][inner] * lower[col][inner]
            if row == col:
                inverse[row] = lax.rsqrt(total)
                lower[row][row] = total * inverse[row]
            else:
                lower[row][col] = total * inverse[col]
    return lower, inverse


def solve_rows(rows, lower, inverse):
    result = []
    for row, current in enumerate(rows):
        for inner in range(row):
            current = current - lower[row][inner] * result[inner]
        result.append(current * inverse[row])
    return result


def popcount(bits):
    bits = bits - jnp.bitwise_and(jnp.right_shift(bits, 1), 0x55555555)
    bits = jnp.bitwise_and(bits, 0x33333333) + jnp.bitwise_and(jnp.right_shift(bits, 2), 0x33333333)
    bits = jnp.bitwise_and(bits + jnp.right_shift(bits, 4), 0x0F0F0F0F)
    bits = bits + jnp.right_shift(bits, 8)
    return jnp.bitwise_and(bits + jnp.right_shift(bits, 16), 63)


def used_stations(rows, low, stations):
    used = jnp.int32(0)
    for pair in range(rows.shape[1]):
        local = rows[1, pair] - low
        here = jnp.logical_and(local >= 0, local < stations)
        bit = jnp.left_shift(jnp.int32(1), jnp.clip(local, 0, stations - 1))
        used = jnp.bitwise_or(used, jnp.where(here, bit, 0))
    return used


def stage_kernel(*refs):
    count = (len(refs) - 2) // 2
    sources, targets, sems = refs[1 : 1 + count], refs[1 + count : -1], refs[-1]
    copies = [
        pltpu.make_async_copy(source, target, sems.at[number])
        for number, (source, target) in enumerate(zip(sources, targets))
    ]
    for copy in copies:
        copy.start()
    for copy in copies:
        copy.wait()


def whiten_kernel(groups, place, far_rows, far_spectra, far_masks, index, *refs):
    whitened, (spectra, masks, rows, sems) = refs[:-4], refs[-4:]
    copies = [
        pltpu.make_async_copy(far_spectra, spectra, sems.at[0]),
        pltpu.make_async_copy(far_masks, masks, sems.at[1]),
        pltpu.make_async_copy(far_rows, rows, sems.at[2]),
    ]
    for copy in copies:
        copy.start()
    stations, windows, seg, _, freq = spectra.shape
    count = freq // BAND
    band = lax.broadcasted_iota(jnp.int32, (count, freq), 0)
    of_bin = lax.broadcasted_iota(jnp.int32, (count, freq), 1) // BAND
    bands = jnp.where(band == of_bin, 1.0, 0.0).astype(BF16)
    for copy in copies:
        copy.wait()
    before = lax.rem(place[0] + groups - 1, groups) * stations
    after = lax.rem(place[0] + 1, groups) * stations
    own = place[0] * stations
    used_before = used_stations(rows, before, stations)
    used_after = used_stations(rows, after, stations)
    for pair in range(rows.shape[1]):
        index[0, pair] = rows[0, pair] - own
        second = rows[1, pair]
        in_before = jnp.logical_and(second >= before, second < before + stations)
        in_own = jnp.logical_and(second >= own, second < own + stations)
        local = second - jnp.where(in_before, before, jnp.where(in_own, own, after))
        below = jnp.left_shift(jnp.int32(1), local) - 1
        slot = popcount(jnp.bitwise_and(jnp.where(in_before, used_before, used_after), below))
        index[1, pair] = jnp.where(
            in_before, slot, jnp.where(in_own, NEAR + local, NEAR + stations + slot)
        )
    values, squares, open_rows = [], [], []
    eye = lax.broadcasted_iota(jnp.int32, (seg, seg), 0) == lax.broadcasted_iota(jnp.int32, (seg, seg), 1)
    for station in range(stations):
        for window in range(windows):
            block = spectra[station, window].astype(F32)
            real, imag = block[:, 0], block[:, 1]
            values.append((real, imag))
            squares.append(real * real + imag * imag)
            mask = masks[station, window : window + 1].astype(F32)
            mask = jnp.where(eye, jnp.broadcast_to(mask, (seg, seg)), 0.0)
            open_rows.append(jnp.sum(mask, 1, keepdims=True))
    high, low = two_parts(jnp.concatenate(squares, 0))
    power = dot_rows(high, bands) + dot_rows(low, bands)
    scale = lax.rsqrt(power * (1.0 / (2 * BAND)) + 1e-06) * jnp.concatenate(open_rows, 0)
    high, low = two_parts(scale)
    scale = dot(high, bands) + dot(low, bands)
    at = 0
    for station in range(stations):
        for window in range(windows):
            real, imag = values[at]
            here = scale[at * seg : (at + 1) * seg]
            whitened[window][station] = jnp.concatenate([real * here, imag * here], 0).astype(BF16)
            at += 1


def select_kernel(stations, place, rows, *refs):
    windows = len(refs) // 2
    needed = used_stations(rows, place[0] * stations, stations)
    slot = jnp.int32(0)
    for station in range(stations):
        wanted = jnp.bitwise_and(jnp.right_shift(needed, station), 1)
        spot = jnp.minimum(slot, NEAR - 1)

        @pl.when(wanted == 1)
        def _():
            for source, target in zip(refs[:windows], refs[windows:]):
                target[spot] = source[station]

        slot = slot + wanted


def window_kernel(sizes, index, own, low, high, table, start, pick, spread, *refs):
    pairs, seg, rank, lags, freq, total_windows, slices, first_window = sizes
    rows = pairs * seg
    if first_window:
        win_out, merged_out, near, cross, vectors, high_part, low_part = refs
    else:
        (core, partial, win_out, send_out, keep_out, near, cross, vectors, high_part, low_part, pieces) = refs
    stations = own.shape[0]
    near[0:NEAR] = low[...]
    near[NEAR : NEAR + stations] = own[...]
    near[NEAR + stations :] = high[...]
    for pair in range(0, pairs, 2):
        real, imag = [], []
        for one in (pair, pair + 1):
            a = near[NEAR + index[0, one]].astype(F32)
            b = near[index[1, one]].astype(F32)
            a_re, a_im, b_re, b_im = a[:seg], a[seg:], b[:seg], b[seg:]
            real.append(a_re * b_re + a_im * b_im)
            imag.append(a_im * b_re - a_re * b_im)
        block = pl.ds(pair * seg, 2 * seg)
        cross[block, 0:freq] = jnp.concatenate(real, 0).astype(BF16)
        cross[block, freq:] = jnp.concatenate(imag, 0).astype(BF16)
    vectors[rows : rows + rank] = start[...]
    vectors[rows + rank :] = jnp.zeros((HEAD - rows - rank, lags), F32)
    step = 512
    for at in range(0, lags, step):
        vectors[0:rows, at : at + step] = dot(cross[...], table[:, at : at + step])
    every = vectors[...]
    high_part[...] = every.astype(BF16)
    low_part[...] = (every - high_part[...].astype(F32)).astype(BF16)
    gram = dot_rows(high_part[...], high_part[...])
    side = dot_rows(low_part[...], high_part[...])
    gram = gram + side + side.T
    lane = lax.broadcasted_iota(jnp.int32, (seg, HEAD), 1)
    sub = lax.broadcasted_iota(jnp.int32, (seg, HEAD), 0)
    blocks = jnp.zeros((seg, HEAD), F32)
    for pair in range(pairs):
        blocks = blocks + jnp.where(lane // seg == pair, gram[pair * seg : (pair + 1) * seg], 0.0)
    basis_rows = gram[rows : rows + 8]
    turned = [
        jnp.where(lane % seg == sub, jnp.broadcast_to(basis_rows[row : row + 1], (seg, HEAD)), 0.0)
        for row in range(rank)
    ]
    stacked = jnp.concatenate([blocks, basis_rows] + turned, 0)
    count = stacked.shape[0]
    moved = dot(jnp.concatenate(three_parts(stacked), 0), pick[...])
    moved = moved[0:count] + moved[count : 2 * count] + moved[2 * count :]
    products = [moved[0:16, k * LANE : (k + 1) * LANE] for k in range(seg)]
    side_at = (seg + rank) * LANE
    for row in range(rank):
        upper = moved[16 + row * seg : 16 + (row + 1) * seg, side_at : side_at + LANE]
        under = moved[8:16, (seg + row) * LANE : (seg + row + 1) * LANE]
        products.append(jnp.concatenate([upper, under], 0))
    level = lax.broadcasted_iota(jnp.int32, (16, LANE), 0)
    of_corr = level < seg
    known = [jnp.where(level == seg + row, 1.0, 0.0) for row in range(rank)]
    reach = [jnp.where(of_corr, products[seg + row], 0.0) for row in range(rank)]
    for turn in range(TURNS):
        known = [known[r] + reach[r] * (1.0 / lags) for r in range(rank)]
        images = []
        for r in range(rank):
            image = known[r][0:1] * products[0]
            for k in range(1, seg + rank):
                image = image + known[r][k : k + 1] * products[k]
            images.append(image)
        inner = [
            [jnp.sum(images[r] * known[s], 0, keepdims=True) for s in range(r + 1)] for r in range(rank)
        ]
        lower, inverse = lower_factor(inner, rank)
        known = solve_rows(known, lower, inverse)
        reach = [jnp.where(of_corr, v, 0.0) for v in solve_rows(images, lower, inverse)]
    outs = [reach[r] + float(lags) * known[r] for r in range(rank)]
    window = jnp.zeros_like(known[0])
    for r in range(rank):
        window = window + jnp.sum(reach[r], 0, keepdims=True) * known[r]
    outs.append(window * (1.0 / math.sqrt(seg)))
    coefs = jnp.concatenate(outs + [jnp.zeros((HEAD - (rank + 1) * 16, LANE), F32)], 0)
    coefs = jnp.concatenate([coefs, jnp.zeros((HEAD, HEAD - LANE), F32)], 1).T[0:LANE]
    wide = dot(jnp.concatenate(two_parts(coefs), 0), spread[...])
    wide = wide[0:LANE] + wide[LANE:]
    row_of = lax.broadcasted_iota(jnp.int32, (LANE, HEAD), 0)
    lane_of = lax.broadcasted_iota(jnp.int32, (LANE, HEAD), 1)
    mine = jnp.logical_or(lane_of // seg == row_of, lane_of >= rows)
    weights = [
        jnp.where(mine, wide[:, r * HEAD : (r + 1) * HEAD], 0.0)[0:pairs] for r in range(rank + 1)
    ]
    filled = (rank + 1) * pairs
    height = -(-filled // 16) * 16
    weights = jnp.concatenate(weights + [jnp.zeros((height - filled, HEAD), F32)], 0)
    w_high, w_low = two_parts(weights)
    both = jnp.concatenate([w_high, w_low], 0)
    scale = 1.0 / math.sqrt(total_windows)
    width = lags // slices
    top = rank * pairs
    for at in range(0, lags, step):
        part = dot(both, high_part[:, at : at + step])
        result = part[0:height] + part[height:] + dot(w_high, low_part[:, at : at + step])
        win_out[:, at : at + step] = result[top:filled]
        result = jnp.concatenate([result[0:top], result[top:] * scale], 0)
        if first_window:
            merged_out[:, at : at + step] = result
        else:
            result = result + partial[:, at : at + step]
            for piece in range(at // width, (at + step) // width):
                pieces[piece] = result[:, piece * width - at : (piece + 1) * width - at]
    if not first_window:
        for piece in range(slices // 2):
            send_out[piece] = pieces[2 * piece + 1 - core[0]].astype(BF16)
            keep_out[piece] = pieces[2 * piece + core[0]]


def add_kernel(top, chip, keep, got, mine_out, *sends):
    chips, height, _ = keep.shape
    for part in range(chips):
        both = keep[part] + got[part].astype(F32)
        mine_out[part] = both
        short = both[0:top].astype(BF16)
        for out in sends:
            out[part * top : (part + 1) * top] = short
    for step, out in enumerate(sends):
        other = jnp.bitwise_xor(chip[0], step + 1)
        out[chips * top :] = mine_out[other, top:height].astype(BF16)


def gram_kernel(pairs, rank, chip, mine, *refs):
    got, (total_out, gram_out, parts) = refs[:-3], refs[-3:]
    chips, height, width = mine.shape
    top = rank * pairs
    sums = [[jnp.zeros((pairs, width), F32) for _ in range(r + 1)] for r in range(rank)]
    for part in range(chips):
        block = mine[part, 0:top].astype(BF16).astype(F32)
        for one in got:
            block = block + one[part * top : (part + 1) * top].astype(F32)
        parts[part] = block
        rows = [block[r * pairs : (r + 1) * pairs] for r in range(rank)]
        sums = [[sums[r][s] + rows[r] * rows[s] for s in range(r + 1)] for r in range(rank)]
    stack = mine[chip[0], top:height]
    for one in got:
        stack = stack + one[chips * top :].astype(F32)
    total_out[0:top] = parts[chip[0]]
    total_out[top:] = stack
    lane = lax.broadcasted_iota(jnp.int32, (pairs, 128), 1)
    gram = jnp.zeros((pairs, 128), F32)
    for r in range(rank):
        for s in range(r + 1):
            value = jnp.sum(sums[r][s], 1, keepdims=True)
            gram = jnp.where(lane == r * rank + s, value, gram)
    gram_out[...] = gram


def finish_kernel(pairs, rank, lags, total, mine, got, stack_out, basis_out):
    gram = mine[...] + got[...]
    shape = (pairs, total.shape[1])
    entries = [
        [jnp.broadcast_to(gram[:, r * rank + s : r * rank + s + 1], shape) for s in range(r + 1)]
        for r in range(rank)
    ]
    lower, inverse = lower_factor(entries, rank)
    rows = [total[r * pairs : (r + 1) * pairs] for r in range(rank)]
    for r, row in enumerate(solve_rows(rows, lower, inverse)):
        basis_out[:, r, :] = row * math.sqrt(lags)
    stack_out[...] = total[rank * pairs : (rank + 1) * pairs]


def call(kernel, out_shape, in_specs, out_specs, scratch=(), flops=0, moved=0):
    return pl.pallas_call(
        kernel,
        out_shape=out_shape,
        in_specs=in_specs,
        out_specs=out_specs,
        scratch_shapes=list(scratch),
        compiler_params=pltpu.CompilerParams(vmem_limit_bytes=12 * 1024 * 1024),
        cost_estimate=pl.CostEstimate(flops=flops, bytes_accessed=moved, transcendentals=0),
    )


def far(value):
    return pltpu.with_memory_space_constraint(value, pltpu.HBM)


def struct(shape, dtype=F32):
    return jax.ShapeDtypeStruct(shape, dtype)


def on_device(spectra, masks, pair_rows, start_basis):
    stations, windows, seg, parts, freq = spectra.shape
    rank, lags = start_basis.shape
    pairs = pair_rows.shape[0]
    groups = lax.axis_size("pairs")
    group_index = lax.axis_index("pairs")
    slices = lax.axis_size("hours")
    hour = lax.axis_index("hours")
    width = lags // slices
    chips = slices // 2
    forward = [(i, (i + 1) % groups) for i in range(groups)]
    backward = [(target, source) for source, target in forward]
    rows = pair_rows.T
    before = lax.ppermute(rows, "pairs", forward)
    after = lax.ppermute(rows, "pairs", backward)
    place = group_index.reshape(1).astype(jnp.int32)
    index, *whitened = call(
        functools.partial(whiten_kernel, groups),
        [struct(rows.shape, jnp.int32)] + [struct((stations, parts * seg, freq), BF16)] * windows,
        [SMEM, HBM, HBM, HBM],
        [SMEM] + [VMEM] * windows,
        [
            pltpu.VMEM(spectra.shape, BF16),
            pltpu.VMEM(masks.shape, jnp.int32),
            pltpu.SMEM(rows.shape, jnp.int32),
            pltpu.SemaphoreType.DMA((3,)),
        ],
    )(place, far(rows), far(spectra), far(masks))
    block = struct((NEAR, parts * seg, freq), BF16)
    def select(wanted):
        return call(
            functools.partial(select_kernel, stations),
            [block] * windows,
            [SMEM] * 2 + [VMEM] * windows,
            [VMEM] * windows,
        )(place, wanted, *whitened)

    to_next, to_last = select(after), select(before)
    lows = [lax.ppermute(one, "pairs", forward) for one in to_next]
    highs = [lax.ppermute(one, "pairs", backward) for one in to_last]
    fixed = [
        jnp.asarray(kernel_table(freq, lags)),
        start_basis,
        jnp.asarray(pick_matrix(pairs, seg, rank)),
        jnp.asarray(spread_matrix(pairs, seg, rank)),
    ]
    table, start, pick, spread = call(
        stage_kernel,
        [struct(one.shape, one.dtype) for one in fixed],
        [VMEM] + [HBM] * len(fixed),
        [VMEM] * len(fixed),
        [pltpu.SemaphoreType.DMA((len(fixed),))],
        moved=parts * freq * lags * 2,
    )(to_last[0], *[far(one) for one in fixed])
    core = jnp.mod(hour, 2).reshape(1).astype(jnp.int32)
    chip = (hour // 2).reshape(1).astype(jnp.int32)
    height = -(-(rank + 1) * pairs // 16) * 16
    total_windows = windows * slices
    partial, stacks = None, []
    for w in range(windows):
        last = w == windows - 1
        sizes = (pairs, seg, rank, lags, freq, total_windows, slices, w == 0)
        scratch = [
            pltpu.VMEM((stations + 2 * NEAR, parts * seg, freq), BF16),
            pltpu.VMEM((pairs * seg, parts * freq), BF16),
            pltpu.VMEM((HEAD, lags), F32),
            pltpu.VMEM((HEAD, lags), BF16),
            pltpu.VMEM((HEAD, lags), BF16),
        ]
        args = [index, whitened[w], lows[w], highs[w], table, start, pick, spread]
        specs = [SMEM] + [VMEM] * 7
        outs = [struct((pairs, lags))]
        if w == 0:
            outs.append(struct((height, lags)))
        else:
            args += [core, partial]
            specs += [SMEM, VMEM]
            outs += [struct((chips, height, width), BF16), struct((chips, height, width))]
            scratch.append(pltpu.VMEM((slices, height, width), F32))
        result = call(
            functools.partial(window_kernel, sizes),
            outs,
            specs,
            [VMEM] * len(outs),
            scratch,
            flops=2 * pairs * seg * parts * freq * lags,
            moved=parts * freq * lags * 2,
        )(*args)
        stacks.append(result[0])
        if w == 0:
            partial = result[1]
        else:
            send, keep = result[1:]
    window_stacks = jnp.stack(stacks, 1)
    swap = lambda value, step: lax.ppermute(value, "hours", [(k, k ^ step) for k in range(slices)])
    got = swap(send, 1)
    top = rank * pairs
    message = struct((chips * top + height - top, width), BF16)
    mine, *sends = call(
        functools.partial(add_kernel, top),
        [struct(keep.shape)] + [message] * (chips - 1),
        [SMEM, VMEM, VMEM],
        [VMEM] * chips,
    )(chip, keep, got)
    arrived = [swap(one, 2 * (step + 1)) for step, one in enumerate(sends)]
    total, gram = call(
        functools.partial(gram_kernel, pairs, rank),
        [struct((height, width)), struct((pairs, 128))],
        [SMEM] + [VMEM] * chips,
        [VMEM] * 2,
        [pltpu.VMEM((chips, top, width), F32)],
    )(chip, mine, *arrived)
    stack, basis = call(
        functools.partial(finish_kernel, pairs, rank, lags),
        [struct((pairs, width)), struct((pairs, rank, width))],
        [VMEM] * 3,
        [VMEM] * 2,
    )(total, gram, swap(gram, 1))
    return (window_stacks, stack, basis)


def solution(mesh):
    in_specs = (
        P("pairs", "hours", None, None, None),
        P("pairs", "hours", None),
        P("pairs", None),
        P(),
    )
    out_specs = (P("pairs", "hours", None), P("pairs", "hours"), P("pairs", None, "hours"))
    return jax.shard_map(
        on_device, mesh=mesh, in_specs=in_specs, out_specs=out_specs, check_vma=False
    )
```

```python
import functools
import math

import jax
import jax.numpy as jnp
import numpy as np
from jax import lax
from jax.experimental import pallas as pl
from jax.experimental.pallas import tpu as pltpu
from jax.sharding import PartitionSpec as P

BAND = 64
TURNS = 2
NEAR = 4
F32 = jnp.float32
BF16 = jnp.bfloat16
VMEM = pl.BlockSpec(memory_space=pltpu.VMEM)
SMEM = pl.BlockSpec(memory_space=pltpu.SMEM)
HBM = pl.BlockSpec(memory_space=pltpu.HBM)
HEAD = 128
LANE = 16


def kernel_table(freq, lags):
    nfft = 2 * lags
    bins = np.arange(1, freq + 1, dtype=np.int64)[:, None]
    shifts = np.append(np.arange(lags // 2, dtype=np.int64), -(lags // 2))[None, :]
    phase = np.mod(bins * shifts, nfft).astype(np.float64) * (2.0 * math.pi / nfft)
    scale = freq ** (-0.5)
    both = np.concatenate([np.cos(phase) * scale, -np.sin(phase) * scale], 0)
    both = both.astype(np.float32).astype(jnp.bfloat16)
    ends = both[:, -1].astype(np.float32).reshape(2, freq)
    return both[:, :-1], ends


def pick_matrix(pairs, seg, rank):
    pick = np.zeros((HEAD, 2 * HEAD), np.float32)
    side = (seg + rank) * LANE
    for pair in range(pairs):
        for part in range(seg):
            pick[pair * seg + part, part * LANE + pair] = 1
            pick[pair * seg + part, side + pair] = 1
    for row in range(rank):
        pick[pairs * seg + row, (seg + row) * LANE : (seg + row + 1) * LANE] = 1
    return pick.astype(jnp.bfloat16)


def spread_matrix(pairs, seg, rank):
    spread = np.zeros((HEAD, (rank + 1) * HEAD), np.float32)
    for row in range(rank + 1):
        for part in range(seg):
            for pair in range(pairs):
                spread[row * LANE + part, row * HEAD + pair * seg + part] = 1
        for other in range(rank):
            spread[row * LANE + seg + other, row * HEAD + pairs * seg + other] = 1
    return spread.astype(jnp.bfloat16)


def two_parts(values):
    high = values.astype(BF16)
    return high, (values - high.astype(F32)).astype(BF16)


def three_parts(values):
    high = values.astype(BF16)
    rest = values - high.astype(F32)
    mid = rest.astype(BF16)
    return high, mid, (rest - mid.astype(F32)).astype(BF16)


def dot(left, right):
    return jnp.dot(left, right, preferred_element_type=F32)


def dot_rows(left, right):
    return lax.dot_general(left, right, (((1,), (1,)), ((), ())), preferred_element_type=F32)


def lower_factor(gram, rank):
    lower = [[None] * rank for _ in range(rank)]
    inverse = [None] * rank
    for row in range(rank):
        for col in range(row + 1):
            total = gram[row][col]
            for inner in range(col):
                total = total - lower[row][inner] * lower[col][inner]
            if row == col:
                inverse[row] = lax.rsqrt(total)
                lower[row][row] = total * inverse[row]
            else:
                lower[row][col] = total * inverse[col]
    return lower, inverse


def solve_rows(rows, lower, inverse):
    result = []
    for row, current in enumerate(rows):
        for inner in range(row):
            current = current - lower[row][inner] * result[inner]
        result.append(current * inverse[row])
    return result


def used_stations(second, low, stations):
    number = lax.broadcasted_iota(jnp.int32, (stations, second.shape[1]), 0)
    return jnp.max(jnp.where(second == low + number, 1.0, 0.0), 1, keepdims=True)


def flip(values):
    rows, width = values.shape
    back = 127 - lax.broadcasted_iota(jnp.int32, (rows, 128), 1)
    turned = []
    for at in range(width - 128, -1, -128):
        turned.append(jnp.take_along_axis(values[:, at : at + 128], back, axis=1))
    return jnp.concatenate(turned, 1)


def first_lane(values, first, other):
    lane = lax.broadcasted_iota(jnp.int32, values, 1)
    return jnp.where(lane == 0, first, other)


def unfold(even, odd):
    shape = even.shape
    root = math.sqrt(2.0)
    right = first_lane(shape, even * root, even + odd)
    left = first_lane(shape, odd * root, even - odd)
    return flip(pltpu.roll(left, shape[1] - 1, 1)), right


def stage_kernel(*refs):
    count = (len(refs) - 3) // 2
    sources, targets, natural, sems = refs[1 : 1 + count], refs[1 + count : -2], refs[-2], refs[-1]
    copies = [
        pltpu.make_async_copy(source, target, sems.at[number])
        for number, (source, target) in enumerate(zip(sources, (natural, *targets[1:])))
    ]
    for copy in copies:
        copy.start()
    copies[0].wait()
    values = natural[...]
    half = values.shape[1] // 2
    right = values[:, half:]
    left = pltpu.roll(flip(values[:, :half]), 1, 1)
    shape = right.shape
    root = math.sqrt(0.5)
    targets[0][:, :half] = first_lane(shape, right * root, (right + left) * 0.5)
    targets[0][:, half:] = first_lane(shape, left * root, (right - left) * 0.5)
    for copy in copies[1:]:
        copy.wait()


def whiten_kernel(groups, place, far_rows, far_spectra, far_masks, index, *refs):
    whitened, (spectra, masks, rows, sems) = refs[:-4], refs[-4:]
    copies = [
        pltpu.make_async_copy(far_spectra, spectra, sems.at[0]),
        pltpu.make_async_copy(far_masks, masks, sems.at[1]),
        pltpu.make_async_copy(far_rows, rows, sems.at[2]),
    ]
    for copy in copies:
        copy.start()
    stations, windows, seg, _, freq = spectra.shape
    count = freq // BAND
    band = lax.broadcasted_iota(jnp.int32, (count, freq), 0)
    of_bin = lax.broadcasted_iota(jnp.int32, (count, freq), 1) // BAND
    bands = jnp.where(band == of_bin, 1.0, 0.0).astype(BF16)
    before = lax.rem(place[0] + groups - 1, groups) * stations
    after = lax.rem(place[0] + 1, groups) * stations
    own = place[0] * stations
    for copy in copies:
        copy.wait()
    second = rows[1:2]
    in_before = jnp.logical_and(second >= before, second < before + stations)
    in_own = jnp.logical_and(second >= own, second < own + stations)
    local = second - jnp.where(in_before, before, jnp.where(in_own, own, after))
    below = lax.broadcasted_iota(jnp.int32, (stations, second.shape[1]), 0) < local
    slots = [
        jnp.sum(jnp.where(below, used_stations(second, low, stations), 0.0), 0, keepdims=True)
        for low in (before, after)
    ]
    spot = jnp.where(in_own, NEAR + local, NEAR + stations + slots[1].astype(jnp.int32))
    index[0:1] = rows[0:1] - own
    index[1:2] = jnp.where(in_before, slots[0].astype(jnp.int32), spot)
    values, squares, open_rows = [], [], []
    eye = lax.broadcasted_iota(jnp.int32, (seg, seg), 0) == lax.broadcasted_iota(jnp.int32, (seg, seg), 1)
    for station in range(stations):
        for window in range(windows):
            block = spectra[station, window].astype(F32)
            real, imag = block[:, 0], block[:, 1]
            values.append((real, imag))
            squares.append(real * real + imag * imag)
            mask = masks[station, window : window + 1].astype(F32)
            mask = jnp.where(eye, jnp.broadcast_to(mask, (seg, seg)), 0.0)
            open_rows.append(jnp.sum(mask, 1, keepdims=True))
    high, low = two_parts(jnp.concatenate(squares, 0))
    power = dot_rows(high, bands) + dot_rows(low, bands)
    scale = lax.rsqrt(power * (1.0 / (2 * BAND)) + 1e-06) * jnp.concatenate(open_rows, 0)
    high, low = two_parts(scale)
    scale = dot(high, bands) + dot(low, bands)
    at = 0
    for station in range(stations):
        for window in range(windows):
            real, imag = values[at]
            here = scale[at * seg : (at + 1) * seg]
            whitened[window][station] = jnp.concatenate([real * here, imag * here], 0).astype(BF16)
            at += 1


def select_kernel(stations, place, rows, *refs):
    windows = len(refs) // 2
    used = used_stations(rows[1:2], place[0] * stations, stations)
    weight = jnp.left_shift(1, lax.broadcasted_iota(jnp.int32, (stations, 1), 0)).astype(F32)
    needed = jnp.sum(used * weight).astype(jnp.int32)
    slot = jnp.int32(0)
    for station in range(stations):
        wanted = jnp.bitwise_and(jnp.right_shift(needed, station), 1)
        spot = jnp.minimum(slot, NEAR - 1)

        @pl.when(wanted == 1)
        def _():
            for source, target in zip(refs[:windows], refs[windows:]):
                target[spot] = source[station]

        slot = slot + wanted


def window_kernel(sizes, index, own, low, high, start, table, ends, pick, spread, *refs):
    pairs, seg, rank, lags, freq, total_windows, slices, first_window = sizes
    rows = pairs * seg
    if first_window:
        win_out, merged_out, near, cross, vectors, high_part, low_part = refs
    else:
        (core, partial, win_out, send_out, keep_out, near, cross, vectors, high_part, low_part, pieces) = refs
    stations = own.shape[0]
    half = lags // 2
    picked = index[...]
    near[0:NEAR] = low[...]
    near[NEAR : NEAR + stations] = own[...]
    near[NEAR + stations :] = high[...]
    edges = []
    for pair in range(0, pairs, 2):
        real, imag = [], []
        for one in (pair, pair + 1):
            a = own[picked[0, one]].astype(F32)
            b = near[picked[1, one]].astype(F32)
            a_re, a_im, b_re, b_im = a[:seg], a[seg:], b[:seg], b[seg:]
            real.append(a_re * b_re + a_im * b_im)
            imag.append(a_im * b_re - a_re * b_im)
        block = pl.ds(pair * seg, 2 * seg)
        real = jnp.concatenate(real, 0).astype(BF16)
        imag = jnp.concatenate(imag, 0).astype(BF16)
        cross[block, 0:freq] = real
        cross[block, freq:] = imag
        last = real.astype(F32) * ends[0:1] + imag.astype(F32) * ends[1:2]
        edges.append(jnp.sum(last, 1, keepdims=True))
    vectors[rows : rows + rank] = start[...]
    vectors[rows + rank :] = jnp.zeros((HEAD - rows - rank, lags), F32)
    step = 512
    for at in range(0, half, step):
        vectors[0:rows, at : at + step] = dot(cross[:, 0:freq], table[0:freq, at : at + step])
        vectors[0:rows, half + at : half + at + step] = dot(cross[:, freq:], table[freq:, at : at + step])
    shape = (rows, 128)
    root = math.sqrt(0.5)
    column = vectors[0:rows, 0:128]
    vectors[0:rows, 0:128] = first_lane(shape, column * root, column)
    edge = jnp.broadcast_to(jnp.concatenate(edges, 0) * root, shape)
    vectors[0:rows, half : half + 128] = first_lane(shape, edge, vectors[0:rows, half : half + 128])
    every = vectors[...]
    high_part[...] = every.astype(BF16)
    low_part[...] = (every - high_part[...].astype(F32)).astype(BF16)
    gram = dot_rows(high_part[...], high_part[...])
    side = dot_rows(low_part[...], high_part[...])
    gram = 2.0 * (gram + side + side.T)
    lane = lax.broadcasted_iota(jnp.int32, (seg, HEAD), 1)
    sub = lax.broadcasted_iota(jnp.int32, (seg, HEAD), 0)
    blocks = jnp.zeros((seg, HEAD), F32)
    for pair in range(pairs):
        blocks = blocks + jnp.where(lane // seg == pair, gram[pair * seg : (pair + 1) * seg], 0.0)
    basis_rows = gram[rows : rows + 8]
    turned = [
        jnp.where(lane % seg == sub, jnp.broadcast_to(basis_rows[row : row + 1], (seg, HEAD)), 0.0)
        for row in range(rank)
    ]
    stacked = jnp.concatenate([blocks, basis_rows] + turned, 0)
    count = stacked.shape[0]
    moved = dot(jnp.concatenate(three_parts(stacked), 0), pick[...])
    moved = moved[0:count] + moved[count : 2 * count] + moved[2 * count :]
    products = [moved[0:16, k * LANE : (k + 1) * LANE] for k in range(seg)]
    side_at = (seg + rank) * LANE
    for row in range(rank):
        upper = moved[16 + row * seg : 16 + (row + 1) * seg, side_at : side_at + LANE]
        under = moved[8:16, (seg + row) * LANE : (seg + row + 1) * LANE]
        products.append(jnp.concatenate([upper, under], 0))
    level = lax.broadcasted_iota(jnp.int32, (16, LANE), 0)
    of_corr = level < seg
    known = [jnp.where(level == seg + row, 1.0, 0.0) for row in range(rank)]
    reach = [jnp.where(of_corr, products[seg + row], 0.0) for row in range(rank)]
    for turn in range(TURNS):
        known = [known[r] + reach[r] * (1.0 / lags) for r in range(rank)]
        images = []
        for r in range(rank):
            image = known[r][0:1] * products[0]
            for k in range(1, seg + rank):
                image = image + known[r][k : k + 1] * products[k]
            images.append(image)
        inner = [
            [jnp.sum(images[r] * known[s], 0, keepdims=True) for s in range(r + 1)] for r in range(rank)
        ]
        lower, inverse = lower_factor(inner, rank)
        known = solve_rows(known, lower, inverse)
        reach = [jnp.where(of_corr, v, 0.0) for v in solve_rows(images, lower, inverse)]
    outs = [reach[r] + float(lags) * known[r] for r in range(rank)]
    window = jnp.zeros_like(known[0])
    for r in range(rank):
        window = window + jnp.sum(reach[r], 0, keepdims=True) * known[r]
    outs.append(window * (1.0 / math.sqrt(seg)))
    coefs = jnp.concatenate(outs + [jnp.zeros((HEAD - (rank + 1) * 16, LANE), F32)], 0)
    coefs = jnp.concatenate([coefs, jnp.zeros((HEAD, HEAD - LANE), F32)], 1).T[0:LANE]
    wide = dot(jnp.concatenate(two_parts(coefs), 0), spread[...])
    wide = wide[0:LANE] + wide[LANE:]
    row_of = lax.broadcasted_iota(jnp.int32, (LANE, HEAD), 0)
    lane_of = lax.broadcasted_iota(jnp.int32, (LANE, HEAD), 1)
    mine = jnp.logical_or(lane_of // seg == row_of, lane_of >= rows)
    weights = [
        jnp.where(mine, wide[:, r * HEAD : (r + 1) * HEAD], 0.0)[0:pairs] for r in range(rank + 1)
    ]
    filled = (rank + 1) * pairs
    height = -(-filled // 16) * 16
    weights = jnp.concatenate(weights + [jnp.zeros((height - filled, HEAD), F32)], 0)
    w_high, w_low = two_parts(weights)
    both = jnp.concatenate([w_high, w_low], 0)
    scale = 1.0 / math.sqrt(total_windows)
    width = lags // slices
    top = rank * pairs

    def combined(at):
        part = dot(both, high_part[:, at : at + step])
        return part[0:height] + part[height:] + dot(w_high, low_part[:, at : at + step])

    result = [jnp.concatenate([combined(side + at) for at in range(0, half, step)], 1) for side in (0, half)]
    left, right = unfold(*[one[top:] for one in result])
    win_out[:, 0:half] = left[0:pairs]
    win_out[:, half:] = right[0:pairs]
    result = [jnp.concatenate([one[0:top], one[top:] * scale], 0) for one in result]
    if first_window:
        merged_out[:, 0:half] = result[0]
        merged_out[:, half:] = result[1]
    else:
        left, right = unfold(result[0] + partial[:, 0:half], result[1] + partial[:, half:])
        for piece in range(slices // 2):
            pieces[piece] = left[:, piece * width : (piece + 1) * width]
            pieces[slices // 2 + piece] = right[:, piece * width : (piece + 1) * width]
    if not first_window:
        for piece in range(slices // 2):
            send_out[piece] = pieces[2 * piece + 1 - core[0]].astype(BF16)
            keep_out[piece] = pieces[2 * piece + core[0]]


def add_kernel(top, chip, keep, got, mine_out, *sends):
    chips, height, _ = keep.shape
    for part in range(chips):
        both = keep[part] + got[part].astype(F32)
        mine_out[part] = both
        short = both[0:top].astype(BF16)
        for out in sends:
            out[part * top : (part + 1) * top] = short
    for step, out in enumerate(sends):
        other = jnp.bitwise_xor(chip[0], step + 1)
        out[chips * top :] = mine_out[other, top:height].astype(BF16)


def gram_kernel(pairs, rank, chip, mine, *refs):
    got, (total_out, gram_out, parts) = refs[:-3], refs[-3:]
    chips, height, width = mine.shape
    top = rank * pairs
    sums = [[jnp.zeros((pairs, width), F32) for _ in range(r + 1)] for r in range(rank)]
    for part in range(chips):
        block = mine[part, 0:top].astype(BF16).astype(F32)
        for one in got:
            block = block + one[part * top : (part + 1) * top].astype(F32)
        parts[part] = block
        rows = [block[r * pairs : (r + 1) * pairs] for r in range(rank)]
        sums = [[sums[r][s] + rows[r] * rows[s] for s in range(r + 1)] for r in range(rank)]
    stack = mine[chip[0], top:height]
    for one in got:
        stack = stack + one[chips * top :].astype(F32)
    total_out[0:top] = parts[chip[0]]
    total_out[top:] = stack
    lane = lax.broadcasted_iota(jnp.int32, (pairs, 128), 1)
    gram = jnp.zeros((pairs, 128), F32)
    for r in range(rank):
        for s in range(r + 1):
            value = jnp.sum(sums[r][s], 1, keepdims=True)
            gram = jnp.where(lane == r * rank + s, value, gram)
    gram_out[...] = gram


def finish_kernel(pairs, rank, lags, total, mine, got, stack_out, basis_out):
    gram = mine[...] + got[...]
    shape = (pairs, total.shape[1])
    entries = [
        [jnp.broadcast_to(gram[:, r * rank + s : r * rank + s + 1], shape) for s in range(r + 1)]
        for r in range(rank)
    ]
    lower, inverse = lower_factor(entries, rank)
    rows = [total[r * pairs : (r + 1) * pairs] for r in range(rank)]
    for r, row in enumerate(solve_rows(rows, lower, inverse)):
        basis_out[:, r, :] = row * math.sqrt(lags)
    stack_out[...] = total[rank * pairs : (rank + 1) * pairs]


def call(kernel, out_shape, in_specs, out_specs, scratch=(), flops=0, moved=0):
    return pl.pallas_call(
        kernel,
        out_shape=out_shape,
        in_specs=in_specs,
        out_specs=out_specs,
        scratch_shapes=list(scratch),
        compiler_params=pltpu.CompilerParams(vmem_limit_bytes=12 * 1024 * 1024),
        cost_estimate=pl.CostEstimate(flops=flops, bytes_accessed=moved, transcendentals=0),
    )


def far(value):
    return pltpu.with_memory_space_constraint(value, pltpu.HBM)


def struct(shape, dtype=F32):
    return jax.ShapeDtypeStruct(shape, dtype)


def on_device(spectra, masks, pair_rows, start_basis):
    stations, windows, seg, parts, freq = spectra.shape
    rank, lags = start_basis.shape
    pairs = pair_rows.shape[0]
    groups = lax.axis_size("pairs")
    group_index = lax.axis_index("pairs")
    slices = lax.axis_size("hours")
    hour = lax.axis_index("hours")
    width = lags // slices
    chips = slices // 2
    forward = [(i, (i + 1) % groups) for i in range(groups)]
    backward = [(target, source) for source, target in forward]
    rows = pair_rows.T
    before = lax.ppermute(rows, "pairs", forward)
    after = lax.ppermute(rows, "pairs", backward)
    place = group_index.reshape(1).astype(jnp.int32)
    index, *whitened = call(
        functools.partial(whiten_kernel, groups),
        [struct(rows.shape, jnp.int32)] + [struct((stations, parts * seg, freq), BF16)] * windows,
        [SMEM, HBM, HBM, HBM],
        [VMEM] * (1 + windows),
        [
            pltpu.VMEM(spectra.shape, BF16),
            pltpu.VMEM(masks.shape, jnp.int32),
            pltpu.VMEM(rows.shape, jnp.int32),
            pltpu.SemaphoreType.DMA((3,)),
        ],
    )(place, far(rows), far(spectra), far(masks))
    block = struct((NEAR, parts * seg, freq), BF16)
    def select(wanted):
        return call(
            functools.partial(select_kernel, stations),
            [block] * windows,
            [SMEM] + [VMEM] * (1 + windows),
            [VMEM] * windows,
        )(place, wanted, *whitened)

    to_next, to_last = select(after), select(before)
    lows = [lax.ppermute(one, "pairs", forward) for one in to_next]
    highs = [lax.ppermute(one, "pairs", backward) for one in to_last]
    table, ends = kernel_table(freq, lags)
    fixed = [
        start_basis,
        jnp.asarray(table),
        jnp.asarray(ends),
        jnp.asarray(pick_matrix(pairs, seg, rank)),
        jnp.asarray(spread_matrix(pairs, seg, rank)),
    ]
    staged = call(
        stage_kernel,
        [struct(one.shape, one.dtype) for one in fixed],
        [VMEM] + [HBM] * len(fixed),
        [VMEM] * len(fixed),
        [pltpu.VMEM(start_basis.shape, F32), pltpu.SemaphoreType.DMA((len(fixed),))],
        moved=parts * freq * lags,
    )(to_last[0], *[far(one) for one in fixed])
    core = jnp.mod(hour, 2).reshape(1).astype(jnp.int32)
    chip = (hour // 2).reshape(1).astype(jnp.int32)
    height = -(-(rank + 1) * pairs // 16) * 16
    total_windows = windows * slices
    partial, stacks = None, []
    for w in range(windows):
        last = w == windows - 1
        sizes = (pairs, seg, rank, lags, freq, total_windows, slices, w == 0)
        scratch = [
            pltpu.VMEM((stations + 2 * NEAR, parts * seg, freq), BF16),
            pltpu.VMEM((pairs * seg, parts * freq), BF16),
            pltpu.VMEM((HEAD, lags), F32),
            pltpu.VMEM((HEAD, lags), BF16),
            pltpu.VMEM((HEAD, lags), BF16),
        ]
        args = [index, whitened[w], lows[w], highs[w], *staged]
        specs = [VMEM] * len(args)
        outs = [struct((pairs, lags))]
        if w == 0:
            outs.append(struct((height, lags)))
        else:
            args += [core, partial]
            specs += [SMEM, VMEM]
            outs += [struct((chips, height, width), BF16), struct((chips, height, width))]
            scratch.append(pltpu.VMEM((slices, height, width), F32))
        result = call(
            functools.partial(window_kernel, sizes),
            outs,
            specs,
            [VMEM] * len(outs),
            scratch,
            flops=pairs * seg * parts * freq * lags,
            moved=parts * freq * lags,
        )(*args)
        stacks.append(result[0])
        if w == 0:
            partial = result[1]
        else:
            send, keep = result[1:]
    window_stacks = jnp.stack(stacks, 1)
    swap = lambda value, step: lax.ppermute(value, "hours", [(k, k ^ step) for k in range(slices)])
    got = swap(send, 1)
    top = rank * pairs
    message = struct((chips * top + height - top, width), BF16)
    mine, *sends = call(
        functools.partial(add_kernel, top),
        [struct(keep.shape)] + [message] * (chips - 1),
        [SMEM, VMEM, VMEM],
        [VMEM] * chips,
    )(chip, keep, got)
    arrived = [swap(one, 2 * (step + 1)) for step, one in enumerate(sends)]
    total, gram = call(
        functools.partial(gram_kernel, pairs, rank),
        [struct((height, width)), struct((pairs, 128))],
        [SMEM] + [VMEM] * chips,
        [VMEM] * 2,
        [pltpu.VMEM((chips, top, width), F32)],
    )(chip, mine, *arrived)
    stack, basis = call(
        functools.partial(finish_kernel, pairs, rank, lags),
        [struct((pairs, width)), struct((pairs, rank, width))],
        [VMEM] * 3,
        [VMEM] * 2,
    )(total, gram, swap(gram, 1))
    return (window_stacks, stack, basis)


def solution(mesh):
    in_specs = (
        P("pairs", "hours", None, None, None),
        P("pairs", "hours", None),
        P("pairs", None),
        P(),
    )
    out_specs = (P("pairs", "hours", None), P("pairs", "hours"), P("pairs", None, "hours"))
    return jax.shard_map(
        on_device, mesh=mesh, in_specs=in_specs, out_specs=out_specs, check_vma=False
    )
```

```python
import functools
import math

import jax
import jax.numpy as jnp
import numpy as np
from jax import lax
from jax.experimental import pallas as pl
from jax.experimental.pallas import tpu as pltpu
from jax.sharding import PartitionSpec as P

BAND = 64
TURNS = 2
NEAR = 4
F32 = jnp.float32
BF16 = jnp.bfloat16
VMEM = pl.BlockSpec(memory_space=pltpu.VMEM)
SMEM = pl.BlockSpec(memory_space=pltpu.SMEM)
HBM = pl.BlockSpec(memory_space=pltpu.HBM)
HEAD = 128
LANE = 16


def kernel_table(freq, lags):
    nfft = 2 * lags
    bins = np.arange(1, freq + 1, dtype=np.int64)[:, None]
    shifts = np.append(np.arange(lags // 2, dtype=np.int64), -(lags // 2))[None, :]
    phase = np.mod(bins * shifts, nfft).astype(np.float64) * (2.0 * math.pi / nfft)
    scale = freq ** (-0.5)
    both = np.concatenate([np.cos(phase) * scale, -np.sin(phase) * scale], 0)
    both = both.astype(np.float32).astype(jnp.bfloat16)
    ends = both[:, -1].astype(np.float32).reshape(2, freq)
    return both[:, :-1], ends


def pick_matrix(pairs, seg, rank):
    pick = np.zeros((HEAD, 2 * HEAD), np.float32)
    side = (seg + rank) * LANE
    for pair in range(pairs):
        for part in range(seg):
            pick[pair * seg + part, part * LANE + pair] = 1
            pick[pair * seg + part, side + pair] = 1
    for row in range(rank):
        pick[pairs * seg + row, (seg + row) * LANE : (seg + row + 1) * LANE] = 1
    return pick.astype(jnp.bfloat16)


def spread_matrix(pairs, seg, rank):
    spread = np.zeros((HEAD, (rank + 1) * HEAD), np.float32)
    for row in range(rank + 1):
        for part in range(seg):
            for pair in range(pairs):
                spread[row * LANE + part, row * HEAD + pair * seg + part] = 1
        for other in range(rank):
            spread[row * LANE + seg + other, row * HEAD + pairs * seg + other] = 1
    return spread.astype(jnp.bfloat16)


def two_parts(values):
    high = values.astype(BF16)
    return high, (values - high.astype(F32)).astype(BF16)


def three_parts(values):
    high = values.astype(BF16)
    rest = values - high.astype(F32)
    mid = rest.astype(BF16)
    return high, mid, (rest - mid.astype(F32)).astype(BF16)


def dot(left, right):
    return jnp.dot(left, right, preferred_element_type=F32)


def dot_rows(left, right):
    return lax.dot_general(left, right, (((1,), (1,)), ((), ())), preferred_element_type=F32)


def lower_factor(gram, rank):
    lower = [[None] * rank for _ in range(rank)]
    inverse = [None] * rank
    for row in range(rank):
        for col in range(row + 1):
            total = gram[row][col]
            for inner in range(col):
                total = total - lower[row][inner] * lower[col][inner]
            if row == col:
                inverse[row] = lax.rsqrt(total)
                lower[row][row] = total * inverse[row]
            else:
                lower[row][col] = total * inverse[col]
    return lower, inverse


def solve_rows(rows, lower, inverse):
    result = []
    for row, current in enumerate(rows):
        for inner in range(row):
            current = current - lower[row][inner] * result[inner]
        result.append(current * inverse[row])
    return result


def used_stations(second, low, stations):
    number = lax.broadcasted_iota(jnp.int32, (stations, second.shape[1]), 0)
    return jnp.max(jnp.where(second == low + number, 1.0, 0.0), 1, keepdims=True)


def flip(values):
    rows, width = values.shape
    back = 127 - lax.broadcasted_iota(jnp.int32, (rows, 128), 1)
    turned = []
    for at in range(width - 128, -1, -128):
        turned.append(jnp.take_along_axis(values[:, at : at + 128], back, axis=1))
    return jnp.concatenate(turned, 1)


def first_lane(values, first, other):
    lane = lax.broadcasted_iota(jnp.int32, values, 1)
    return jnp.where(lane == 0, first, other)


def unfold(even, odd):
    shape = even.shape
    root = math.sqrt(2.0)
    right = first_lane(shape, even * root, even + odd)
    left = first_lane(shape, odd * root, even - odd)
    return flip(pltpu.roll(left, shape[1] - 1, 1)), right


def stage_kernel(groups, stations, place, early, far_rows, *refs):
    *refs, index, natural, rows, sems = refs
    count = len(refs) // 2
    sources, targets = refs[:count], refs[count:]
    copies = [
        pltpu.make_async_copy(source, target, sems.at[number])
        for number, (source, target) in enumerate(zip(sources, (natural, *targets[1:])))
    ]
    for copy in copies:
        copy.start()
    known = pltpu.make_async_copy(far_rows, rows, sems.at[count])
    known.start()
    known.wait()
    before = lax.rem(place[0] + groups - 1, groups) * stations
    after = lax.rem(place[0] + 1, groups) * stations
    own = place[0] * stations
    second = rows[1:2]
    in_before = jnp.logical_and(second >= before, second < before + stations)
    in_own = jnp.logical_and(second >= own, second < own + stations)
    local = second - jnp.where(in_before, before, jnp.where(in_own, own, after))
    below = lax.broadcasted_iota(jnp.int32, (stations, second.shape[1]), 0) < local
    slots = [
        jnp.sum(jnp.where(below, used_stations(second, low, stations), 0.0), 0, keepdims=True)
        for low in (before, after)
    ]
    spot = jnp.where(in_own, NEAR + local, NEAR + stations + slots[1].astype(jnp.int32))
    index[0:1] = rows[0:1] - own
    index[1:2] = jnp.where(in_before, slots[0].astype(jnp.int32), spot)
    copies[0].wait()
    values = natural[...]
    half = values.shape[1] // 2
    right = values[:, half:]
    left = pltpu.roll(flip(values[:, :half]), 1, 1)
    shape = right.shape
    root = math.sqrt(0.5)
    targets[0][:, :half] = first_lane(shape, right * root, (right + left) * 0.5)
    targets[0][:, half:] = first_lane(shape, left * root, (right - left) * 0.5)
    for copy in copies[1:]:
        copy.wait()


def whiten_kernel(far_spectra, far_masks, *refs):
    whitened, (spectra, masks, sems) = refs[:-3], refs[-3:]
    stations, windows, seg, _, freq = spectra.shape
    small = [pltpu.make_async_copy(far_masks, masks, sems.at[0])]
    large = [pltpu.make_async_copy(far_spectra, spectra, sems.at[1])]
    for copy in small + large:
        copy.start()
    count = freq // BAND
    of_bin = lax.broadcasted_iota(jnp.int32, (count, freq), 1) // BAND
    bands = jnp.where(lax.broadcasted_iota(jnp.int32, (count, freq), 0) == of_bin, 1.0, 0.0).astype(BF16)
    of_bin = lax.broadcasted_iota(jnp.int32, (freq, count), 0) // BAND
    sums = jnp.where(lax.broadcasted_iota(jnp.int32, (freq, count), 1) == of_bin, 1.0, 0.0).astype(BF16)
    for copy in small:
        copy.wait()
    eye = lax.broadcasted_iota(jnp.int32, (seg, seg), 0) == lax.broadcasted_iota(jnp.int32, (seg, seg), 1)
    open_rows = []
    for station in range(stations):
        for window in range(windows):
            mask = masks[station, window : window + 1].astype(F32)
            mask = jnp.where(eye, jnp.broadcast_to(mask, (seg, seg)), 0.0)
            open_rows.append(jnp.sum(mask, 1, keepdims=True))
    large[0].wait()
    values, squares = [], []
    for station in range(stations):
        for window in range(windows):
            block = spectra[station, window].astype(F32)
            real, imag = block[:, 0], block[:, 1]
            values.append((real, imag))
            squares.append(real * real + imag * imag)
    height = len(values) * seg
    power = dot(jnp.concatenate(two_parts(jnp.concatenate(squares, 0)), 0), sums)
    power = power[0:height] + power[height:]
    scale = lax.rsqrt(power * (1.0 / (2 * BAND)) + 1e-06) * jnp.concatenate(open_rows, 0)
    scale = dot(jnp.concatenate(two_parts(scale), 0), bands)
    scale = scale[0:height] + scale[height:]
    for number, (real, imag) in enumerate(values):
        here = scale[number * seg : (number + 1) * seg]
        block = jnp.concatenate([real * here, imag * here], 0).astype(BF16)
        whitened[number % windows][number // windows] = block


def select_kernel(stations, place, rows, *refs):
    windows = len(refs) // 2
    used = used_stations(rows[1:2], place[0] * stations, stations)
    weight = jnp.left_shift(1, lax.broadcasted_iota(jnp.int32, (stations, 1), 0)).astype(F32)
    needed = jnp.sum(used * weight).astype(jnp.int32)
    slot = jnp.int32(0)
    for station in range(stations):
        wanted = jnp.bitwise_and(jnp.right_shift(needed, station), 1)
        spot = jnp.minimum(slot, NEAR - 1)

        @pl.when(wanted == 1)
        def _():
            for source, target in zip(refs[:windows], refs[windows:]):
                target[spot] = source[station]

        slot = slot + wanted


def window_kernel(sizes, index, own, low, high, start, table, ends, pick, spread, *refs):
    pairs, seg, rank, lags, freq, total_windows, slices, first_window = sizes
    rows = pairs * seg
    if first_window:
        win_out, merged_out, near, cross, vectors, high_part, low_part = refs
    else:
        (core, partial, win_out, send_out, keep_out, near, cross, vectors, high_part, low_part, pieces) = refs
    stations = own.shape[0]
    half = lags // 2
    picked = index[...]
    near[0:NEAR] = low[...]
    near[NEAR : NEAR + stations] = own[...]
    near[NEAR + stations :] = high[...]
    edges = []
    for pair in range(0, pairs, 2):
        real, imag = [], []
        for one in (pair, pair + 1):
            a = own[picked[0, one]].astype(F32)
            b = near[picked[1, one]].astype(F32)
            a_re, a_im, b_re, b_im = a[:seg], a[seg:], b[:seg], b[seg:]
            real.append(a_re * b_re + a_im * b_im)
            imag.append(a_im * b_re - a_re * b_im)
        block = pl.ds(pair * seg, 2 * seg)
        real = jnp.concatenate(real, 0).astype(BF16)
        imag = jnp.concatenate(imag, 0).astype(BF16)
        cross[block, 0:freq] = real
        cross[block, freq:] = imag
        last = real.astype(F32) * ends[0:1] + imag.astype(F32) * ends[1:2]
        edges.append(jnp.sum(last, 1, keepdims=True))
    vectors[rows : rows + rank] = start[...]
    vectors[rows + rank :] = jnp.zeros((HEAD - rows - rank, lags), F32)
    step = 512
    for at in range(0, half, step):
        vectors[0:rows, at : at + step] = dot(cross[:, 0:freq], table[0:freq, at : at + step])
        vectors[0:rows, half + at : half + at + step] = dot(cross[:, freq:], table[freq:, at : at + step])
    shape = (rows, 128)
    root = math.sqrt(0.5)
    column = vectors[0:rows, 0:128]
    vectors[0:rows, 0:128] = first_lane(shape, column * root, column)
    edge = jnp.broadcast_to(jnp.concatenate(edges, 0) * root, shape)
    vectors[0:rows, half : half + 128] = first_lane(shape, edge, vectors[0:rows, half : half + 128])
    every = vectors[...]
    high_part[...] = every.astype(BF16)
    low_part[...] = (every - high_part[...].astype(F32)).astype(BF16)
    gram = dot_rows(high_part[...], high_part[...])
    side = dot_rows(low_part[...], high_part[...])
    gram = 2.0 * (gram + side + side.T)
    lane = lax.broadcasted_iota(jnp.int32, (seg, HEAD), 1)
    sub = lax.broadcasted_iota(jnp.int32, (seg, HEAD), 0)
    blocks = jnp.zeros((seg, HEAD), F32)
    for pair in range(pairs):
        blocks = blocks + jnp.where(lane // seg == pair, gram[pair * seg : (pair + 1) * seg], 0.0)
    basis_rows = gram[rows : rows + 8]
    turned = [
        jnp.where(lane % seg == sub, jnp.broadcast_to(basis_rows[row : row + 1], (seg, HEAD)), 0.0)
        for row in range(rank)
    ]
    stacked = jnp.concatenate([blocks, basis_rows] + turned, 0)
    count = stacked.shape[0]
    moved = dot(jnp.concatenate(three_parts(stacked), 0), pick[...])
    moved = moved[0:count] + moved[count : 2 * count] + moved[2 * count :]
    products = [moved[0:16, k * LANE : (k + 1) * LANE] for k in range(seg)]
    side_at = (seg + rank) * LANE
    for row in range(rank):
        upper = moved[16 + row * seg : 16 + (row + 1) * seg, side_at : side_at + LANE]
        under = moved[8:16, (seg + row) * LANE : (seg + row + 1) * LANE]
        products.append(jnp.concatenate([upper, under], 0))
    level = lax.broadcasted_iota(jnp.int32, (16, LANE), 0)
    of_corr = level < seg
    known = [jnp.where(level == seg + row, 1.0, 0.0) for row in range(rank)]
    reach = [jnp.where(of_corr, products[seg + row], 0.0) for row in range(rank)]
    for turn in range(TURNS):
        known = [known[r] + reach[r] * (1.0 / lags) for r in range(rank)]
        images = []
        for r in range(rank):
            image = known[r][0:1] * products[0]
            for k in range(1, seg + rank):
                image = image + known[r][k : k + 1] * products[k]
            images.append(image)
        inner = [
            [jnp.sum(images[r] * known[s], 0, keepdims=True) for s in range(r + 1)] for r in range(rank)
        ]
        lower, inverse = lower_factor(inner, rank)
        known = solve_rows(known, lower, inverse)
        reach = [jnp.where(of_corr, v, 0.0) for v in solve_rows(images, lower, inverse)]
    outs = [reach[r] + float(lags) * known[r] for r in range(rank)]
    window = jnp.zeros_like(known[0])
    for r in range(rank):
        window = window + jnp.sum(reach[r], 0, keepdims=True) * known[r]
    outs.append(window * (1.0 / math.sqrt(seg)))
    coefs = jnp.concatenate(outs + [jnp.zeros((HEAD - (rank + 1) * 16, LANE), F32)], 0)
    coefs = jnp.concatenate([coefs, jnp.zeros((HEAD, HEAD - LANE), F32)], 1).T[0:LANE]
    wide = dot(jnp.concatenate(two_parts(coefs), 0), spread[...])
    wide = wide[0:LANE] + wide[LANE:]
    row_of = lax.broadcasted_iota(jnp.int32, (LANE, HEAD), 0)
    lane_of = lax.broadcasted_iota(jnp.int32, (LANE, HEAD), 1)
    mine = jnp.logical_or(lane_of // seg == row_of, lane_of >= rows)
    weights = [
        jnp.where(mine, wide[:, r * HEAD : (r + 1) * HEAD], 0.0)[0:pairs] for r in range(rank + 1)
    ]
    filled = (rank + 1) * pairs
    height = -(-filled // 16) * 16
    weights = jnp.concatenate(weights + [jnp.zeros((height - filled, HEAD), F32)], 0)
    w_high, w_low = two_parts(weights)
    both = jnp.concatenate([w_high, w_low], 0)
    scale = 1.0 / math.sqrt(total_windows)
    width = lags // slices
    top = rank * pairs

    def combined(at):
        part = dot(both, high_part[:, at : at + step])
        return part[0:height] + part[height:] + dot(w_high, low_part[:, at : at + step])

    result = [jnp.concatenate([combined(side + at) for at in range(0, half, step)], 1) for side in (0, half)]
    left, right = unfold(*[one[top:] for one in result])
    win_out[:, 0:half] = left[0:pairs]
    win_out[:, half:] = right[0:pairs]
    result = [jnp.concatenate([one[0:top], one[top:] * scale], 0) for one in result]
    if first_window:
        merged_out[:, 0:half] = result[0]
        merged_out[:, half:] = result[1]
    else:
        left, right = unfold(result[0] + partial[:, 0:half], result[1] + partial[:, half:])
        for piece in range(slices // 2):
            pieces[piece] = left[:, piece * width : (piece + 1) * width]
            pieces[slices // 2 + piece] = right[:, piece * width : (piece + 1) * width]
    if not first_window:
        for piece in range(slices // 2):
            send_out[piece] = pieces[2 * piece + 1 - core[0]].astype(BF16)
            keep_out[piece] = pieces[2 * piece + core[0]]


def add_kernel(top, chip, keep, got, mine_out, *sends):
    chips, height, _ = keep.shape
    for part in range(chips):
        both = keep[part] + got[part].astype(F32)
        mine_out[part] = both
        short = both[0:top].astype(BF16)
        for out in sends:
            out[part * top : (part + 1) * top] = short
    for step, out in enumerate(sends):
        other = jnp.bitwise_xor(chip[0], step + 1)
        out[chips * top :] = mine_out[other, top:height].astype(BF16)


def gram_kernel(pairs, rank, chip, mine, *refs):
    got, (total_out, gram_out, parts) = refs[:-3], refs[-3:]
    chips, height, width = mine.shape
    top = rank * pairs
    sums = [[jnp.zeros((pairs, width), F32) for _ in range(r + 1)] for r in range(rank)]
    for part in range(chips):
        block = mine[part, 0:top].astype(BF16).astype(F32)
        for one in got:
            block = block + one[part * top : (part + 1) * top].astype(F32)
        parts[part] = block
        rows = [block[r * pairs : (r + 1) * pairs] for r in range(rank)]
        sums = [[sums[r][s] + rows[r] * rows[s] for s in range(r + 1)] for r in range(rank)]
    stack = mine[chip[0], top:height]
    for one in got:
        stack = stack + one[chips * top :].astype(F32)
    total_out[0:top] = parts[chip[0]]
    total_out[top:] = stack
    lane = lax.broadcasted_iota(jnp.int32, (pairs, 128), 1)
    gram = jnp.zeros((pairs, 128), F32)
    for r in range(rank):
        for s in range(r + 1):
            value = jnp.sum(sums[r][s], 1, keepdims=True)
            gram = jnp.where(lane == r * rank + s, value, gram)
    gram_out[...] = gram


def finish_kernel(pairs, rank, lags, total, mine, got, stack_out, basis_out):
    gram = mine[...] + got[...]
    shape = (pairs, total.shape[1])
    entries = [
        [jnp.broadcast_to(gram[:, r * rank + s : r * rank + s + 1], shape) for s in range(r + 1)]
        for r in range(rank)
    ]
    lower, inverse = lower_factor(entries, rank)
    rows = [total[r * pairs : (r + 1) * pairs] for r in range(rank)]
    for r, row in enumerate(solve_rows(rows, lower, inverse)):
        basis_out[:, r, :] = row * math.sqrt(lags)
    stack_out[...] = total[rank * pairs : (rank + 1) * pairs]


def call(kernel, out_shape, in_specs, out_specs, scratch=(), flops=0, moved=0):
    return pl.pallas_call(
        kernel,
        out_shape=out_shape,
        in_specs=in_specs,
        out_specs=out_specs,
        scratch_shapes=list(scratch),
        compiler_params=pltpu.CompilerParams(vmem_limit_bytes=12 * 1024 * 1024),
        cost_estimate=pl.CostEstimate(flops=flops, bytes_accessed=moved, transcendentals=0),
    )


def far(value):
    return pltpu.with_memory_space_constraint(value, pltpu.HBM)


def struct(shape, dtype=F32):
    return jax.ShapeDtypeStruct(shape, dtype)


def on_device(spectra, masks, pair_rows, start_basis):
    stations, windows, seg, parts, freq = spectra.shape
    rank, lags = start_basis.shape
    pairs = pair_rows.shape[0]
    groups = lax.axis_size("pairs")
    group_index = lax.axis_index("pairs")
    slices = lax.axis_size("hours")
    hour = lax.axis_index("hours")
    width = lags // slices
    chips = slices // 2
    forward = [(i, (i + 1) % groups) for i in range(groups)]
    backward = [(target, source) for source, target in forward]
    rows = pair_rows.T
    before = lax.ppermute(rows, "pairs", forward)
    after = lax.ppermute(rows, "pairs", backward)
    place = group_index.reshape(1).astype(jnp.int32)
    whitened = call(
        whiten_kernel,
        [struct((stations, parts * seg, freq), BF16)] * windows,
        [HBM] * 2,
        [VMEM] * windows,
        [
            pltpu.VMEM(spectra.shape, BF16),
            pltpu.VMEM(masks.shape, jnp.int32),
            pltpu.SemaphoreType.DMA((2,)),
        ],
    )(far(spectra), far(masks))
    block = struct((NEAR, parts * seg, freq), BF16)
    def select(wanted):
        return call(
            functools.partial(select_kernel, stations),
            [block] * windows,
            [SMEM] + [VMEM] * (1 + windows),
            [VMEM] * windows,
        )(place, wanted, *whitened)

    to_next, to_last = select(after), select(before)
    lows = [lax.ppermute(one, "pairs", forward) for one in to_next]
    highs = [lax.ppermute(one, "pairs", backward) for one in to_last]
    table, ends = kernel_table(freq, lags)
    fixed = [
        start_basis,
        jnp.asarray(table),
        jnp.asarray(ends),
        jnp.asarray(pick_matrix(pairs, seg, rank)),
        jnp.asarray(spread_matrix(pairs, seg, rank)),
    ]
    *staged, index = call(
        functools.partial(stage_kernel, groups, stations),
        [struct(one.shape, one.dtype) for one in fixed] + [struct(rows.shape, jnp.int32)],
        [SMEM, VMEM] + [HBM] * (len(fixed) + 1),
        [VMEM] * (len(fixed) + 1),
        [
            pltpu.VMEM(start_basis.shape, F32),
            pltpu.VMEM(rows.shape, jnp.int32),
            pltpu.SemaphoreType.DMA((len(fixed) + 1,)),
        ],
        moved=parts * freq * lags,
    )(place, to_next[0], far(rows), *[far(one) for one in fixed])
    core = jnp.mod(hour, 2).reshape(1).astype(jnp.int32)
    chip = (hour // 2).reshape(1).astype(jnp.int32)
    height = -(-(rank + 1) * pairs // 16) * 16
    total_windows = windows * slices
    partial, stacks = None, []
    for w in range(windows):
        last = w == windows - 1
        sizes = (pairs, seg, rank, lags, freq, total_windows, slices, w == 0)
        scratch = [
            pltpu.VMEM((stations + 2 * NEAR, parts * seg, freq), BF16),
            pltpu.VMEM((pairs * seg, parts * freq), BF16),
            pltpu.VMEM((HEAD, lags), F32),
            pltpu.VMEM((HEAD, lags), BF16),
            pltpu.VMEM((HEAD, lags), BF16),
        ]
        args = [index, whitened[w], lows[w], highs[w], *staged]
        specs = [VMEM] * len(args)
        outs = [struct((pairs, lags))]
        if w == 0:
            outs.append(struct((height, lags)))
        else:
            args += [core, partial]
            specs += [SMEM, VMEM]
            outs += [struct((chips, height, width), BF16), struct((chips, height, width))]
            scratch.append(pltpu.VMEM((slices, height, width), F32))
        result = call(
            functools.partial(window_kernel, sizes),
            outs,
            specs,
            [VMEM] * len(outs),
            scratch,
            flops=pairs * seg * parts * freq * lags,
            moved=parts * freq * lags,
        )(*args)
        stacks.append(result[0])
        if w == 0:
            partial = result[1]
        else:
            send, keep = result[1:]
    window_stacks = jnp.stack(stacks, 1)
    swap = lambda value, step: lax.ppermute(value, "hours", [(k, k ^ step) for k in range(slices)])
    got = swap(send, 1)
    top = rank * pairs
    message = struct((chips * top + height - top, width), BF16)
    mine, *sends = call(
        functools.partial(add_kernel, top),
        [struct(keep.shape)] + [message] * (chips - 1),
        [SMEM, VMEM, VMEM],
        [VMEM] * chips,
    )(chip, keep, got)
    arrived = [swap(one, 2 * (step + 1)) for step, one in reversed(list(enumerate(sends)))]
    total, gram = call(
        functools.partial(gram_kernel, pairs, rank),
        [struct((height, width)), struct((pairs, 128))],
        [SMEM] + [VMEM] * chips,
        [VMEM] * 2,
        [pltpu.VMEM((chips, top, width), F32)],
    )(chip, mine, *arrived)
    stack, basis = call(
        functools.partial(finish_kernel, pairs, rank, lags),
        [struct((pairs, width)), struct((pairs, rank, width))],
        [VMEM] * 3,
        [VMEM] * 2,
    )(total, gram, swap(gram, 1))
    return (window_stacks, stack, basis)


def solution(mesh):
    in_specs = (
        P("pairs", "hours", None, None, None),
        P("pairs", "hours", None),
        P("pairs", None),
        P(),
    )
    out_specs = (P("pairs", "hours", None), P("pairs", "hours"), P("pairs", None, "hours"))
    return jax.shard_map(
        on_device, mesh=mesh, in_specs=in_specs, out_specs=out_specs, check_vma=False
    )
```

```python
import functools
import math

import jax
import jax.numpy as jnp
import numpy as np
from jax import lax
from jax.experimental import pallas as pl
from jax.experimental.pallas import tpu as pltpu
from jax.sharding import PartitionSpec as P

BAND = 64
TURNS = 2
NEAR = 4
F32 = jnp.float32
BF16 = jnp.bfloat16
VMEM = pl.BlockSpec(memory_space=pltpu.VMEM)
SMEM = pl.BlockSpec(memory_space=pltpu.SMEM)
HBM = pl.BlockSpec(memory_space=pltpu.HBM)
HEAD = 128
LANE = 16


def kernel_table(freq, lags):
    nfft = 2 * lags
    bins = np.arange(1, freq + 1, dtype=np.int64)[:, None]
    shifts = np.append(np.arange(lags // 2, dtype=np.int64), -(lags // 2))[None, :]
    phase = np.mod(bins * shifts, nfft).astype(np.float64) * (2.0 * math.pi / nfft)
    scale = freq ** (-0.5)
    both = np.concatenate([np.cos(phase) * scale, -np.sin(phase) * scale], 0)
    both = both.astype(np.float32).astype(jnp.bfloat16)
    ends = both[:, -1].astype(np.float32).reshape(2, freq)
    return both[:, :-1], ends


def pick_matrix(pairs, seg, rank):
    pick = np.zeros((HEAD, 2 * HEAD), np.float32)
    side = (seg + rank) * LANE
    for pair in range(pairs):
        for part in range(seg):
            pick[pair * seg + part, part * LANE + pair] = 1
            pick[pair * seg + part, side + pair] = 1
    for row in range(rank):
        pick[pairs * seg + row, (seg + row) * LANE : (seg + row + 1) * LANE] = 1
    return pick.astype(jnp.bfloat16)


def spread_matrix(pairs, seg, rank):
    spread = np.zeros((HEAD, (rank + 1) * HEAD), np.float32)
    for row in range(rank + 1):
        for part in range(seg):
            for pair in range(pairs):
                spread[row * LANE + part, row * HEAD + pair * seg + part] = 1
        for other in range(rank):
            spread[row * LANE + seg + other, row * HEAD + pairs * seg + other] = 1
    return spread.astype(jnp.bfloat16)


def two_parts(values):
    high = values.astype(BF16)
    return high, (values - high.astype(F32)).astype(BF16)


def three_parts(values):
    high = values.astype(BF16)
    rest = values - high.astype(F32)
    mid = rest.astype(BF16)
    return high, mid, (rest - mid.astype(F32)).astype(BF16)


def dot(left, right):
    return jnp.dot(left, right, preferred_element_type=F32)


def dot_rows(left, right):
    return lax.dot_general(left, right, (((1,), (1,)), ((), ())), preferred_element_type=F32)


def lower_factor(gram, rank):
    lower = [[None] * rank for _ in range(rank)]
    inverse = [None] * rank
    for row in range(rank):
        for col in range(row + 1):
            total = gram[row][col]
            for inner in range(col):
                total = total - lower[row][inner] * lower[col][inner]
            if row == col:
                inverse[row] = lax.rsqrt(total)
                lower[row][row] = total * inverse[row]
            else:
                lower[row][col] = total * inverse[col]
    return lower, inverse


def solve_rows(rows, lower, inverse):
    result = []
    for row, current in enumerate(rows):
        for inner in range(row):
            current = current - lower[row][inner] * result[inner]
        result.append(current * inverse[row])
    return result


def used_stations(second, low, stations):
    number = lax.broadcasted_iota(jnp.int32, (stations, second.shape[1]), 0)
    return jnp.max(jnp.where(second == low + number, 1.0, 0.0), 1, keepdims=True)


def flip(values):
    rows, width = values.shape
    back = 127 - lax.broadcasted_iota(jnp.int32, (rows, 128), 1)
    turned = []
    for at in range(width - 128, -1, -128):
        turned.append(jnp.take_along_axis(values[:, at : at + 128], back, axis=1))
    return jnp.concatenate(turned, 1)


def first_lane(values, first, other):
    lane = lax.broadcasted_iota(jnp.int32, values, 1)
    return jnp.where(lane == 0, first, other)


def unfold(even, odd):
    shape = even.shape
    root = math.sqrt(2.0)
    right = first_lane(shape, even * root, even + odd)
    left = first_lane(shape, odd * root, even - odd)
    return flip(pltpu.roll(left, shape[1] - 1, 1)), right


def stage_kernel(groups, stations, place, early, far_rows, *refs):
    *refs, index, natural, rows, sems = refs
    count = len(refs) // 2
    sources, targets = refs[:count], refs[count:]
    copies = [
        pltpu.make_async_copy(source, target, sems.at[number])
        for number, (source, target) in enumerate(zip(sources, (natural, *targets[1:])))
    ]
    for copy in copies:
        copy.start()
    known = pltpu.make_async_copy(far_rows, rows, sems.at[count])
    known.start()
    known.wait()
    before = lax.rem(place[0] + groups - 1, groups) * stations
    after = lax.rem(place[0] + 1, groups) * stations
    own = place[0] * stations
    second = rows[1:2]
    in_before = jnp.logical_and(second >= before, second < before + stations)
    in_own = jnp.logical_and(second >= own, second < own + stations)
    local = second - jnp.where(in_before, before, jnp.where(in_own, own, after))
    below = lax.broadcasted_iota(jnp.int32, (stations, second.shape[1]), 0) < local
    slots = [
        jnp.sum(jnp.where(below, used_stations(second, low, stations), 0.0), 0, keepdims=True)
        for low in (before, after)
    ]
    spot = jnp.where(in_own, NEAR + local, NEAR + stations + slots[1].astype(jnp.int32))
    index[0:1] = rows[0:1] - own
    index[1:2] = jnp.where(in_before, slots[0].astype(jnp.int32), spot)
    copies[0].wait()
    values = natural[...]
    half = values.shape[1] // 2
    right = values[:, half:]
    left = pltpu.roll(flip(values[:, :half]), 1, 1)
    shape = right.shape
    root = math.sqrt(0.5)
    targets[0][:, :half] = first_lane(shape, right * root, (right + left) * 0.5)
    targets[0][:, half:] = first_lane(shape, left * root, (right - left) * 0.5)
    for copy in copies[1:]:
        copy.wait()


def whiten_kernel(far_spectra, far_masks, *refs):
    whitened, (spectra, masks, sems) = refs[:-3], refs[-3:]
    stations, windows, seg, _, freq = spectra.shape
    small = [pltpu.make_async_copy(far_masks, masks, sems.at[0])]
    large = [pltpu.make_async_copy(far_spectra, spectra, sems.at[1])]
    for copy in small + large:
        copy.start()
    tile = (128, 128)
    same = lax.broadcasted_iota(jnp.int32, tile, 0) // BAND == lax.broadcasted_iota(jnp.int32, tile, 1) // BAND
    bands = jnp.where(same, 1.0, 0.0).astype(BF16)
    for copy in small:
        copy.wait()
    eye = lax.broadcasted_iota(jnp.int32, (seg, seg), 0) == lax.broadcasted_iota(jnp.int32, (seg, seg), 1)
    open_rows = []
    for station in range(stations):
        for window in range(windows):
            mask = masks[station, window : window + 1].astype(F32)
            mask = jnp.where(eye, jnp.broadcast_to(mask, (seg, seg)), 0.0)
            open_rows.append(jnp.sum(mask, 1, keepdims=True))
    large[0].wait()
    values, squares = [], []
    for station in range(stations):
        for window in range(windows):
            block = spectra[station, window].astype(F32)
            real, imag = block[:, 0], block[:, 1]
            values.append((real, imag))
            squares.append(real * real + imag * imag)
    height = len(values) * seg
    squares = jnp.concatenate(squares, 0)
    here = jnp.concatenate(open_rows, 0)
    scales = []
    for at in range(0, freq, 128):
        power = dot(jnp.concatenate(two_parts(squares[:, at : at + 128]), 1), jnp.concatenate([bands, bands], 0))
        scales.append(lax.rsqrt(power * (1.0 / (2 * BAND)) + 1e-06) * here)
    scale = jnp.concatenate(scales, 1)
    for number, (real, imag) in enumerate(values):
        here = scale[number * seg : (number + 1) * seg]
        block = jnp.concatenate([real * here, imag * here], 0).astype(BF16)
        whitened[number % windows][number // windows] = block


def select_kernel(stations, place, rows, *refs):
    windows = len(refs) // 2
    used = used_stations(rows[1:2], place[0] * stations, stations)
    weight = jnp.left_shift(1, lax.broadcasted_iota(jnp.int32, (stations, 1), 0)).astype(F32)
    needed = jnp.sum(used * weight).astype(jnp.int32)
    slot = jnp.int32(0)
    for station in range(stations):
        wanted = jnp.bitwise_and(jnp.right_shift(needed, station), 1)
        spot = jnp.minimum(slot, NEAR - 1)

        @pl.when(wanted == 1)
        def _():
            for source, target in zip(refs[:windows], refs[windows:]):
                target[spot] = source[station]

        slot = slot + wanted


def window_kernel(sizes, index, own, low, high, start, table, ends, pick, spread, *refs):
    pairs, seg, rank, lags, freq, total_windows, slices, first_window = sizes
    rows = pairs * seg
    if first_window:
        win_out, merged_out, near, cross, vectors, high_part, low_part = refs
    else:
        (core, partial, win_out, send_out, keep_out, near, cross, vectors, high_part, low_part, pieces) = refs
    stations = own.shape[0]
    half = lags // 2
    picked = index[...]
    near[0:NEAR] = low[...]
    near[NEAR : NEAR + stations] = own[...]
    near[NEAR + stations :] = high[...]
    edges = []
    for pair in range(0, pairs, 2):
        real, imag = [], []
        for one in (pair, pair + 1):
            a = own[picked[0, one]].astype(F32)
            b = near[picked[1, one]].astype(F32)
            a_re, a_im, b_re, b_im = a[:seg], a[seg:], b[:seg], b[seg:]
            real.append(a_re * b_re + a_im * b_im)
            imag.append(a_im * b_re - a_re * b_im)
        block = pl.ds(pair * seg, 2 * seg)
        real = jnp.concatenate(real, 0).astype(BF16)
        imag = jnp.concatenate(imag, 0).astype(BF16)
        cross[block, 0:freq] = real
        cross[block, freq:] = imag
        last = real.astype(F32) * ends[0:1] + imag.astype(F32) * ends[1:2]
        edges.append(jnp.sum(last, 1, keepdims=True))
    vectors[rows : rows + rank] = start[...]
    vectors[rows + rank :] = jnp.zeros((HEAD - rows - rank, lags), F32)
    step = 512
    for at in range(0, half, step):
        vectors[0:rows, at : at + step] = dot(cross[:, 0:freq], table[0:freq, at : at + step])
        vectors[0:rows, half + at : half + at + step] = dot(cross[:, freq:], table[freq:, at : at + step])
    shape = (rows, 128)
    root = math.sqrt(0.5)
    column = vectors[0:rows, 0:128]
    vectors[0:rows, 0:128] = first_lane(shape, column * root, column)
    edge = jnp.broadcast_to(jnp.concatenate(edges, 0) * root, shape)
    vectors[0:rows, half : half + 128] = first_lane(shape, edge, vectors[0:rows, half : half + 128])
    every = vectors[...]
    high_part[...] = every.astype(BF16)
    low_part[...] = (every - high_part[...].astype(F32)).astype(BF16)
    gram = dot_rows(high_part[...], high_part[...])
    side = dot_rows(low_part[...], high_part[...])
    gram = 2.0 * (gram + side + side.T)
    lane = lax.broadcasted_iota(jnp.int32, (seg, HEAD), 1)
    sub = lax.broadcasted_iota(jnp.int32, (seg, HEAD), 0)
    blocks = jnp.zeros((seg, HEAD), F32)
    for pair in range(pairs):
        blocks = blocks + jnp.where(lane // seg == pair, gram[pair * seg : (pair + 1) * seg], 0.0)
    basis_rows = gram[rows : rows + 8]
    turned = [
        jnp.where(lane % seg == sub, jnp.broadcast_to(basis_rows[row : row + 1], (seg, HEAD)), 0.0)
        for row in range(rank)
    ]
    stacked = jnp.concatenate([blocks, basis_rows] + turned, 0)
    count = stacked.shape[0]
    moved = dot(jnp.concatenate(three_parts(stacked), 0), pick[...])
    moved = moved[0:count] + moved[count : 2 * count] + moved[2 * count :]
    products = [moved[0:16, k * LANE : (k + 1) * LANE] for k in range(seg)]
    side_at = (seg + rank) * LANE
    for row in range(rank):
        upper = moved[16 + row * seg : 16 + (row + 1) * seg, side_at : side_at + LANE]
        under = moved[8:16, (seg + row) * LANE : (seg + row + 1) * LANE]
        products.append(jnp.concatenate([upper, under], 0))
    level = lax.broadcasted_iota(jnp.int32, (16, LANE), 0)
    of_corr = level < seg
    known = [jnp.where(level == seg + row, 1.0, 0.0) for row in range(rank)]
    reach = [jnp.where(of_corr, products[seg + row], 0.0) for row in range(rank)]
    for turn in range(TURNS):
        known = [known[r] + reach[r] * (1.0 / lags) for r in range(rank)]
        images = []
        for r in range(rank):
            image = known[r][0:1] * products[0]
            for k in range(1, seg + rank):
                image = image + known[r][k : k + 1] * products[k]
            images.append(image)
        inner = [
            [jnp.sum(images[r] * known[s], 0, keepdims=True) for s in range(r + 1)] for r in range(rank)
        ]
        lower, inverse = lower_factor(inner, rank)
        known = solve_rows(known, lower, inverse)
        reach = [jnp.where(of_corr, v, 0.0) for v in solve_rows(images, lower, inverse)]
    outs = [reach[r] + float(lags) * known[r] for r in range(rank)]
    window = jnp.zeros_like(known[0])
    for r in range(rank):
        window = window + jnp.sum(reach[r], 0, keepdims=True) * known[r]
    outs.append(window * (1.0 / math.sqrt(seg)))
    coefs = jnp.concatenate(outs + [jnp.zeros((HEAD - (rank + 1) * 16, LANE), F32)], 0)
    coefs = jnp.concatenate([coefs, jnp.zeros((HEAD, HEAD - LANE), F32)], 1).T[0:LANE]
    wide = dot(jnp.concatenate(two_parts(coefs), 0), spread[...])
    wide = wide[0:LANE] + wide[LANE:]
    row_of = lax.broadcasted_iota(jnp.int32, (LANE, HEAD), 0)
    lane_of = lax.broadcasted_iota(jnp.int32, (LANE, HEAD), 1)
    mine = jnp.logical_or(lane_of // seg == row_of, lane_of >= rows)
    weights = [
        jnp.where(mine, wide[:, r * HEAD : (r + 1) * HEAD], 0.0)[0:pairs] for r in range(rank + 1)
    ]
    filled = (rank + 1) * pairs
    height = -(-filled // 16) * 16
    weights = jnp.concatenate(weights + [jnp.zeros((height - filled, HEAD), F32)], 0)
    w_high, w_low = two_parts(weights)
    both = jnp.concatenate([w_high, w_low], 0)
    scale = 1.0 / math.sqrt(total_windows)
    width = lags // slices
    top = rank * pairs

    def combined(at):
        part = dot(both, high_part[:, at : at + step])
        return part[0:height] + part[height:] + dot(w_high, low_part[:, at : at + step])

    result = [jnp.concatenate([combined(side + at) for at in range(0, half, step)], 1) for side in (0, half)]
    left, right = unfold(*[one[top:] for one in result])
    win_out[:, 0:half] = left[0:pairs]
    win_out[:, half:] = right[0:pairs]
    result = [jnp.concatenate([one[0:top], one[top:] * scale], 0) for one in result]
    if first_window:
        merged_out[:, 0:half] = result[0]
        merged_out[:, half:] = result[1]
    else:
        left, right = unfold(result[0] + partial[:, 0:half], result[1] + partial[:, half:])
        for piece in range(slices // 2):
            pieces[piece] = left[:, piece * width : (piece + 1) * width]
            pieces[slices // 2 + piece] = right[:, piece * width : (piece + 1) * width]
    if not first_window:
        for piece in range(slices // 2):
            send_out[piece] = pieces[2 * piece + 1 - core[0]].astype(BF16)
            keep_out[piece] = pieces[2 * piece + core[0]]


def add_kernel(top, chip, keep, got, mine_out, *sends):
    chips, height, _ = keep.shape
    for part in range(chips):
        both = keep[part] + got[part].astype(F32)
        mine_out[part] = both
        short = both[0:top].astype(BF16)
        for out in sends:
            out[part * top : (part + 1) * top] = short
    for step, out in enumerate(sends):
        other = jnp.bitwise_xor(chip[0], step + 1)
        out[chips * top :] = mine_out[other, top:height].astype(BF16)


def gram_kernel(pairs, rank, chip, mine, *refs):
    got, (total_out, gram_out, parts) = refs[:-3], refs[-3:]
    chips, height, width = mine.shape
    top = rank * pairs
    sums = [[jnp.zeros((pairs, width), F32) for _ in range(r + 1)] for r in range(rank)]
    for part in range(chips):
        block = mine[part, 0:top].astype(BF16).astype(F32)
        for one in got:
            block = block + one[part * top : (part + 1) * top].astype(F32)
        parts[part] = block
        rows = [block[r * pairs : (r + 1) * pairs] for r in range(rank)]
        sums = [[sums[r][s] + rows[r] * rows[s] for s in range(r + 1)] for r in range(rank)]
    stack = mine[chip[0], top:height]
    for one in got:
        stack = stack + one[chips * top :].astype(F32)
    total_out[0:top] = parts[chip[0]]
    total_out[top:] = stack
    lane = lax.broadcasted_iota(jnp.int32, (pairs, 128), 1)
    gram = jnp.zeros((pairs, 128), F32)
    for r in range(rank):
        for s in range(r + 1):
            value = jnp.sum(sums[r][s], 1, keepdims=True)
            gram = jnp.where(lane == r * rank + s, value, gram)
    gram_out[...] = gram


def finish_kernel(pairs, rank, lags, total, mine, got, stack_out, basis_out):
    gram = mine[...] + got[...]
    shape = (pairs, total.shape[1])
    entries = [
        [jnp.broadcast_to(gram[:, r * rank + s : r * rank + s + 1], shape) for s in range(r + 1)]
        for r in range(rank)
    ]
    lower, inverse = lower_factor(entries, rank)
    rows = [total[r * pairs : (r + 1) * pairs] for r in range(rank)]
    for r, row in enumerate(solve_rows(rows, lower, inverse)):
        basis_out[:, r, :] = row * math.sqrt(lags)
    stack_out[...] = total[rank * pairs : (rank + 1) * pairs]


def call(kernel, out_shape, in_specs, out_specs, scratch=(), flops=0, moved=0):
    return pl.pallas_call(
        kernel,
        out_shape=out_shape,
        in_specs=in_specs,
        out_specs=out_specs,
        scratch_shapes=list(scratch),
        compiler_params=pltpu.CompilerParams(vmem_limit_bytes=12 * 1024 * 1024),
        cost_estimate=pl.CostEstimate(flops=flops, bytes_accessed=moved, transcendentals=0),
    )


def far(value):
    return pltpu.with_memory_space_constraint(value, pltpu.HBM)


def struct(shape, dtype=F32):
    return jax.ShapeDtypeStruct(shape, dtype)


def on_device(spectra, masks, pair_rows, start_basis):
    stations, windows, seg, parts, freq = spectra.shape
    rank, lags = start_basis.shape
    pairs = pair_rows.shape[0]
    groups = lax.axis_size("pairs")
    group_index = lax.axis_index("pairs")
    slices = lax.axis_size("hours")
    hour = lax.axis_index("hours")
    width = lags // slices
    chips = slices // 2
    forward = [(i, (i + 1) % groups) for i in range(groups)]
    backward = [(target, source) for source, target in forward]
    rows = pair_rows.T
    before = lax.ppermute(rows, "pairs", forward)
    after = lax.ppermute(rows, "pairs", backward)
    place = group_index.reshape(1).astype(jnp.int32)
    whitened = call(
        whiten_kernel,
        [struct((stations, parts * seg, freq), BF16)] * windows,
        [HBM] * 2,
        [VMEM] * windows,
        [
            pltpu.VMEM(spectra.shape, BF16),
            pltpu.VMEM(masks.shape, jnp.int32),
            pltpu.SemaphoreType.DMA((2,)),
        ],
    )(far(spectra), far(masks))
    block = struct((NEAR, parts * seg, freq), BF16)
    def select(wanted):
        return call(
            functools.partial(select_kernel, stations),
            [block] * windows,
            [SMEM] + [VMEM] * (1 + windows),
            [VMEM] * windows,
        )(place, wanted, *whitened)

    to_next, to_last = select(after), select(before)
    lows = [lax.ppermute(one, "pairs", forward) for one in to_next]
    highs = [lax.ppermute(one, "pairs", backward) for one in to_last]
    table, ends = kernel_table(freq, lags)
    fixed = [
        start_basis,
        jnp.asarray(table),
        jnp.asarray(ends),
        jnp.asarray(pick_matrix(pairs, seg, rank)),
        jnp.asarray(spread_matrix(pairs, seg, rank)),
    ]
    *staged, index = call(
        functools.partial(stage_kernel, groups, stations),
        [struct(one.shape, one.dtype) for one in fixed] + [struct(rows.shape, jnp.int32)],
        [SMEM, VMEM] + [HBM] * (len(fixed) + 1),
        [VMEM] * (len(fixed) + 1),
        [
            pltpu.VMEM(start_basis.shape, F32),
            pltpu.VMEM(rows.shape, jnp.int32),
            pltpu.SemaphoreType.DMA((len(fixed) + 1,)),
        ],
        moved=parts * freq * lags,
    )(place, to_next[0], far(rows), *[far(one) for one in fixed])
    core = jnp.mod(hour, 2).reshape(1).astype(jnp.int32)
    chip = (hour // 2).reshape(1).astype(jnp.int32)
    height = -(-(rank + 1) * pairs // 16) * 16
    total_windows = windows * slices
    partial, stacks = None, []
    for w in range(windows):
        last = w == windows - 1
        sizes = (pairs, seg, rank, lags, freq, total_windows, slices, w == 0)
        scratch = [
            pltpu.VMEM((stations + 2 * NEAR, parts * seg, freq), BF16),
            pltpu.VMEM((pairs * seg, parts * freq), BF16),
            pltpu.VMEM((HEAD, lags), F32),
            pltpu.VMEM((HEAD, lags), BF16),
            pltpu.VMEM((HEAD, lags), BF16),
        ]
        args = [index, whitened[w], lows[w], highs[w], *staged]
        specs = [VMEM] * len(args)
        outs = [struct((pairs, lags))]
        if w == 0:
            outs.append(struct((height, lags)))
        else:
            args += [core, partial]
            specs += [SMEM, VMEM]
            outs += [struct((chips, height, width), BF16), struct((chips, height, width))]
            scratch.append(pltpu.VMEM((slices, height, width), F32))
        result = call(
            functools.partial(window_kernel, sizes),
            outs,
            specs,
            [VMEM] * len(outs),
            scratch,
            flops=pairs * seg * parts * freq * lags,
            moved=parts * freq * lags,
        )(*args)
        stacks.append(result[0])
        if w == 0:
            partial = result[1]
        else:
            send, keep = result[1:]
    window_stacks = jnp.stack(stacks, 1)
    swap = lambda value, step: lax.ppermute(value, "hours", [(k, k ^ step) for k in range(slices)])
    got = swap(send, 1)
    top = rank * pairs
    message = struct((chips * top + height - top, width), BF16)
    mine, *sends = call(
        functools.partial(add_kernel, top),
        [struct(keep.shape)] + [message] * (chips - 1),
        [SMEM, VMEM, VMEM],
        [VMEM] * chips,
    )(chip, keep, got)
    arrived = [swap(one, 2 * (step + 1)) for step, one in reversed(list(enumerate(sends)))]
    total, gram = call(
        functools.partial(gram_kernel, pairs, rank),
        [struct((height, width)), struct((pairs, 128))],
        [SMEM] + [VMEM] * chips,
        [VMEM] * 2,
        [pltpu.VMEM((chips, top, width), F32)],
    )(chip, mine, *arrived)
    stack, basis = call(
        functools.partial(finish_kernel, pairs, rank, lags),
        [struct((pairs, width)), struct((pairs, rank, width))],
        [VMEM] * 3,
        [VMEM] * 2,
    )(total, gram, swap(gram, 1))
    return (window_stacks, stack, basis)


def solution(mesh):
    in_specs = (
        P("pairs", "hours", None, None, None),
        P("pairs", "hours", None),
        P("pairs", None),
        P(),
    )
    out_specs = (P("pairs", "hours", None), P("pairs", "hours"), P("pairs", None, "hours"))
    return jax.shard_map(
        on_device, mesh=mesh, in_specs=in_specs, out_specs=out_specs, check_vma=False
    )
```

```python
import functools
import math

import jax
import jax.numpy as jnp
import numpy as np
from jax import lax
from jax.experimental import pallas as pl
from jax.experimental.pallas import tpu as pltpu
from jax.sharding import PartitionSpec as P

BAND = 64
TURNS = 2
NEAR = 4
F32 = jnp.float32
BF16 = jnp.bfloat16
VMEM = pl.BlockSpec(memory_space=pltpu.VMEM)
SMEM = pl.BlockSpec(memory_space=pltpu.SMEM)
HBM = pl.BlockSpec(memory_space=pltpu.HBM)
HEAD = 128
LANE = 16


def kernel_table(freq, lags):
    nfft = 2 * lags
    bins = np.arange(1, freq + 1, dtype=np.int64)[:, None]
    shifts = np.append(np.arange(lags // 2, dtype=np.int64), -(lags // 2))[None, :]
    phase = np.mod(bins * shifts, nfft).astype(np.float64) * (2.0 * math.pi / nfft)
    scale = freq ** (-0.5)
    both = np.concatenate([np.cos(phase) * scale, -np.sin(phase) * scale], 0)
    both = both.astype(np.float32).astype(jnp.bfloat16)
    ends = both[:, -1].astype(np.float32).reshape(2, freq)
    return both[:, :-1], ends


def pick_matrix(pairs, seg, rank):
    pick = np.zeros((HEAD, 2 * HEAD), np.float32)
    side = (seg + rank) * LANE
    for pair in range(pairs):
        for part in range(seg):
            pick[pair * seg + part, part * LANE + pair] = 1
            pick[pair * seg + part, side + pair] = 1
    for row in range(rank):
        pick[pairs * seg + row, (seg + row) * LANE : (seg + row + 1) * LANE] = 1
    return pick.astype(jnp.bfloat16)


def spread_matrix(pairs, seg, rank):
    spread = np.zeros((HEAD, (rank + 1) * HEAD), np.float32)
    for row in range(rank + 1):
        for part in range(seg):
            for pair in range(pairs):
                spread[row * LANE + part, row * HEAD + pair * seg + part] = 1
        for other in range(rank):
            spread[row * LANE + seg + other, row * HEAD + pairs * seg + other] = 1
    return spread.astype(jnp.bfloat16)


def two_parts(values):
    high = values.astype(BF16)
    return high, (values - high.astype(F32)).astype(BF16)


def three_parts(values):
    high = values.astype(BF16)
    rest = values - high.astype(F32)
    mid = rest.astype(BF16)
    return high, mid, (rest - mid.astype(F32)).astype(BF16)


def dot(left, right):
    return jnp.dot(left, right, preferred_element_type=F32)


def dot_rows(left, right):
    return lax.dot_general(left, right, (((1,), (1,)), ((), ())), preferred_element_type=F32)


def lower_factor(gram, rank):
    lower = [[None] * rank for _ in range(rank)]
    inverse = [None] * rank
    for row in range(rank):
        for col in range(row + 1):
            total = gram[row][col]
            for inner in range(col):
                total = total - lower[row][inner] * lower[col][inner]
            if row == col:
                inverse[row] = lax.rsqrt(total)
                lower[row][row] = total * inverse[row]
            else:
                lower[row][col] = total * inverse[col]
    return lower, inverse


def solve_rows(rows, lower, inverse):
    result = []
    for row, current in enumerate(rows):
        for inner in range(row):
            current = current - lower[row][inner] * result[inner]
        result.append(current * inverse[row])
    return result


def used_stations(second, low, stations):
    number = lax.broadcasted_iota(jnp.int32, (stations, second.shape[1]), 0)
    return jnp.max(jnp.where(second == low + number, 1.0, 0.0), 1, keepdims=True)


def flip(values):
    rows, width = values.shape
    back = 127 - lax.broadcasted_iota(jnp.int32, (rows, 128), 1)
    turned = []
    for at in range(width - 128, -1, -128):
        turned.append(jnp.take_along_axis(values[:, at : at + 128], back, axis=1))
    return jnp.concatenate(turned, 1)


def first_lane(values, first, other):
    lane = lax.broadcasted_iota(jnp.int32, values, 1)
    return jnp.where(lane == 0, first, other)


def unfold(even, odd):
    shape = even.shape
    root = math.sqrt(2.0)
    right = first_lane(shape, even * root, even + odd)
    left = first_lane(shape, odd * root, even - odd)
    return flip(pltpu.roll(left, shape[1] - 1, 1)), right


def stage_kernel(groups, stations, place, early, far_rows, *refs):
    *refs, index, natural, rows, sems = refs
    count = len(refs) // 2
    sources, targets = refs[:count], refs[count:]
    copies = [
        pltpu.make_async_copy(source, target, sems.at[number])
        for number, (source, target) in enumerate(zip(sources, (natural, *targets[1:])))
    ]
    for copy in copies:
        copy.start()
    known = pltpu.make_async_copy(far_rows, rows, sems.at[count])
    known.start()
    known.wait()
    before = lax.rem(place[0] + groups - 1, groups) * stations
    after = lax.rem(place[0] + 1, groups) * stations
    own = place[0] * stations
    second = rows[1:2]
    in_before = jnp.logical_and(second >= before, second < before + stations)
    in_own = jnp.logical_and(second >= own, second < own + stations)
    local = second - jnp.where(in_before, before, jnp.where(in_own, own, after))
    below = lax.broadcasted_iota(jnp.int32, (stations, second.shape[1]), 0) < local
    slots = [
        jnp.sum(jnp.where(below, used_stations(second, low, stations), 0.0), 0, keepdims=True)
        for low in (before, after)
    ]
    spot = jnp.where(in_own, NEAR + local, NEAR + stations + slots[1].astype(jnp.int32))
    index[0:1] = rows[0:1] - own
    index[1:2] = jnp.where(in_before, slots[0].astype(jnp.int32), spot)
    copies[0].wait()
    values = natural[...]
    half = values.shape[1] // 2
    right = values[:, half:]
    left = pltpu.roll(flip(values[:, :half]), 1, 1)
    shape = right.shape
    root = math.sqrt(0.5)
    targets[0][:, :half] = first_lane(shape, right * root, (right + left) * 0.5)
    targets[0][:, half:] = first_lane(shape, left * root, (right - left) * 0.5)
    for copy in copies[1:]:
        copy.wait()


def whiten_kernel(far_spectra, far_masks, *refs):
    whitened, (spectra, masks, sems) = refs[:-3], refs[-3:]
    stations, windows, seg, _, freq = spectra.shape
    small = [pltpu.make_async_copy(far_masks, masks, sems.at[0])]
    large = [pltpu.make_async_copy(far_spectra, spectra, sems.at[1])]
    for copy in small + large:
        copy.start()
    tile = (128, 128)
    same = lax.broadcasted_iota(jnp.int32, tile, 0) // BAND == lax.broadcasted_iota(jnp.int32, tile, 1) // BAND
    bands = jnp.where(same, 1.0, 0.0).astype(BF16)
    for copy in small:
        copy.wait()
    eye = lax.broadcasted_iota(jnp.int32, (seg, seg), 0) == lax.broadcasted_iota(jnp.int32, (seg, seg), 1)
    open_rows = []
    for station in range(stations):
        for window in range(windows):
            mask = masks[station, window : window + 1].astype(F32)
            mask = jnp.where(eye, jnp.broadcast_to(mask, (seg, seg)), 0.0)
            open_rows.append(jnp.sum(mask, 1, keepdims=True))
    large[0].wait()
    values, squares = [], []
    for station in range(stations):
        for window in range(windows):
            block = spectra[station, window].astype(F32)
            real, imag = block[:, 0], block[:, 1]
            values.append((real, imag))
            squares.append(real * real + imag * imag)
    height = len(values) * seg
    squares = jnp.concatenate(squares, 0)
    here = jnp.concatenate(open_rows, 0)
    scales = []
    for at in range(0, freq, 128):
        power = dot(jnp.concatenate(two_parts(squares[:, at : at + 128]), 1), jnp.concatenate([bands, bands], 0))
        scales.append(lax.rsqrt(power * (1.0 / (2 * BAND)) + 1e-06) * here)
    scale = jnp.concatenate(scales, 1)
    for number, (real, imag) in enumerate(values):
        here = scale[number * seg : (number + 1) * seg]
        block = jnp.concatenate([real * here, imag * here], 0).astype(BF16)
        whitened[number % windows][number // windows] = block


def select_kernel(stations, place, early, rows, *refs):
    windows = len(refs) // 2
    used = used_stations(rows[1:2], place[0] * stations, stations)
    weight = jnp.left_shift(1, lax.broadcasted_iota(jnp.int32, (stations, 1), 0)).astype(F32)
    needed = jnp.sum(used * weight).astype(jnp.int32)
    slot = jnp.int32(0)
    for station in range(stations):
        wanted = jnp.bitwise_and(jnp.right_shift(needed, station), 1)
        spot = jnp.minimum(slot, NEAR - 1)

        @pl.when(wanted == 1)
        def _():
            for source, target in zip(refs[:windows], refs[windows:]):
                target[spot] = source[station]

        slot = slot + wanted


def window_kernel(sizes, index, own, low, high, start, table, ends, pick, spread, *refs):
    pairs, seg, rank, lags, freq, total_windows, slices, first_window = sizes
    rows = pairs * seg
    if first_window:
        win_out, merged_out, near, cross, vectors, high_part, low_part = refs
    else:
        (core, partial, win_out, send_out, keep_out, near, cross, vectors, high_part, low_part, pieces) = refs
    stations = own.shape[0]
    half = lags // 2
    picked = index[...]
    near[0:NEAR] = low[...]
    near[NEAR : NEAR + stations] = own[...]
    near[NEAR + stations :] = high[...]
    edges = []
    for pair in range(0, pairs, 2):
        real, imag = [], []
        for one in (pair, pair + 1):
            a = own[picked[0, one]].astype(F32)
            b = near[picked[1, one]].astype(F32)
            a_re, a_im, b_re, b_im = a[:seg], a[seg:], b[:seg], b[seg:]
            real.append(a_re * b_re + a_im * b_im)
            imag.append(a_im * b_re - a_re * b_im)
        block = pl.ds(pair * seg, 2 * seg)
        real = jnp.concatenate(real, 0).astype(BF16)
        imag = jnp.concatenate(imag, 0).astype(BF16)
        cross[block, 0:freq] = real
        cross[block, freq:] = imag
        last = real.astype(F32) * ends[0:1] + imag.astype(F32) * ends[1:2]
        edges.append(jnp.sum(last, 1, keepdims=True))
    vectors[rows : rows + rank] = start[...]
    vectors[rows + rank :] = jnp.zeros((HEAD - rows - rank, lags), F32)
    step = 512
    for at in range(0, half, step):
        vectors[0:rows, at : at + step] = dot(cross[:, 0:freq], table[0:freq, at : at + step])
        vectors[0:rows, half + at : half + at + step] = dot(cross[:, freq:], table[freq:, at : at + step])
    shape = (rows, 128)
    root = math.sqrt(0.5)
    column = vectors[0:rows, 0:128]
    vectors[0:rows, 0:128] = first_lane(shape, column * root, column)
    edge = jnp.broadcast_to(jnp.concatenate(edges, 0) * root, shape)
    vectors[0:rows, half : half + 128] = first_lane(shape, edge, vectors[0:rows, half : half + 128])
    every = vectors[...]
    high_part[...] = every.astype(BF16)
    low_part[...] = (every - high_part[...].astype(F32)).astype(BF16)
    gram = dot_rows(high_part[...], high_part[...])
    side = dot_rows(low_part[...], high_part[...])
    gram = 2.0 * (gram + side + side.T)
    lane = lax.broadcasted_iota(jnp.int32, (seg, HEAD), 1)
    sub = lax.broadcasted_iota(jnp.int32, (seg, HEAD), 0)
    blocks = jnp.zeros((seg, HEAD), F32)
    for pair in range(pairs):
        blocks = blocks + jnp.where(lane // seg == pair, gram[pair * seg : (pair + 1) * seg], 0.0)
    basis_rows = gram[rows : rows + 8]
    turned = [
        jnp.where(lane % seg == sub, jnp.broadcast_to(basis_rows[row : row + 1], (seg, HEAD)), 0.0)
        for row in range(rank)
    ]
    stacked = jnp.concatenate([blocks, basis_rows] + turned, 0)
    count = stacked.shape[0]
    moved = dot(jnp.concatenate(three_parts(stacked), 0), pick[...])
    moved = moved[0:count] + moved[count : 2 * count] + moved[2 * count :]
    products = [moved[0:16, k * LANE : (k + 1) * LANE] for k in range(seg)]
    side_at = (seg + rank) * LANE
    for row in range(rank):
        upper = moved[16 + row * seg : 16 + (row + 1) * seg, side_at : side_at + LANE]
        under = moved[8:16, (seg + row) * LANE : (seg + row + 1) * LANE]
        products.append(jnp.concatenate([upper, under], 0))
    level = lax.broadcasted_iota(jnp.int32, (16, LANE), 0)
    of_corr = level < seg
    known = [jnp.where(level == seg + row, 1.0, 0.0) for row in range(rank)]
    reach = [jnp.where(of_corr, products[seg + row], 0.0) for row in range(rank)]
    for turn in range(TURNS):
        known = [known[r] + reach[r] * (1.0 / lags) for r in range(rank)]
        images = []
        for r in range(rank):
            image = known[r][0:1] * products[0]
            for k in range(1, seg + rank):
                image = image + known[r][k : k + 1] * products[k]
            images.append(image)
        inner = [
            [jnp.sum(images[r] * known[s], 0, keepdims=True) for s in range(r + 1)] for r in range(rank)
        ]
        lower, inverse = lower_factor(inner, rank)
        known = solve_rows(known, lower, inverse)
        reach = [jnp.where(of_corr, v, 0.0) for v in solve_rows(images, lower, inverse)]
    outs = [reach[r] + float(lags) * known[r] for r in range(rank)]
    window = jnp.zeros_like(known[0])
    for r in range(rank):
        window = window + jnp.sum(reach[r], 0, keepdims=True) * known[r]
    outs.append(window * (1.0 / math.sqrt(seg)))
    coefs = jnp.concatenate(outs + [jnp.zeros((HEAD - (rank + 1) * 16, LANE), F32)], 0)
    coefs = jnp.concatenate([coefs, jnp.zeros((HEAD, HEAD - LANE), F32)], 1).T[0:LANE]
    wide = dot(jnp.concatenate(two_parts(coefs), 0), spread[...])
    wide = wide[0:LANE] + wide[LANE:]
    row_of = lax.broadcasted_iota(jnp.int32, (LANE, HEAD), 0)
    lane_of = lax.broadcasted_iota(jnp.int32, (LANE, HEAD), 1)
    mine = jnp.logical_or(lane_of // seg == row_of, lane_of >= rows)
    weights = [
        jnp.where(mine, wide[:, r * HEAD : (r + 1) * HEAD], 0.0)[0:pairs] for r in range(rank + 1)
    ]
    filled = (rank + 1) * pairs
    height = -(-filled // 16) * 16
    weights = jnp.concatenate(weights + [jnp.zeros((height - filled, HEAD), F32)], 0)
    w_high, w_low = two_parts(weights)
    both = jnp.concatenate([w_high, w_low], 0)
    scale = 1.0 / math.sqrt(total_windows)
    width = lags // slices
    top = rank * pairs

    def combined(at):
        part = dot(both, high_part[:, at : at + step])
        return part[0:height] + part[height:] + dot(w_high, low_part[:, at : at + step])

    result = [jnp.concatenate([combined(side + at) for at in range(0, half, step)], 1) for side in (0, half)]
    left, right = unfold(*[one[top:] for one in result])
    win_out[:, 0:half] = left[0:pairs]
    win_out[:, half:] = right[0:pairs]
    result = [jnp.concatenate([one[0:top], one[top:] * scale], 0) for one in result]
    if first_window:
        merged_out[:, 0:half] = result[0]
        merged_out[:, half:] = result[1]
    else:
        left, right = unfold(result[0] + partial[:, 0:half], result[1] + partial[:, half:])
        for piece in range(slices // 2):
            pieces[piece] = left[:, piece * width : (piece + 1) * width]
            pieces[slices // 2 + piece] = right[:, piece * width : (piece + 1) * width]
    if not first_window:
        for piece in range(slices // 2):
            send_out[piece] = pieces[2 * piece + 1 - core[0]].astype(BF16)
            keep_out[piece] = pieces[2 * piece + core[0]]


def add_kernel(top, chip, keep, got, mine_out, *sends):
    chips, height, _ = keep.shape
    for part in range(chips):
        both = keep[part] + got[part].astype(F32)
        mine_out[part] = both
        short = both[0:top].astype(BF16)
        for out in sends:
            out[part * top : (part + 1) * top] = short
    for step, out in enumerate(sends):
        other = jnp.bitwise_xor(chip[0], step + 1)
        out[chips * top :] = mine_out[other, top:height].astype(BF16)


def gram_kernel(pairs, rank, chip, mine, *refs):
    got, (total_out, gram_out, parts) = refs[:-3], refs[-3:]
    chips, height, width = mine.shape
    top = rank * pairs
    sums = [[jnp.zeros((pairs, width), F32) for _ in range(r + 1)] for r in range(rank)]
    for part in range(chips):
        block = mine[part, 0:top].astype(BF16).astype(F32)
        for one in got:
            block = block + one[part * top : (part + 1) * top].astype(F32)
        parts[part] = block
        rows = [block[r * pairs : (r + 1) * pairs] for r in range(rank)]
        sums = [[sums[r][s] + rows[r] * rows[s] for s in range(r + 1)] for r in range(rank)]
    stack = mine[chip[0], top:height]
    for one in got:
        stack = stack + one[chips * top :].astype(F32)
    total_out[0:top] = parts[chip[0]]
    total_out[top:] = stack
    lane = lax.broadcasted_iota(jnp.int32, (pairs, 128), 1)
    gram = jnp.zeros((pairs, 128), F32)
    for r in range(rank):
        for s in range(r + 1):
            value = jnp.sum(sums[r][s], 1, keepdims=True)
            gram = jnp.where(lane == r * rank + s, value, gram)
    gram_out[...] = gram


def finish_kernel(pairs, rank, lags, total, mine, got, stack_out, basis_out):
    gram = mine[...] + got[...]
    shape = (pairs, total.shape[1])
    entries = [
        [jnp.broadcast_to(gram[:, r * rank + s : r * rank + s + 1], shape) for s in range(r + 1)]
        for r in range(rank)
    ]
    lower, inverse = lower_factor(entries, rank)
    rows = [total[r * pairs : (r + 1) * pairs] for r in range(rank)]
    for r, row in enumerate(solve_rows(rows, lower, inverse)):
        basis_out[:, r, :] = row * math.sqrt(lags)
    stack_out[...] = total[rank * pairs : (rank + 1) * pairs]


def call(kernel, out_shape, in_specs, out_specs, scratch=(), flops=0, moved=0):
    return pl.pallas_call(
        kernel,
        out_shape=out_shape,
        in_specs=in_specs,
        out_specs=out_specs,
        scratch_shapes=list(scratch),
        compiler_params=pltpu.CompilerParams(vmem_limit_bytes=12 * 1024 * 1024),
        cost_estimate=pl.CostEstimate(flops=flops, bytes_accessed=moved, transcendentals=0),
    )


def far(value):
    return pltpu.with_memory_space_constraint(value, pltpu.HBM)


def struct(shape, dtype=F32):
    return jax.ShapeDtypeStruct(shape, dtype)


def on_device(spectra, masks, pair_rows, start_basis):
    stations, windows, seg, parts, freq = spectra.shape
    rank, lags = start_basis.shape
    pairs = pair_rows.shape[0]
    groups = lax.axis_size("pairs")
    group_index = lax.axis_index("pairs")
    slices = lax.axis_size("hours")
    hour = lax.axis_index("hours")
    width = lags // slices
    chips = slices // 2
    forward = [(i, (i + 1) % groups) for i in range(groups)]
    backward = [(target, source) for source, target in forward]
    rows = pair_rows.T
    before = lax.ppermute(rows, "pairs", forward)
    after = lax.ppermute(rows, "pairs", backward)
    place = group_index.reshape(1).astype(jnp.int32)
    whitened = call(
        whiten_kernel,
        [struct((stations, parts * seg, freq), BF16)] * windows,
        [HBM] * 2,
        [VMEM] * windows,
        [
            pltpu.VMEM(spectra.shape, BF16),
            pltpu.VMEM(masks.shape, jnp.int32),
            pltpu.SemaphoreType.DMA((2,)),
        ],
    )(far(spectra), far(masks))
    block = struct((NEAR, parts * seg, freq), BF16)
    def select(wanted, early):
        return call(
            functools.partial(select_kernel, stations),
            [block] * windows,
            [SMEM] + [VMEM] * (2 + windows),
            [VMEM] * windows,
        )(place, early, wanted, *whitened)

    to_next = select(after, whitened[0])
    to_last = select(before, to_next[0])
    lows = [lax.ppermute(one, "pairs", forward) for one in to_next]
    highs = [lax.ppermute(one, "pairs", backward) for one in to_last]
    table, ends = kernel_table(freq, lags)
    fixed = [
        start_basis,
        jnp.asarray(table),
        jnp.asarray(ends),
        jnp.asarray(pick_matrix(pairs, seg, rank)),
        jnp.asarray(spread_matrix(pairs, seg, rank)),
    ]
    *staged, index = call(
        functools.partial(stage_kernel, groups, stations),
        [struct(one.shape, one.dtype) for one in fixed] + [struct(rows.shape, jnp.int32)],
        [SMEM, VMEM] + [HBM] * (len(fixed) + 1),
        [VMEM] * (len(fixed) + 1),
        [
            pltpu.VMEM(start_basis.shape, F32),
            pltpu.VMEM(rows.shape, jnp.int32),
            pltpu.SemaphoreType.DMA((len(fixed) + 1,)),
        ],
        moved=parts * freq * lags,
    )(place, to_next[0], far(rows), *[far(one) for one in fixed])
    core = jnp.mod(hour, 2).reshape(1).astype(jnp.int32)
    chip = (hour // 2).reshape(1).astype(jnp.int32)
    height = -(-(rank + 1) * pairs // 16) * 16
    total_windows = windows * slices
    partial, stacks = None, []
    for w in range(windows):
        last = w == windows - 1
        sizes = (pairs, seg, rank, lags, freq, total_windows, slices, w == 0)
        scratch = [
            pltpu.VMEM((stations + 2 * NEAR, parts * seg, freq), BF16),
            pltpu.VMEM((pairs * seg, parts * freq), BF16),
            pltpu.VMEM((HEAD, lags), F32),
            pltpu.VMEM((HEAD, lags), BF16),
            pltpu.VMEM((HEAD, lags), BF16),
        ]
        args = [index, whitened[w], lows[w], highs[w], *staged]
        specs = [VMEM] * len(args)
        outs = [struct((pairs, lags))]
        if w == 0:
            outs.append(struct((height, lags)))
        else:
            args += [core, partial]
            specs += [SMEM, VMEM]
            outs += [struct((chips, height, width), BF16), struct((chips, height, width))]
            scratch.append(pltpu.VMEM((slices, height, width), F32))
        result = call(
            functools.partial(window_kernel, sizes),
            outs,
            specs,
            [VMEM] * len(outs),
            scratch,
            flops=pairs * seg * parts * freq * lags,
            moved=parts * freq * lags,
        )(*args)
        stacks.append(result[0])
        if w == 0:
            partial = result[1]
        else:
            send, keep = result[1:]
    window_stacks = jnp.stack(stacks, 1)
    swap = lambda value, step: lax.ppermute(value, "hours", [(k, k ^ step) for k in range(slices)])
    got = swap(send, 1)
    top = rank * pairs
    message = struct((chips * top + height - top, width), BF16)
    mine, *sends = call(
        functools.partial(add_kernel, top),
        [struct(keep.shape)] + [message] * (chips - 1),
        [SMEM, VMEM, VMEM],
        [VMEM] * chips,
    )(chip, keep, got)
    arrived = [swap(one, 2 * (step + 1)) for step, one in reversed(list(enumerate(sends)))]
    total, gram = call(
        functools.partial(gram_kernel, pairs, rank),
        [struct((height, width)), struct((pairs, 128))],
        [SMEM] + [VMEM] * chips,
        [VMEM] * 2,
        [pltpu.VMEM((chips, top, width), F32)],
    )(chip, mine, *arrived)
    stack, basis = call(
        functools.partial(finish_kernel, pairs, rank, lags),
        [struct((pairs, width)), struct((pairs, rank, width))],
        [VMEM] * 3,
        [VMEM] * 2,
    )(total, gram, swap(gram, 1))
    return (window_stacks, stack, basis)


def solution(mesh):
    in_specs = (
        P("pairs", "hours", None, None, None),
        P("pairs", "hours", None),
        P("pairs", None),
        P(),
    )
    out_specs = (P("pairs", "hours", None), P("pairs", "hours"), P("pairs", None, "hours"))
    return jax.shard_map(
        on_device, mesh=mesh, in_specs=in_specs, out_specs=out_specs, check_vma=False
    )
```

```python
import functools
import math

import jax
import jax.numpy as jnp
import numpy as np
from jax import lax
from jax.experimental import pallas as pl
from jax.experimental.pallas import tpu as pltpu
from jax.sharding import PartitionSpec as P

BAND = 64
TURNS = 2
NEAR = 4
F32 = jnp.float32
BF16 = jnp.bfloat16
VMEM = pl.BlockSpec(memory_space=pltpu.VMEM)
SMEM = pl.BlockSpec(memory_space=pltpu.SMEM)
HBM = pl.BlockSpec(memory_space=pltpu.HBM)
HEAD = 128
LANE = 16


def kernel_table(freq, lags):
    nfft = 2 * lags
    bins = np.arange(1, freq + 1, dtype=np.int64)[:, None]
    shifts = np.append(np.arange(lags // 2, dtype=np.int64), -(lags // 2))[None, :]
    phase = np.mod(bins * shifts, nfft).astype(np.float64) * (2.0 * math.pi / nfft)
    scale = freq ** (-0.5)
    both = np.concatenate([np.cos(phase) * scale, -np.sin(phase) * scale], 0)
    both = both.astype(np.float32).astype(jnp.bfloat16)
    ends = both[:, -1].astype(np.float32).reshape(2, freq)
    return both[:, :-1], ends


def pick_matrix(pairs, seg, rank):
    pick = np.zeros((HEAD, 2 * HEAD), np.float32)
    side = (seg + rank) * LANE
    for pair in range(pairs):
        for part in range(seg):
            pick[pair * seg + part, part * LANE + pair] = 1
            pick[pair * seg + part, side + pair] = 1
    for row in range(rank):
        pick[pairs * seg + row, (seg + row) * LANE : (seg + row + 1) * LANE] = 1
    return pick.astype(jnp.bfloat16)


def spread_matrix(pairs, seg, rank):
    spread = np.zeros((HEAD, (rank + 1) * HEAD), np.float32)
    for row in range(rank + 1):
        for part in range(seg):
            for pair in range(pairs):
                spread[row * LANE + part, row * HEAD + pair * seg + part] = 1
        for other in range(rank):
            spread[row * LANE + seg + other, row * HEAD + pairs * seg + other] = 1
    return spread.astype(jnp.bfloat16)


def two_parts(values):
    high = values.astype(BF16)
    return high, (values - high.astype(F32)).astype(BF16)


def three_parts(values):
    high = values.astype(BF16)
    rest = values - high.astype(F32)
    mid = rest.astype(BF16)
    return high, mid, (rest - mid.astype(F32)).astype(BF16)


def dot(left, right):
    return jnp.dot(left, right, preferred_element_type=F32)


def dot_rows(left, right):
    return lax.dot_general(left, right, (((1,), (1,)), ((), ())), preferred_element_type=F32)


def lower_factor(gram, rank):
    lower = [[None] * rank for _ in range(rank)]
    inverse = [None] * rank
    for row in range(rank):
        for col in range(row + 1):
            total = gram[row][col]
            for inner in range(col):
                total = total - lower[row][inner] * lower[col][inner]
            if row == col:
                inverse[row] = lax.rsqrt(total)
                lower[row][row] = total * inverse[row]
            else:
                lower[row][col] = total * inverse[col]
    return lower, inverse


def solve_rows(rows, lower, inverse):
    result = []
    for row, current in enumerate(rows):
        for inner in range(row):
            current = current - lower[row][inner] * result[inner]
        result.append(current * inverse[row])
    return result


def used_stations(second, low, stations):
    number = lax.broadcasted_iota(jnp.int32, (stations, second.shape[1]), 0)
    return jnp.max(jnp.where(second == low + number, 1.0, 0.0), 1, keepdims=True)


def flip(values):
    rows, width = values.shape
    back = 127 - lax.broadcasted_iota(jnp.int32, (rows, 128), 1)
    turned = []
    for at in range(width - 128, -1, -128):
        turned.append(jnp.take_along_axis(values[:, at : at + 128], back, axis=1))
    return jnp.concatenate(turned, 1)


def first_lane(values, first, other):
    lane = lax.broadcasted_iota(jnp.int32, values, 1)
    return jnp.where(lane == 0, first, other)


def unfold(even, odd):
    shape = even.shape
    root = math.sqrt(2.0)
    right = first_lane(shape, even * root, even + odd)
    left = first_lane(shape, odd * root, even - odd)
    return flip(pltpu.roll(left, shape[1] - 1, 1)), right


def stage_kernel(groups, stations, place, early, far_rows, *refs):
    *refs, index, natural, rows, sems = refs
    count = len(refs) // 2
    sources, targets = refs[:count], refs[count:]
    copies = [
        pltpu.make_async_copy(source, target, sems.at[number])
        for number, (source, target) in enumerate(zip(sources, (natural, *targets[1:])))
    ]
    for copy in copies:
        copy.start()
    known = pltpu.make_async_copy(far_rows, rows, sems.at[count])
    known.start()
    known.wait()
    before = lax.rem(place[0] + groups - 1, groups) * stations
    after = lax.rem(place[0] + 1, groups) * stations
    own = place[0] * stations
    second = rows[1:2]
    in_before = jnp.logical_and(second >= before, second < before + stations)
    in_own = jnp.logical_and(second >= own, second < own + stations)
    local = second - jnp.where(in_before, before, jnp.where(in_own, own, after))
    below = lax.broadcasted_iota(jnp.int32, (stations, second.shape[1]), 0) < local
    slots = [
        jnp.sum(jnp.where(below, used_stations(second, low, stations), 0.0), 0, keepdims=True)
        for low in (before, after)
    ]
    spot = jnp.where(in_own, NEAR + local, NEAR + stations + slots[1].astype(jnp.int32))
    index[0:1] = rows[0:1] - own
    index[1:2] = jnp.where(in_before, slots[0].astype(jnp.int32), spot)
    copies[0].wait()
    values = natural[...]
    half = values.shape[1] // 2
    right = values[:, half:]
    left = pltpu.roll(flip(values[:, :half]), 1, 1)
    shape = right.shape
    root = math.sqrt(0.5)
    targets[0][:, :half] = first_lane(shape, right * root, (right + left) * 0.5)
    targets[0][:, half:] = first_lane(shape, left * root, (right - left) * 0.5)
    for copy in copies[1:]:
        copy.wait()


def whiten_kernel(far_spectra, far_masks, *refs):
    whitened, (spectra, masks, sems) = refs[:-3], refs[-3:]
    stations, windows, seg, _, freq = spectra.shape
    small = [pltpu.make_async_copy(far_masks, masks, sems.at[0])]
    large = [pltpu.make_async_copy(far_spectra, spectra, sems.at[1])]
    for copy in small + large:
        copy.start()
    tile = (128, 128)
    same = lax.broadcasted_iota(jnp.int32, tile, 0) // BAND == lax.broadcasted_iota(jnp.int32, tile, 1) // BAND
    bands = jnp.where(same, 1.0, 0.0).astype(BF16)
    for copy in small:
        copy.wait()
    eye = lax.broadcasted_iota(jnp.int32, (seg, seg), 0) == lax.broadcasted_iota(jnp.int32, (seg, seg), 1)
    open_rows = []
    for station in range(stations):
        for window in range(windows):
            mask = masks[station, window : window + 1].astype(F32)
            mask = jnp.where(eye, jnp.broadcast_to(mask, (seg, seg)), 0.0)
            open_rows.append(jnp.sum(mask, 1, keepdims=True))
    large[0].wait()
    values, squares = [], []
    for station in range(stations):
        for window in range(windows):
            block = spectra[station, window].astype(F32)
            real, imag = block[:, 0], block[:, 1]
            values.append((real, imag))
            squares.append(real * real + imag * imag)
    height = len(values) * seg
    squares = jnp.concatenate(squares, 0)
    here = jnp.concatenate(open_rows, 0)
    scales = []
    for at in range(0, freq, 128):
        power = dot(jnp.concatenate(two_parts(squares[:, at : at + 128]), 1), jnp.concatenate([bands, bands], 0))
        scales.append(lax.rsqrt(power * (1.0 / (2 * BAND)) + 1e-06) * here)
    scale = jnp.concatenate(scales, 1)
    for number, (real, imag) in enumerate(values):
        here = scale[number * seg : (number + 1) * seg]
        block = jnp.concatenate([real * here, imag * here], 0).astype(BF16)
        whitened[number % windows][number // windows] = block


def select_kernel(stations, place, early, rows, *refs):
    windows = len(refs) // 2
    used = used_stations(rows[1:2], place[0] * stations, stations)
    weight = jnp.left_shift(1, lax.broadcasted_iota(jnp.int32, (stations, 1), 0)).astype(F32)
    needed = jnp.sum(used * weight).astype(jnp.int32)
    slot = jnp.int32(0)
    for station in range(stations):
        wanted = jnp.bitwise_and(jnp.right_shift(needed, station), 1)
        spot = jnp.minimum(slot, NEAR - 1)

        @pl.when(wanted == 1)
        def _():
            for source, target in zip(refs[:windows], refs[windows:]):
                target[spot] = source[station]

        slot = slot + wanted


def window_kernel(sizes, index, own, low, high, start, table, ends, pick, spread, *refs):
    pairs, seg, rank, lags, freq, total_windows, slices, first_window = sizes
    rows = pairs * seg
    if first_window:
        win_out, merged_out, near, cross, vectors, high_part, low_part = refs
    else:
        (core, partial, win_out, send_out, keep_out, near, cross, vectors, high_part, low_part, pieces) = refs
    stations = own.shape[0]
    half = lags // 2
    picked = index[...]
    near[0:NEAR] = low[...]
    near[NEAR : NEAR + stations] = own[...]
    near[NEAR + stations :] = high[...]
    edges = []
    for pair in range(0, pairs, 2):
        real, imag = [], []
        for one in (pair, pair + 1):
            a = own[picked[0, one]].astype(F32)
            b = near[picked[1, one]].astype(F32)
            a_re, a_im, b_re, b_im = a[:seg], a[seg:], b[:seg], b[seg:]
            real.append(a_re * b_re + a_im * b_im)
            imag.append(a_im * b_re - a_re * b_im)
        block = pl.ds(pair * seg, 2 * seg)
        real = jnp.concatenate(real, 0).astype(BF16)
        imag = jnp.concatenate(imag, 0).astype(BF16)
        cross[block, 0:freq] = real
        cross[block, freq:] = imag
        last = real.astype(F32) * ends[0:1] + imag.astype(F32) * ends[1:2]
        edges.append(jnp.sum(last, 1, keepdims=True))
    vectors[rows : rows + rank] = start[...]
    vectors[rows + rank :] = jnp.zeros((HEAD - rows - rank, lags), F32)
    step = 512
    for at in range(0, half, step):
        for part in (0, 1):
            block = cross[:, part * freq : (part + 1) * freq]
            block = jnp.concatenate([block, block[0 : HEAD - rows]], 0)
            block = dot(block, table[part * freq : (part + 1) * freq, at : at + step])
            vectors[0:rows, part * half + at : part * half + at + step] = block[0:rows]
    shape = (rows, 128)
    root = math.sqrt(0.5)
    column = vectors[0:rows, 0:128]
    vectors[0:rows, 0:128] = first_lane(shape, column * root, column)
    edge = jnp.broadcast_to(jnp.concatenate(edges, 0) * root, shape)
    vectors[0:rows, half : half + 128] = first_lane(shape, edge, vectors[0:rows, half : half + 128])
    every = vectors[...]
    high_part[...] = every.astype(BF16)
    low_part[...] = (every - high_part[...].astype(F32)).astype(BF16)
    gram = dot_rows(high_part[...], high_part[...])
    side = dot_rows(low_part[...], high_part[...])
    gram = 2.0 * (gram + side + side.T)
    lane = lax.broadcasted_iota(jnp.int32, (seg, HEAD), 1)
    sub = lax.broadcasted_iota(jnp.int32, (seg, HEAD), 0)
    blocks = jnp.zeros((seg, HEAD), F32)
    for pair in range(pairs):
        blocks = blocks + jnp.where(lane // seg == pair, gram[pair * seg : (pair + 1) * seg], 0.0)
    basis_rows = gram[rows : rows + 8]
    turned = [
        jnp.where(lane % seg == sub, jnp.broadcast_to(basis_rows[row : row + 1], (seg, HEAD)), 0.0)
        for row in range(rank)
    ]
    stacked = jnp.concatenate([blocks, basis_rows] + turned, 0)
    count = stacked.shape[0]
    moved = dot(jnp.concatenate(three_parts(stacked), 0), pick[...])
    moved = moved[0:count] + moved[count : 2 * count] + moved[2 * count :]
    products = [moved[0:16, k * LANE : (k + 1) * LANE] for k in range(seg)]
    side_at = (seg + rank) * LANE
    for row in range(rank):
        upper = moved[16 + row * seg : 16 + (row + 1) * seg, side_at : side_at + LANE]
        under = moved[8:16, (seg + row) * LANE : (seg + row + 1) * LANE]
        products.append(jnp.concatenate([upper, under], 0))
    level = lax.broadcasted_iota(jnp.int32, (16, LANE), 0)
    of_corr = level < seg
    known = [jnp.where(level == seg + row, 1.0, 0.0) for row in range(rank)]
    reach = [jnp.where(of_corr, products[seg + row], 0.0) for row in range(rank)]
    for turn in range(TURNS):
        known = [known[r] + reach[r] * (1.0 / lags) for r in range(rank)]
        images = []
        for r in range(rank):
            image = known[r][0:1] * products[0]
            for k in range(1, seg + rank):
                image = image + known[r][k : k + 1] * products[k]
            images.append(image)
        inner = [
            [jnp.sum(images[r] * known[s], 0, keepdims=True) for s in range(r + 1)] for r in range(rank)
        ]
        lower, inverse = lower_factor(inner, rank)
        known = solve_rows(known, lower, inverse)
        reach = [jnp.where(of_corr, v, 0.0) for v in solve_rows(images, lower, inverse)]
    outs = [reach[r] + float(lags) * known[r] for r in range(rank)]
    window = jnp.zeros_like(known[0])
    for r in range(rank):
        window = window + jnp.sum(reach[r], 0, keepdims=True) * known[r]
    outs.append(window * (1.0 / math.sqrt(seg)))
    coefs = jnp.concatenate(outs + [jnp.zeros((HEAD - (rank + 1) * 16, LANE), F32)], 0)
    coefs = jnp.concatenate([coefs, jnp.zeros((HEAD, HEAD - LANE), F32)], 1).T[0:LANE]
    wide = dot(jnp.concatenate(two_parts(coefs), 0), spread[...])
    wide = wide[0:LANE] + wide[LANE:]
    row_of = lax.broadcasted_iota(jnp.int32, (LANE, HEAD), 0)
    lane_of = lax.broadcasted_iota(jnp.int32, (LANE, HEAD), 1)
    mine = jnp.logical_or(lane_of // seg == row_of, lane_of >= rows)
    weights = [
        jnp.where(mine, wide[:, r * HEAD : (r + 1) * HEAD], 0.0)[0:pairs] for r in range(rank + 1)
    ]
    filled = (rank + 1) * pairs
    height = -(-filled // 16) * 16
    weights = jnp.concatenate(weights + [jnp.zeros((height - filled, HEAD), F32)], 0)
    w_high, w_low = two_parts(weights)
    both = jnp.concatenate([w_high, w_low], 0)
    scale = 1.0 / math.sqrt(total_windows)
    width = lags // slices
    top = rank * pairs

    def combined(at):
        part = dot(both, high_part[:, at : at + step])
        return part[0:height] + part[height:] + dot(w_high, low_part[:, at : at + step])

    result = [jnp.concatenate([combined(side + at) for at in range(0, half, step)], 1) for side in (0, half)]
    left, right = unfold(*[one[top:] for one in result])
    win_out[:, 0:half] = left[0:pairs]
    win_out[:, half:] = right[0:pairs]
    result = [jnp.concatenate([one[0:top], one[top:] * scale], 0) for one in result]
    if first_window:
        merged_out[:, 0:half] = result[0]
        merged_out[:, half:] = result[1]
    else:
        left, right = unfold(result[0] + partial[:, 0:half], result[1] + partial[:, half:])
        for piece in range(slices // 2):
            pieces[piece] = left[:, piece * width : (piece + 1) * width]
            pieces[slices // 2 + piece] = right[:, piece * width : (piece + 1) * width]
    if not first_window:
        for piece in range(slices // 2):
            send_out[piece] = pieces[2 * piece + 1 - core[0]].astype(BF16)
            keep_out[piece] = pieces[2 * piece + core[0]]


def add_kernel(top, chip, keep, got, mine_out, *sends):
    chips, height, _ = keep.shape
    for part in range(chips):
        both = keep[part] + got[part].astype(F32)
        mine_out[part] = both
        short = both[0:top].astype(BF16)
        for out in sends:
            out[part * top : (part + 1) * top] = short
    for step, out in enumerate(sends):
        other = jnp.bitwise_xor(chip[0], step + 1)
        out[chips * top :] = mine_out[other, top:height].astype(BF16)


def gram_kernel(pairs, rank, chip, mine, *refs):
    got, (total_out, gram_out, parts) = refs[:-3], refs[-3:]
    chips, height, width = mine.shape
    top = rank * pairs
    sums = [[jnp.zeros((pairs, width), F32) for _ in range(r + 1)] for r in range(rank)]
    for part in range(chips):
        block = mine[part, 0:top].astype(BF16).astype(F32)
        for one in got:
            block = block + one[part * top : (part + 1) * top].astype(F32)
        parts[part] = block
        rows = [block[r * pairs : (r + 1) * pairs] for r in range(rank)]
        sums = [[sums[r][s] + rows[r] * rows[s] for s in range(r + 1)] for r in range(rank)]
    stack = mine[chip[0], top:height]
    for one in got:
        stack = stack + one[chips * top :].astype(F32)
    total_out[0:top] = parts[chip[0]]
    total_out[top:] = stack
    lane = lax.broadcasted_iota(jnp.int32, (pairs, 128), 1)
    gram = jnp.zeros((pairs, 128), F32)
    for r in range(rank):
        for s in range(r + 1):
            value = jnp.sum(sums[r][s], 1, keepdims=True)
            gram = jnp.where(lane == r * rank + s, value, gram)
    gram_out[...] = gram


def finish_kernel(pairs, rank, lags, total, mine, got, stack_out, basis_out):
    gram = mine[...] + got[...]
    shape = (pairs, total.shape[1])
    entries = [
        [jnp.broadcast_to(gram[:, r * rank + s : r * rank + s + 1], shape) for s in range(r + 1)]
        for r in range(rank)
    ]
    lower, inverse = lower_factor(entries, rank)
    rows = [total[r * pairs : (r + 1) * pairs] for r in range(rank)]
    for r, row in enumerate(solve_rows(rows, lower, inverse)):
        basis_out[:, r, :] = row * math.sqrt(lags)
    stack_out[...] = total[rank * pairs : (rank + 1) * pairs]


def call(kernel, out_shape, in_specs, out_specs, scratch=(), flops=0, moved=0):
    return pl.pallas_call(
        kernel,
        out_shape=out_shape,
        in_specs=in_specs,
        out_specs=out_specs,
        scratch_shapes=list(scratch),
        compiler_params=pltpu.CompilerParams(vmem_limit_bytes=12 * 1024 * 1024),
        cost_estimate=pl.CostEstimate(flops=flops, bytes_accessed=moved, transcendentals=0),
    )


def far(value):
    return pltpu.with_memory_space_constraint(value, pltpu.HBM)


def struct(shape, dtype=F32):
    return jax.ShapeDtypeStruct(shape, dtype)


def on_device(spectra, masks, pair_rows, start_basis):
    stations, windows, seg, parts, freq = spectra.shape
    rank, lags = start_basis.shape
    pairs = pair_rows.shape[0]
    groups = lax.axis_size("pairs")
    group_index = lax.axis_index("pairs")
    slices = lax.axis_size("hours")
    hour = lax.axis_index("hours")
    width = lags // slices
    chips = slices // 2
    forward = [(i, (i + 1) % groups) for i in range(groups)]
    backward = [(target, source) for source, target in forward]
    rows = pair_rows.T
    before = lax.ppermute(rows, "pairs", forward)
    after = lax.ppermute(rows, "pairs", backward)
    place = group_index.reshape(1).astype(jnp.int32)
    whitened = call(
        whiten_kernel,
        [struct((stations, parts * seg, freq), BF16)] * windows,
        [HBM] * 2,
        [VMEM] * windows,
        [
            pltpu.VMEM(spectra.shape, BF16),
            pltpu.VMEM(masks.shape, jnp.int32),
            pltpu.SemaphoreType.DMA((2,)),
        ],
    )(far(spectra), far(masks))
    block = struct((NEAR, parts * seg, freq), BF16)
    def select(wanted, early):
        return call(
            functools.partial(select_kernel, stations),
            [block] * windows,
            [SMEM] + [VMEM] * (2 + windows),
            [VMEM] * windows,
        )(place, early, wanted, *whitened)

    to_next = select(after, whitened[0])
    to_last = select(before, to_next[0])
    lows = [lax.ppermute(one, "pairs", forward) for one in to_next]
    highs = [lax.ppermute(one, "pairs", backward) for one in to_last]
    table, ends = kernel_table(freq, lags)
    fixed = [
        start_basis,
        jnp.asarray(table),
        jnp.asarray(ends),
        jnp.asarray(pick_matrix(pairs, seg, rank)),
        jnp.asarray(spread_matrix(pairs, seg, rank)),
    ]
    *staged, index = call(
        functools.partial(stage_kernel, groups, stations),
        [struct(one.shape, one.dtype) for one in fixed] + [struct(rows.shape, jnp.int32)],
        [SMEM, VMEM] + [HBM] * (len(fixed) + 1),
        [VMEM] * (len(fixed) + 1),
        [
            pltpu.VMEM(start_basis.shape, F32),
            pltpu.VMEM(rows.shape, jnp.int32),
            pltpu.SemaphoreType.DMA((len(fixed) + 1,)),
        ],
        moved=parts * freq * lags,
    )(place, to_next[0], far(rows), *[far(one) for one in fixed])
    core = jnp.mod(hour, 2).reshape(1).astype(jnp.int32)
    chip = (hour // 2).reshape(1).astype(jnp.int32)
    height = -(-(rank + 1) * pairs // 16) * 16
    total_windows = windows * slices
    partial, stacks = None, []
    for w in range(windows):
        last = w == windows - 1
        sizes = (pairs, seg, rank, lags, freq, total_windows, slices, w == 0)
        scratch = [
            pltpu.VMEM((stations + 2 * NEAR, parts * seg, freq), BF16),
            pltpu.VMEM((pairs * seg, parts * freq), BF16),
            pltpu.VMEM((HEAD, lags), F32),
            pltpu.VMEM((HEAD, lags), BF16),
            pltpu.VMEM((HEAD, lags), BF16),
        ]
        args = [index, whitened[w], lows[w], highs[w], *staged]
        specs = [VMEM] * len(args)
        outs = [struct((pairs, lags))]
        if w == 0:
            outs.append(struct((height, lags)))
        else:
            args += [core, partial]
            specs += [SMEM, VMEM]
            outs += [struct((chips, height, width), BF16), struct((chips, height, width))]
            scratch.append(pltpu.VMEM((slices, height, width), F32))
        result = call(
            functools.partial(window_kernel, sizes),
            outs,
            specs,
            [VMEM] * len(outs),
            scratch,
            flops=pairs * seg * parts * freq * lags,
            moved=parts * freq * lags,
        )(*args)
        stacks.append(result[0])
        if w == 0:
            partial = result[1]
        else:
            send, keep = result[1:]
    window_stacks = jnp.stack(stacks, 1)
    swap = lambda value, step: lax.ppermute(value, "hours", [(k, k ^ step) for k in range(slices)])
    got = swap(send, 1)
    top = rank * pairs
    message = struct((chips * top + height - top, width), BF16)
    mine, *sends = call(
        functools.partial(add_kernel, top),
        [struct(keep.shape)] + [message] * (chips - 1),
        [SMEM, VMEM, VMEM],
        [VMEM] * chips,
    )(chip, keep, got)
    arrived = [swap(one, 2 * (step + 1)) for step, one in reversed(list(enumerate(sends)))]
    total, gram = call(
        functools.partial(gram_kernel, pairs, rank),
        [struct((height, width)), struct((pairs, 128))],
        [SMEM] + [VMEM] * chips,
        [VMEM] * 2,
        [pltpu.VMEM((chips, top, width), F32)],
    )(chip, mine, *arrived)
    stack, basis = call(
        functools.partial(finish_kernel, pairs, rank, lags),
        [struct((pairs, width)), struct((pairs, rank, width))],
        [VMEM] * 3,
        [VMEM] * 2,
    )(total, gram, swap(gram, 1))
    return (window_stacks, stack, basis)


def solution(mesh):
    in_specs = (
        P("pairs", "hours", None, None, None),
        P("pairs", "hours", None),
        P("pairs", None),
        P(),
    )
    out_specs = (P("pairs", "hours", None), P("pairs", "hours"), P("pairs", None, "hours"))
    return jax.shard_map(
        on_device, mesh=mesh, in_specs=in_specs, out_specs=out_specs, check_vma=False
    )
```

```python
import functools
import math

import jax
import jax.numpy as jnp
import numpy as np
from jax import lax
from jax.experimental import pallas as pl
from jax.experimental.pallas import tpu as pltpu
from jax.sharding import PartitionSpec as P

BAND = 64
TURNS = 2
NEAR = 4
F32 = jnp.float32
BF16 = jnp.bfloat16
VMEM = pl.BlockSpec(memory_space=pltpu.VMEM)
SMEM = pl.BlockSpec(memory_space=pltpu.SMEM)
HBM = pl.BlockSpec(memory_space=pltpu.HBM)
HEAD = 128
LANE = 16


def kernel_table(freq, lags):
    nfft = 2 * lags
    bins = np.arange(1, freq + 1, dtype=np.int64)[:, None]
    shifts = np.append(np.arange(lags // 2, dtype=np.int64), -(lags // 2))[None, :]
    phase = np.mod(bins * shifts, nfft).astype(np.float64) * (2.0 * math.pi / nfft)
    scale = freq ** (-0.5)
    both = np.concatenate([np.cos(phase) * scale, -np.sin(phase) * scale], 0)
    both = both.astype(np.float32).astype(jnp.bfloat16)
    ends = both[:, -1].astype(np.float32).reshape(2, freq)
    return both[:, :-1], ends


def pick_matrix(pairs, seg, rank):
    pick = np.zeros((HEAD, 2 * HEAD), np.float32)
    side = (seg + rank) * LANE
    for pair in range(pairs):
        for part in range(seg):
            pick[pair * seg + part, part * LANE + pair] = 1
            pick[pair * seg + part, side + pair] = 1
    for row in range(rank):
        pick[pairs * seg + row, (seg + row) * LANE : (seg + row + 1) * LANE] = 1
    return pick.astype(jnp.bfloat16)


def spread_matrix(pairs, seg, rank):
    spread = np.zeros((HEAD, (rank + 1) * HEAD), np.float32)
    for row in range(rank + 1):
        for part in range(seg):
            for pair in range(pairs):
                spread[row * LANE + part, row * HEAD + pair * seg + part] = 1
        for other in range(rank):
            spread[row * LANE + seg + other, row * HEAD + pairs * seg + other] = 1
    return spread.astype(jnp.bfloat16)


def two_parts(values):
    high = values.astype(BF16)
    return high, (values - high.astype(F32)).astype(BF16)


def three_parts(values):
    high = values.astype(BF16)
    rest = values - high.astype(F32)
    mid = rest.astype(BF16)
    return high, mid, (rest - mid.astype(F32)).astype(BF16)


def dot(left, right):
    return jnp.dot(left, right, preferred_element_type=F32)


def dot_rows(left, right):
    return lax.dot_general(left, right, (((1,), (1,)), ((), ())), preferred_element_type=F32)


def lower_factor(gram, rank):
    lower = [[None] * rank for _ in range(rank)]
    inverse = [None] * rank
    for row in range(rank):
        for col in range(row + 1):
            total = gram[row][col]
            for inner in range(col):
                total = total - lower[row][inner] * lower[col][inner]
            if row == col:
                inverse[row] = lax.rsqrt(total)
                lower[row][row] = total * inverse[row]
            else:
                lower[row][col] = total * inverse[col]
    return lower, inverse


def solve_rows(rows, lower, inverse):
    result = []
    for row, current in enumerate(rows):
        for inner in range(row):
            current = current - lower[row][inner] * result[inner]
        result.append(current * inverse[row])
    return result


def used_stations(second, low, stations):
    number = lax.broadcasted_iota(jnp.int32, (stations, second.shape[1]), 0)
    return jnp.max(jnp.where(second == low + number, 1.0, 0.0), 1, keepdims=True)


def flip(values):
    rows, width = values.shape
    back = 127 - lax.broadcasted_iota(jnp.int32, (rows, 128), 1)
    turned = []
    for at in range(width - 128, -1, -128):
        turned.append(jnp.take_along_axis(values[:, at : at + 128], back, axis=1))
    return jnp.concatenate(turned, 1)


def first_lane(values, first, other):
    lane = lax.broadcasted_iota(jnp.int32, values, 1)
    return jnp.where(lane == 0, first, other)


def unfold(even, odd):
    shape = even.shape
    root = math.sqrt(2.0)
    right = first_lane(shape, even * root, even + odd)
    left = first_lane(shape, odd * root, even - odd)
    return flip(pltpu.roll(left, shape[1] - 1, 1)), right


def stage_kernel(groups, stations, place, early, far_rows, *refs):
    *refs, index, natural, rows, sems = refs
    count = len(refs) // 2
    sources, targets = refs[:count], refs[count:]
    copies = [
        pltpu.make_async_copy(source, target, sems.at[number])
        for number, (source, target) in enumerate(zip(sources, (natural, *targets[1:])))
    ]
    for copy in copies:
        copy.start()
    known = pltpu.make_async_copy(far_rows, rows, sems.at[count])
    known.start()
    known.wait()
    before = lax.rem(place[0] + groups - 1, groups) * stations
    after = lax.rem(place[0] + 1, groups) * stations
    own = place[0] * stations
    second = rows[1:2]
    in_before = jnp.logical_and(second >= before, second < before + stations)
    in_own = jnp.logical_and(second >= own, second < own + stations)
    local = second - jnp.where(in_before, before, jnp.where(in_own, own, after))
    below = lax.broadcasted_iota(jnp.int32, (stations, second.shape[1]), 0) < local
    slots = [
        jnp.sum(jnp.where(below, used_stations(second, low, stations), 0.0), 0, keepdims=True)
        for low in (before, after)
    ]
    spot = jnp.where(in_own, NEAR + local, NEAR + stations + slots[1].astype(jnp.int32))
    index[0:1] = rows[0:1] - own
    index[1:2] = jnp.where(in_before, slots[0].astype(jnp.int32), spot)
    copies[0].wait()
    values = natural[...]
    half = values.shape[1] // 2
    right = values[:, half:]
    left = pltpu.roll(flip(values[:, :half]), 1, 1)
    shape = right.shape
    root = math.sqrt(0.5)
    targets[0][:, :half] = first_lane(shape, right * root, (right + left) * 0.5)
    targets[0][:, half:] = first_lane(shape, left * root, (right - left) * 0.5)
    for copy in copies[1:]:
        copy.wait()


def whiten_kernel(far_spectra, far_masks, *refs):
    whitened, (spectra, masks, sems) = refs[:-3], refs[-3:]
    stations, windows, seg, _, freq = spectra.shape
    small = [pltpu.make_async_copy(far_masks, masks, sems.at[0])]
    large = [pltpu.make_async_copy(far_spectra, spectra, sems.at[1])]
    for copy in small + large:
        copy.start()
    tile = (128, 128)
    same = lax.broadcasted_iota(jnp.int32, tile, 0) // BAND == lax.broadcasted_iota(jnp.int32, tile, 1) // BAND
    bands = jnp.where(same, 1.0, 0.0).astype(BF16)
    for copy in small:
        copy.wait()
    eye = lax.broadcasted_iota(jnp.int32, (seg, seg), 0) == lax.broadcasted_iota(jnp.int32, (seg, seg), 1)
    open_rows = []
    for station in range(stations):
        for window in range(windows):
            mask = masks[station, window : window + 1].astype(F32)
            mask = jnp.where(eye, jnp.broadcast_to(mask, (seg, seg)), 0.0)
            open_rows.append(jnp.sum(mask, 1, keepdims=True))
    large[0].wait()
    values, squares = [], []
    for station in range(stations):
        for window in range(windows):
            block = spectra[station, window].astype(F32)
            real, imag = block[:, 0], block[:, 1]
            values.append((real, imag))
            squares.append(real * real + imag * imag)
    height = len(values) * seg
    squares = jnp.concatenate(squares, 0)
    here = jnp.concatenate(open_rows, 0)
    scales = []
    for at in range(0, freq, 128):
        power = dot(jnp.concatenate(two_parts(squares[:, at : at + 128]), 1), jnp.concatenate([bands, bands], 0))
        scales.append(lax.rsqrt(power * (1.0 / (2 * BAND)) + 1e-06) * here)
    scale = jnp.concatenate(scales, 1)
    for number, (real, imag) in enumerate(values):
        here = scale[number * seg : (number + 1) * seg]
        block = jnp.concatenate([real * here, imag * here], 0).astype(BF16)
        whitened[number % windows][number // windows] = block


def select_kernel(stations, place, early, rows, *refs):
    windows = len(refs) // 2
    used = used_stations(rows[1:2], place[0] * stations, stations)
    weight = jnp.left_shift(1, lax.broadcasted_iota(jnp.int32, (stations, 1), 0)).astype(F32)
    needed = jnp.sum(used * weight).astype(jnp.int32)
    slot = jnp.int32(0)
    for station in range(stations):
        wanted = jnp.bitwise_and(jnp.right_shift(needed, station), 1)
        spot = jnp.minimum(slot, NEAR - 1)

        @pl.when(wanted == 1)
        def _():
            for source, target in zip(refs[:windows], refs[windows:]):
                target[spot] = source[station]

        slot = slot + wanted


def window_kernel(sizes, index, own, low, high, start, table, ends, pick, spread, *refs):
    pairs, seg, rank, lags, freq, total_windows, slices, first_window = sizes
    rows = pairs * seg
    if first_window:
        win_out, merged_out, near, cross, vectors, high_part, low_part = refs
    else:
        (core, partial, win_out, send_out, keep_out, near, cross, vectors, high_part, low_part) = refs
    stations = own.shape[0]
    half = lags // 2
    picked = index[...]
    near[0:NEAR] = low[...]
    near[NEAR : NEAR + stations] = own[...]
    near[NEAR + stations :] = high[...]
    edges = []
    for pair in range(0, pairs, 2):
        real, imag = [], []
        for one in (pair, pair + 1):
            a = own[picked[0, one]].astype(F32)
            b = near[picked[1, one]].astype(F32)
            a_re, a_im, b_re, b_im = a[:seg], a[seg:], b[:seg], b[seg:]
            real.append(a_re * b_re + a_im * b_im)
            imag.append(a_im * b_re - a_re * b_im)
        block = pl.ds(pair * seg, 2 * seg)
        real = jnp.concatenate(real, 0).astype(BF16)
        imag = jnp.concatenate(imag, 0).astype(BF16)
        cross[block, 0:freq] = real
        cross[block, freq:] = imag
        last = real.astype(F32) * ends[0:1] + imag.astype(F32) * ends[1:2]
        edges.append(jnp.sum(last, 1, keepdims=True))
    vectors[rows : rows + rank] = start[...]
    vectors[rows + rank :] = jnp.zeros((HEAD - rows - rank, lags), F32)
    step = 512
    for at in range(0, half, step):
        for part in (0, 1):
            block = cross[:, part * freq : (part + 1) * freq]
            block = jnp.concatenate([block, block[0 : HEAD - rows]], 0)
            block = dot(block, table[part * freq : (part + 1) * freq, at : at + step])
            vectors[0:rows, part * half + at : part * half + at + step] = block[0:rows]
    shape = (rows, 128)
    root = math.sqrt(0.5)
    column = vectors[0:rows, 0:128]
    vectors[0:rows, 0:128] = first_lane(shape, column * root, column)
    edge = jnp.broadcast_to(jnp.concatenate(edges, 0) * root, shape)
    vectors[0:rows, half : half + 128] = first_lane(shape, edge, vectors[0:rows, half : half + 128])
    every = vectors[...]
    high_part[...] = every.astype(BF16)
    low_part[...] = (every - high_part[...].astype(F32)).astype(BF16)
    gram = dot_rows(high_part[...], high_part[...])
    side = dot_rows(low_part[...], high_part[...])
    gram = 2.0 * (gram + side + side.T)
    lane = lax.broadcasted_iota(jnp.int32, (seg, HEAD), 1)
    sub = lax.broadcasted_iota(jnp.int32, (seg, HEAD), 0)
    blocks = jnp.zeros((seg, HEAD), F32)
    for pair in range(pairs):
        blocks = blocks + jnp.where(lane // seg == pair, gram[pair * seg : (pair + 1) * seg], 0.0)
    basis_rows = gram[rows : rows + 8]
    turned = [
        jnp.where(lane % seg == sub, jnp.broadcast_to(basis_rows[row : row + 1], (seg, HEAD)), 0.0)
        for row in range(rank)
    ]
    stacked = jnp.concatenate([blocks, basis_rows] + turned, 0)
    count = stacked.shape[0]
    moved = dot(jnp.concatenate(three_parts(stacked), 0), pick[...])
    moved = moved[0:count] + moved[count : 2 * count] + moved[2 * count :]
    products = [moved[0:16, k * LANE : (k + 1) * LANE] for k in range(seg)]
    side_at = (seg + rank) * LANE
    for row in range(rank):
        upper = moved[16 + row * seg : 16 + (row + 1) * seg, side_at : side_at + LANE]
        under = moved[8:16, (seg + row) * LANE : (seg + row + 1) * LANE]
        products.append(jnp.concatenate([upper, under], 0))
    level = lax.broadcasted_iota(jnp.int32, (16, LANE), 0)
    of_corr = level < seg
    known = [jnp.where(level == seg + row, 1.0, 0.0) for row in range(rank)]
    reach = [jnp.where(of_corr, products[seg + row], 0.0) for row in range(rank)]
    for turn in range(TURNS):
        known = [known[r] + reach[r] * (1.0 / lags) for r in range(rank)]
        images = []
        for r in range(rank):
            image = known[r][0:1] * products[0]
            for k in range(1, seg + rank):
                image = image + known[r][k : k + 1] * products[k]
            images.append(image)
        inner = [
            [jnp.sum(images[r] * known[s], 0, keepdims=True) for s in range(r + 1)] for r in range(rank)
        ]
        lower, inverse = lower_factor(inner, rank)
        known = solve_rows(known, lower, inverse)
        reach = [jnp.where(of_corr, v, 0.0) for v in solve_rows(images, lower, inverse)]
    outs = [reach[r] + float(lags) * known[r] for r in range(rank)]
    window = jnp.zeros_like(known[0])
    for r in range(rank):
        window = window + jnp.sum(reach[r], 0, keepdims=True) * known[r]
    outs.append(window * (1.0 / math.sqrt(seg)))
    coefs = jnp.concatenate(outs + [jnp.zeros((HEAD - (rank + 1) * 16, LANE), F32)], 0)
    coefs = jnp.concatenate([coefs, jnp.zeros((HEAD, HEAD - LANE), F32)], 1).T[0:LANE]
    wide = dot(jnp.concatenate(two_parts(coefs), 0), spread[...])
    wide = wide[0:LANE] + wide[LANE:]
    row_of = lax.broadcasted_iota(jnp.int32, (LANE, HEAD), 0)
    lane_of = lax.broadcasted_iota(jnp.int32, (LANE, HEAD), 1)
    mine = jnp.logical_or(lane_of // seg == row_of, lane_of >= rows)
    weights = [
        jnp.where(mine, wide[:, r * HEAD : (r + 1) * HEAD], 0.0)[0:pairs] for r in range(rank + 1)
    ]
    filled = (rank + 1) * pairs
    height = -(-filled // 16) * 16
    weights = jnp.concatenate(weights + [jnp.zeros((height - filled, HEAD), F32)], 0)
    w_high, w_low = two_parts(weights)
    both = jnp.concatenate([w_high, w_low], 0)
    scale = 1.0 / math.sqrt(total_windows)
    width = lags // slices
    top = rank * pairs

    def combined(at):
        part = dot(both, high_part[:, at : at + step])
        return part[0:height] + part[height:] + dot(w_high, low_part[:, at : at + step])

    result = [jnp.concatenate([combined(side + at) for at in range(0, half, step)], 1) for side in (0, half)]
    left, right = unfold(*[one[top:] for one in result])
    win_out[:, 0:half] = left[0:pairs]
    win_out[:, half:] = right[0:pairs]
    result = [jnp.concatenate([one[0:top], one[top:] * scale], 0) for one in result]
    if first_window:
        merged_out[:, 0:half] = result[0]
        merged_out[:, half:] = result[1]
    else:
        left, right = unfold(result[0] + partial[:, 0:half], result[1] + partial[:, half:])
        swapped = core[0] == 1
        for piece in range(slices // 2):
            side, at = (left, right)[piece // (slices // 4)], 2 * piece * width % half
            one, two = side[:, at : at + width], side[:, at + width : at + 2 * width]
            send_out[piece] = jnp.where(swapped, one, two).astype(BF16)
            keep_out[piece] = jnp.where(swapped, two, one)


def add_kernel(top, chip, keep, got, mine_out, *sends):
    chips, height, _ = keep.shape
    for part in range(chips):
        both = keep[part] + got[part].astype(F32)
        mine_out[part] = both
        short = both[0:top].astype(BF16)
        for out in sends:
            out[part * top : (part + 1) * top] = short
    for step, out in enumerate(sends):
        other = jnp.bitwise_xor(chip[0], step + 1)
        out[chips * top :] = mine_out[other, top:height].astype(BF16)


def gram_kernel(pairs, rank, chip, mine, *refs):
    got, (total_out, gram_out, parts) = refs[:-3], refs[-3:]
    chips, height, width = mine.shape
    top = rank * pairs
    sums = [[jnp.zeros((pairs, width), F32) for _ in range(r + 1)] for r in range(rank)]
    for part in range(chips):
        block = mine[part, 0:top].astype(BF16).astype(F32)
        for one in got:
            block = block + one[part * top : (part + 1) * top].astype(F32)
        parts[part] = block
        rows = [block[r * pairs : (r + 1) * pairs] for r in range(rank)]
        sums = [[sums[r][s] + rows[r] * rows[s] for s in range(r + 1)] for r in range(rank)]
    stack = mine[chip[0], top:height]
    for one in got:
        stack = stack + one[chips * top :].astype(F32)
    total_out[0:top] = parts[chip[0]]
    total_out[top:] = stack
    lane = lax.broadcasted_iota(jnp.int32, (pairs, 128), 1)
    gram = jnp.zeros((pairs, 128), F32)
    for r in range(rank):
        for s in range(r + 1):
            value = jnp.sum(sums[r][s], 1, keepdims=True)
            gram = jnp.where(lane == r * rank + s, value, gram)
    gram_out[...] = gram


def finish_kernel(pairs, rank, lags, total, mine, got, stack_out, basis_out):
    gram = mine[...] + got[...]
    shape = (pairs, total.shape[1])
    entries = [
        [jnp.broadcast_to(gram[:, r * rank + s : r * rank + s + 1], shape) for s in range(r + 1)]
        for r in range(rank)
    ]
    lower, inverse = lower_factor(entries, rank)
    rows = [total[r * pairs : (r + 1) * pairs] for r in range(rank)]
    for r, row in enumerate(solve_rows(rows, lower, inverse)):
        basis_out[:, r, :] = row * math.sqrt(lags)
    stack_out[...] = total[rank * pairs : (rank + 1) * pairs]


def call(kernel, out_shape, in_specs, out_specs, scratch=(), flops=0, moved=0):
    return pl.pallas_call(
        kernel,
        out_shape=out_shape,
        in_specs=in_specs,
        out_specs=out_specs,
        scratch_shapes=list(scratch),
        compiler_params=pltpu.CompilerParams(vmem_limit_bytes=12 * 1024 * 1024),
        cost_estimate=pl.CostEstimate(flops=flops, bytes_accessed=moved, transcendentals=0),
    )


def far(value):
    return pltpu.with_memory_space_constraint(value, pltpu.HBM)


def struct(shape, dtype=F32):
    return jax.ShapeDtypeStruct(shape, dtype)


def on_device(spectra, masks, pair_rows, start_basis):
    stations, windows, seg, parts, freq = spectra.shape
    rank, lags = start_basis.shape
    pairs = pair_rows.shape[0]
    groups = lax.axis_size("pairs")
    group_index = lax.axis_index("pairs")
    slices = lax.axis_size("hours")
    hour = lax.axis_index("hours")
    width = lags // slices
    chips = slices // 2
    forward = [(i, (i + 1) % groups) for i in range(groups)]
    backward = [(target, source) for source, target in forward]
    rows = pair_rows.T
    before = lax.ppermute(rows, "pairs", forward)
    after = lax.ppermute(rows, "pairs", backward)
    place = group_index.reshape(1).astype(jnp.int32)
    whitened = call(
        whiten_kernel,
        [struct((stations, parts * seg, freq), BF16)] * windows,
        [HBM] * 2,
        [VMEM] * windows,
        [
            pltpu.VMEM(spectra.shape, BF16),
            pltpu.VMEM(masks.shape, jnp.int32),
            pltpu.SemaphoreType.DMA((2,)),
        ],
    )(far(spectra), far(masks))
    block = struct((NEAR, parts * seg, freq), BF16)
    def select(wanted, early):
        return call(
            functools.partial(select_kernel, stations),
            [block] * windows,
            [SMEM] + [VMEM] * (2 + windows),
            [VMEM] * windows,
        )(place, early, wanted, *whitened)

    to_next = select(after, whitened[0])
    to_last = select(before, to_next[0])
    lows = [lax.ppermute(one, "pairs", forward) for one in to_next]
    highs = [lax.ppermute(one, "pairs", backward) for one in to_last]
    table, ends = kernel_table(freq, lags)
    fixed = [
        start_basis,
        jnp.asarray(table),
        jnp.asarray(ends),
        jnp.asarray(pick_matrix(pairs, seg, rank)),
        jnp.asarray(spread_matrix(pairs, seg, rank)),
    ]
    *staged, index = call(
        functools.partial(stage_kernel, groups, stations),
        [struct(one.shape, one.dtype) for one in fixed] + [struct(rows.shape, jnp.int32)],
        [SMEM, VMEM] + [HBM] * (len(fixed) + 1),
        [VMEM] * (len(fixed) + 1),
        [
            pltpu.VMEM(start_basis.shape, F32),
            pltpu.VMEM(rows.shape, jnp.int32),
            pltpu.SemaphoreType.DMA((len(fixed) + 1,)),
        ],
        moved=parts * freq * lags,
    )(place, to_next[0], far(rows), *[far(one) for one in fixed])
    core = jnp.mod(hour, 2).reshape(1).astype(jnp.int32)
    chip = (hour // 2).reshape(1).astype(jnp.int32)
    height = -(-(rank + 1) * pairs // 16) * 16
    total_windows = windows * slices
    partial, stacks = None, []
    for w in range(windows):
        last = w == windows - 1
        sizes = (pairs, seg, rank, lags, freq, total_windows, slices, w == 0)
        scratch = [
            pltpu.VMEM((stations + 2 * NEAR, parts * seg, freq), BF16),
            pltpu.VMEM((pairs * seg, parts * freq), BF16),
            pltpu.VMEM((HEAD, lags), F32),
            pltpu.VMEM((HEAD, lags), BF16),
            pltpu.VMEM((HEAD, lags), BF16),
        ]
        args = [index, whitened[w], lows[w], highs[w], *staged]
        specs = [VMEM] * len(args)
        outs = [struct((pairs, lags))]
        if w == 0:
            outs.append(struct((height, lags)))
        else:
            args += [core, partial]
            specs += [SMEM, VMEM]
            outs += [struct((chips, height, width), BF16), struct((chips, height, width))]
        result = call(
            functools.partial(window_kernel, sizes),
            outs,
            specs,
            [VMEM] * len(outs),
            scratch,
            flops=pairs * seg * parts * freq * lags,
            moved=parts * freq * lags,
        )(*args)
        stacks.append(result[0])
        if w == 0:
            partial = result[1]
        else:
            send, keep = result[1:]
    window_stacks = jnp.stack(stacks, 1)
    swap = lambda value, step: lax.ppermute(value, "hours", [(k, k ^ step) for k in range(slices)])
    got = swap(send, 1)
    top = rank * pairs
    message = struct((chips * top + height - top, width), BF16)
    mine, *sends = call(
        functools.partial(add_kernel, top),
        [struct(keep.shape)] + [message] * (chips - 1),
        [SMEM, VMEM, VMEM],
        [VMEM] * chips,
    )(chip, keep, got)
    arrived = [swap(one, 2 * (step + 1)) for step, one in reversed(list(enumerate(sends)))]
    total, gram = call(
        functools.partial(gram_kernel, pairs, rank),
        [struct((height, width)), struct((pairs, 128))],
        [SMEM] + [VMEM] * chips,
        [VMEM] * 2,
        [pltpu.VMEM((chips, top, width), F32)],
    )(chip, mine, *arrived)
    stack, basis = call(
        functools.partial(finish_kernel, pairs, rank, lags),
        [struct((pairs, width)), struct((pairs, rank, width))],
        [VMEM] * 3,
        [VMEM] * 2,
    )(total, gram, swap(gram, 1))
    return (window_stacks, stack, basis)


def solution(mesh):
    in_specs = (
        P("pairs", "hours", None, None, None),
        P("pairs", "hours", None),
        P("pairs", None),
        P(),
    )
    out_specs = (P("pairs", "hours", None), P("pairs", "hours"), P("pairs", None, "hours"))
    return jax.shard_map(
        on_device, mesh=mesh, in_specs=in_specs, out_specs=out_specs, check_vma=False
    )
```

```python
import functools
import math

import jax
import jax.numpy as jnp
import numpy as np
from jax import lax
from jax.experimental import pallas as pl
from jax.experimental.pallas import tpu as pltpu
from jax.sharding import PartitionSpec as P

BAND = 64
TURNS = 2
NEAR = 4
F32 = jnp.float32
BF16 = jnp.bfloat16
VMEM = pl.BlockSpec(memory_space=pltpu.VMEM)
SMEM = pl.BlockSpec(memory_space=pltpu.SMEM)
HBM = pl.BlockSpec(memory_space=pltpu.HBM)
HEAD = 128
LANE = 16


def kernel_table(freq, lags):
    nfft = 2 * lags
    bins = np.arange(1, freq + 1, dtype=np.int64)[:, None]
    shifts = np.append(np.arange(lags // 2, dtype=np.int64), -(lags // 2))[None, :]
    phase = np.mod(bins * shifts, nfft).astype(np.float64) * (2.0 * math.pi / nfft)
    scale = freq ** (-0.5)
    both = np.concatenate([np.cos(phase) * scale, -np.sin(phase) * scale], 0)
    both = both.astype(np.float32).astype(jnp.bfloat16)
    ends = both[:, -1].astype(np.float32).reshape(2, freq)
    return both[:, :-1], ends


def pick_matrix(pairs, seg, rank):
    pick = np.zeros((HEAD, 2 * HEAD), np.float32)
    side = (seg + rank) * LANE
    for pair in range(pairs):
        for part in range(seg):
            pick[pair * seg + part, part * LANE + pair] = 1
            pick[pair * seg + part, side + pair] = 1
    for row in range(rank):
        pick[pairs * seg + row, (seg + row) * LANE : (seg + row + 1) * LANE] = 1
    return pick.astype(jnp.bfloat16)


def spread_matrix(pairs, seg, rank):
    spread = np.zeros((HEAD, (rank + 1) * HEAD), np.float32)
    for row in range(rank + 1):
        for part in range(seg):
            for pair in range(pairs):
                spread[row * LANE + part, row * HEAD + pair * seg + part] = 1
        for other in range(rank):
            spread[row * LANE + seg + other, row * HEAD + pairs * seg + other] = 1
    return spread.astype(jnp.bfloat16)


def two_parts(values):
    high = values.astype(BF16)
    return high, (values - high.astype(F32)).astype(BF16)


def three_parts(values):
    high = values.astype(BF16)
    rest = values - high.astype(F32)
    mid = rest.astype(BF16)
    return high, mid, (rest - mid.astype(F32)).astype(BF16)


def dot(left, right):
    return jnp.dot(left, right, preferred_element_type=F32)


def dot_rows(left, right):
    return lax.dot_general(left, right, (((1,), (1,)), ((), ())), preferred_element_type=F32)


def lower_factor(gram, rank):
    lower = [[None] * rank for _ in range(rank)]
    inverse = [None] * rank
    for row in range(rank):
        for col in range(row + 1):
            total = gram[row][col]
            for inner in range(col):
                total = total - lower[row][inner] * lower[col][inner]
            if row == col:
                inverse[row] = lax.rsqrt(total)
                lower[row][row] = total * inverse[row]
            else:
                lower[row][col] = total * inverse[col]
    return lower, inverse


def solve_rows(rows, lower, inverse):
    result = []
    for row, current in enumerate(rows):
        for inner in range(row):
            current = current - lower[row][inner] * result[inner]
        result.append(current * inverse[row])
    return result


def used_stations(second, low, stations):
    number = lax.broadcasted_iota(jnp.int32, (stations, second.shape[1]), 0)
    return jnp.max(jnp.where(second == low + number, 1.0, 0.0), 1, keepdims=True)


def flip(values):
    rows, width = values.shape
    back = 127 - lax.broadcasted_iota(jnp.int32, (rows, 128), 1)
    turned = []
    for at in range(width - 128, -1, -128):
        turned.append(jnp.take_along_axis(values[:, at : at + 128], back, axis=1))
    return jnp.concatenate(turned, 1)


def first_lane(values, first, other):
    lane = lax.broadcasted_iota(jnp.int32, values, 1)
    return jnp.where(lane == 0, first, other)


def unfold(even, odd):
    shape = even.shape
    root = math.sqrt(2.0)
    right = first_lane(shape, even * root, even + odd)
    left = first_lane(shape, odd * root, even - odd)
    return flip(pltpu.roll(left, shape[1] - 1, 1)), right


def stage_kernel(groups, stations, place, early, far_rows, *refs):
    *refs, index, natural, rows, sems = refs
    count = len(refs) // 2
    sources, targets = refs[:count], refs[count:]
    copies = [
        pltpu.make_async_copy(source, target, sems.at[number])
        for number, (source, target) in enumerate(zip(sources, (natural, *targets[1:])))
    ]
    for copy in copies:
        copy.start()
    known = pltpu.make_async_copy(far_rows, rows, sems.at[count])
    known.start()
    known.wait()
    before = lax.rem(place[0] + groups - 1, groups) * stations
    after = lax.rem(place[0] + 1, groups) * stations
    own = place[0] * stations
    second = rows[1:2]
    in_before = jnp.logical_and(second >= before, second < before + stations)
    in_own = jnp.logical_and(second >= own, second < own + stations)
    local = second - jnp.where(in_before, before, jnp.where(in_own, own, after))
    below = lax.broadcasted_iota(jnp.int32, (stations, second.shape[1]), 0) < local
    slots = [
        jnp.sum(jnp.where(below, used_stations(second, low, stations), 0.0), 0, keepdims=True)
        for low in (before, after)
    ]
    spot = jnp.where(in_own, NEAR + local, NEAR + stations + slots[1].astype(jnp.int32))
    index[0:1] = rows[0:1] - own
    index[1:2] = jnp.where(in_before, slots[0].astype(jnp.int32), spot)
    copies[0].wait()
    values = natural[...]
    half = values.shape[1] // 2
    right = values[:, half:]
    left = pltpu.roll(flip(values[:, :half]), 1, 1)
    shape = right.shape
    root = math.sqrt(0.5)
    targets[0][:, :half] = first_lane(shape, right * root, (right + left) * 0.5)
    targets[0][:, half:] = first_lane(shape, left * root, (right - left) * 0.5)
    for copy in copies[1:]:
        copy.wait()


def whiten_kernel(far_spectra, far_masks, *refs):
    whitened, (spectra, masks, sems) = refs[:-3], refs[-3:]
    stations, windows, seg, _, freq = spectra.shape
    small = [pltpu.make_async_copy(far_masks, masks, sems.at[0])]
    large = [pltpu.make_async_copy(far_spectra, spectra, sems.at[1])]
    for copy in small + large:
        copy.start()
    tile = (128, 128)
    same = lax.broadcasted_iota(jnp.int32, tile, 0) // BAND == lax.broadcasted_iota(jnp.int32, tile, 1) // BAND
    bands = jnp.where(same, 1.0, 0.0).astype(BF16)
    for copy in small:
        copy.wait()
    eye = lax.broadcasted_iota(jnp.int32, (seg, seg), 0) == lax.broadcasted_iota(jnp.int32, (seg, seg), 1)
    open_rows = []
    for station in range(stations):
        for window in range(windows):
            mask = masks[station, window : window + 1].astype(F32)
            mask = jnp.where(eye, jnp.broadcast_to(mask, (seg, seg)), 0.0)
            open_rows.append(jnp.sum(mask, 1, keepdims=True))
    large[0].wait()
    values, squares = [], []
    for station in range(stations):
        for window in range(windows):
            block = spectra[station, window].astype(F32)
            real, imag = block[:, 0], block[:, 1]
            values.append((real, imag))
            squares.append(real * real + imag * imag)
    height = len(values) * seg
    squares = jnp.concatenate(squares, 0)
    here = jnp.concatenate(open_rows, 0)
    scales = []
    for at in range(0, freq, 128):
        power = dot(jnp.concatenate(two_parts(squares[:, at : at + 128]), 1), jnp.concatenate([bands, bands], 0))
        scales.append(lax.rsqrt(power * (1.0 / (2 * BAND)) + 1e-06) * here)
    scale = jnp.concatenate(scales, 1)
    for number, (real, imag) in enumerate(values):
        here = scale[number * seg : (number + 1) * seg]
        block = jnp.concatenate([real * here, imag * here], 0).astype(BF16)
        whitened[number % windows][number // windows] = block


def select_kernel(stations, place, early, rows, *refs):
    windows = len(refs) // 2
    used = used_stations(rows[1:2], place[0] * stations, stations)
    weight = jnp.left_shift(1, lax.broadcasted_iota(jnp.int32, (stations, 1), 0)).astype(F32)
    needed = jnp.sum(used * weight).astype(jnp.int32)
    for slot in range(NEAR):
        lowest = jnp.bitwise_and(needed, -needed)
        station = jnp.int32(0)
        for number in range(1, stations):
            station = station + jnp.where(lowest >= (1 << number), 1, 0)
        for source, target in zip(refs[:windows], refs[windows:]):
            target[slot] = source[station]
        needed = needed - lowest


def window_kernel(sizes, index, own, low, high, start, table, ends, pick, spread, *refs):
    pairs, seg, rank, lags, freq, total_windows, slices, first_window = sizes
    rows = pairs * seg
    if first_window:
        win_out, merged_out, near, cross, vectors, high_part, low_part = refs
    else:
        (core, partial, win_out, send_out, keep_out, near, cross, vectors, high_part, low_part) = refs
    stations = own.shape[0]
    half = lags // 2
    picked = index[...]
    near[0:NEAR] = low[...]
    near[NEAR : NEAR + stations] = own[...]
    near[NEAR + stations :] = high[...]
    edges = []
    for pair in range(0, pairs, 2):
        real, imag = [], []
        for one in (pair, pair + 1):
            a = own[picked[0, one]].astype(F32)
            b = near[picked[1, one]].astype(F32)
            a_re, a_im, b_re, b_im = a[:seg], a[seg:], b[:seg], b[seg:]
            real.append(a_re * b_re + a_im * b_im)
            imag.append(a_im * b_re - a_re * b_im)
        block = pl.ds(pair * seg, 2 * seg)
        real = jnp.concatenate(real, 0).astype(BF16)
        imag = jnp.concatenate(imag, 0).astype(BF16)
        cross[block, 0:freq] = real
        cross[block, freq:] = imag
        last = real.astype(F32) * ends[0:1] + imag.astype(F32) * ends[1:2]
        edges.append(jnp.sum(last, 1, keepdims=True))
    vectors[rows : rows + rank] = start[...]
    vectors[rows + rank :] = jnp.zeros((HEAD - rows - rank, lags), F32)
    step = 512
    for at in range(0, half, step):
        for part in (0, 1):
            block = cross[:, part * freq : (part + 1) * freq]
            block = jnp.concatenate([block, block[0 : HEAD - rows]], 0)
            block = dot(block, table[part * freq : (part + 1) * freq, at : at + step])
            vectors[0:rows, part * half + at : part * half + at + step] = block[0:rows]
    shape = (rows, 128)
    root = math.sqrt(0.5)
    column = vectors[0:rows, 0:128]
    vectors[0:rows, 0:128] = first_lane(shape, column * root, column)
    edge = jnp.broadcast_to(jnp.concatenate(edges, 0) * root, shape)
    vectors[0:rows, half : half + 128] = first_lane(shape, edge, vectors[0:rows, half : half + 128])
    every = vectors[...]
    high_part[...] = every.astype(BF16)
    low_part[...] = (every - high_part[...].astype(F32)).astype(BF16)
    gram = dot_rows(high_part[...], high_part[...])
    side = dot_rows(low_part[...], high_part[...])
    gram = 2.0 * (gram + side + side.T)
    lane = lax.broadcasted_iota(jnp.int32, (seg, HEAD), 1)
    sub = lax.broadcasted_iota(jnp.int32, (seg, HEAD), 0)
    blocks = jnp.zeros((seg, HEAD), F32)
    for pair in range(pairs):
        blocks = blocks + jnp.where(lane // seg == pair, gram[pair * seg : (pair + 1) * seg], 0.0)
    basis_rows = gram[rows : rows + 8]
    turned = [
        jnp.where(lane % seg == sub, jnp.broadcast_to(basis_rows[row : row + 1], (seg, HEAD)), 0.0)
        for row in range(rank)
    ]
    stacked = jnp.concatenate([blocks, basis_rows] + turned, 0)
    count = stacked.shape[0]
    moved = dot(jnp.concatenate(three_parts(stacked), 0), pick[...])
    moved = moved[0:count] + moved[count : 2 * count] + moved[2 * count :]
    products = [moved[0:16, k * LANE : (k + 1) * LANE] for k in range(seg)]
    side_at = (seg + rank) * LANE
    for row in range(rank):
        upper = moved[16 + row * seg : 16 + (row + 1) * seg, side_at : side_at + LANE]
        under = moved[8:16, (seg + row) * LANE : (seg + row + 1) * LANE]
        products.append(jnp.concatenate([upper, under], 0))
    level = lax.broadcasted_iota(jnp.int32, (16, LANE), 0)
    of_corr = level < seg
    known = [jnp.where(level == seg + row, 1.0, 0.0) for row in range(rank)]
    reach = [jnp.where(of_corr, products[seg + row], 0.0) for row in range(rank)]
    for turn in range(TURNS):
        known = [known[r] + reach[r] * (1.0 / lags) for r in range(rank)]
        images = []
        for r in range(rank):
            image = known[r][0:1] * products[0]
            for k in range(1, seg + rank):
                image = image + known[r][k : k + 1] * products[k]
            images.append(image)
        inner = [
            [jnp.sum(images[r] * known[s], 0, keepdims=True) for s in range(r + 1)] for r in range(rank)
        ]
        lower, inverse = lower_factor(inner, rank)
        known = solve_rows(known, lower, inverse)
        reach = [jnp.where(of_corr, v, 0.0) for v in solve_rows(images, lower, inverse)]
    outs = [reach[r] + float(lags) * known[r] for r in range(rank)]
    window = jnp.zeros_like(known[0])
    for r in range(rank):
        window = window + jnp.sum(reach[r], 0, keepdims=True) * known[r]
    outs.append(window * (1.0 / math.sqrt(seg)))
    coefs = jnp.concatenate(outs + [jnp.zeros((HEAD - (rank + 1) * 16, LANE), F32)], 0)
    coefs = jnp.concatenate([coefs, jnp.zeros((HEAD, HEAD - LANE), F32)], 1).T[0:LANE]
    wide = dot(jnp.concatenate(two_parts(coefs), 0), spread[...])
    wide = wide[0:LANE] + wide[LANE:]
    row_of = lax.broadcasted_iota(jnp.int32, (LANE, HEAD), 0)
    lane_of = lax.broadcasted_iota(jnp.int32, (LANE, HEAD), 1)
    mine = jnp.logical_or(lane_of // seg == row_of, lane_of >= rows)
    weights = [
        jnp.where(mine, wide[:, r * HEAD : (r + 1) * HEAD], 0.0)[0:pairs] for r in range(rank + 1)
    ]
    filled = (rank + 1) * pairs
    height = -(-filled // 16) * 16
    weights = jnp.concatenate(weights + [jnp.zeros((height - filled, HEAD), F32)], 0)
    w_high, w_low = two_parts(weights)
    both = jnp.concatenate([w_high, w_low], 0)
    scale = 1.0 / math.sqrt(total_windows)
    width = lags // slices
    top = rank * pairs

    def combined(at):
        part = dot(both, high_part[:, at : at + step])
        return part[0:height] + part[height:] + dot(w_high, low_part[:, at : at + step])

    result = [jnp.concatenate([combined(side + at) for at in range(0, half, step)], 1) for side in (0, half)]
    left, right = unfold(*[one[top:] for one in result])
    win_out[:, 0:half] = left[0:pairs]
    win_out[:, half:] = right[0:pairs]
    result = [jnp.concatenate([one[0:top], one[top:] * scale], 0) for one in result]
    if first_window:
        merged_out[:, 0:half] = result[0]
        merged_out[:, half:] = result[1]
    else:
        left, right = unfold(result[0] + partial[:, 0:half], result[1] + partial[:, half:])
        swapped = core[0] == 1
        for piece in range(slices // 2):
            side, at = (left, right)[piece // (slices // 4)], 2 * piece * width % half
            one, two = side[:, at : at + width], side[:, at + width : at + 2 * width]
            send_out[piece] = jnp.where(swapped, one, two).astype(BF16)
            keep_out[piece] = jnp.where(swapped, two, one)


def add_kernel(top, chip, keep, got, mine_out, *sends):
    chips, height, _ = keep.shape
    for part in range(chips):
        both = keep[part] + got[part].astype(F32)
        mine_out[part] = both
        short = both[0:top].astype(BF16)
        for out in sends:
            out[part * top : (part + 1) * top] = short
    for step, out in enumerate(sends):
        other = jnp.bitwise_xor(chip[0], step + 1)
        out[chips * top :] = mine_out[other, top:height].astype(BF16)


def gram_kernel(pairs, rank, chip, mine, *refs):
    got, (total_out, gram_out, parts) = refs[:-3], refs[-3:]
    chips, height, width = mine.shape
    top = rank * pairs
    sums = [[jnp.zeros((pairs, width), F32) for _ in range(r + 1)] for r in range(rank)]
    for part in range(chips):
        block = mine[part, 0:top].astype(BF16).astype(F32)
        for one in got:
            block = block + one[part * top : (part + 1) * top].astype(F32)
        parts[part] = block
        rows = [block[r * pairs : (r + 1) * pairs] for r in range(rank)]
        sums = [[sums[r][s] + rows[r] * rows[s] for s in range(r + 1)] for r in range(rank)]
    stack = mine[chip[0], top:height]
    for one in got:
        stack = stack + one[chips * top :].astype(F32)
    total_out[0:top] = parts[chip[0]]
    total_out[top:] = stack
    lane = lax.broadcasted_iota(jnp.int32, (pairs, 128), 1)
    gram = jnp.zeros((pairs, 128), F32)
    for r in range(rank):
        for s in range(r + 1):
            value = jnp.sum(sums[r][s], 1, keepdims=True)
            gram = jnp.where(lane == r * rank + s, value, gram)
    gram_out[...] = gram


def finish_kernel(pairs, rank, lags, total, mine, got, stack_out, basis_out):
    gram = mine[...] + got[...]
    shape = (pairs, total.shape[1])
    entries = [
        [jnp.broadcast_to(gram[:, r * rank + s : r * rank + s + 1], shape) for s in range(r + 1)]
        for r in range(rank)
    ]
    lower, inverse = lower_factor(entries, rank)
    rows = [total[r * pairs : (r + 1) * pairs] for r in range(rank)]
    for r, row in enumerate(solve_rows(rows, lower, inverse)):
        basis_out[:, r, :] = row * math.sqrt(lags)
    stack_out[...] = total[rank * pairs : (rank + 1) * pairs]


def call(kernel, out_shape, in_specs, out_specs, scratch=(), flops=0, moved=0):
    return pl.pallas_call(
        kernel,
        out_shape=out_shape,
        in_specs=in_specs,
        out_specs=out_specs,
        scratch_shapes=list(scratch),
        compiler_params=pltpu.CompilerParams(vmem_limit_bytes=12 * 1024 * 1024),
        cost_estimate=pl.CostEstimate(flops=flops, bytes_accessed=moved, transcendentals=0),
    )


def far(value):
    return pltpu.with_memory_space_constraint(value, pltpu.HBM)


def struct(shape, dtype=F32):
    return jax.ShapeDtypeStruct(shape, dtype)


def on_device(spectra, masks, pair_rows, start_basis):
    stations, windows, seg, parts, freq = spectra.shape
    rank, lags = start_basis.shape
    pairs = pair_rows.shape[0]
    groups = lax.axis_size("pairs")
    group_index = lax.axis_index("pairs")
    slices = lax.axis_size("hours")
    hour = lax.axis_index("hours")
    width = lags // slices
    chips = slices // 2
    forward = [(i, (i + 1) % groups) for i in range(groups)]
    backward = [(target, source) for source, target in forward]
    rows = pair_rows.T
    before = lax.ppermute(rows, "pairs", forward)
    after = lax.ppermute(rows, "pairs", backward)
    place = group_index.reshape(1).astype(jnp.int32)
    whitened = call(
        whiten_kernel,
        [struct((stations, parts * seg, freq), BF16)] * windows,
        [HBM] * 2,
        [VMEM] * windows,
        [
            pltpu.VMEM(spectra.shape, BF16),
            pltpu.VMEM(masks.shape, jnp.int32),
            pltpu.SemaphoreType.DMA((2,)),
        ],
    )(far(spectra), far(masks))
    block = struct((NEAR, parts * seg, freq), BF16)
    def select(wanted, early):
        return call(
            functools.partial(select_kernel, stations),
            [block] * windows,
            [SMEM] + [VMEM] * (2 + windows),
            [VMEM] * windows,
        )(place, early, wanted, *whitened)

    to_next = select(after, whitened[0])
    to_last = select(before, to_next[0])
    lows = [lax.ppermute(one, "pairs", forward) for one in to_next]
    highs = [lax.ppermute(one, "pairs", backward) for one in to_last]
    table, ends = kernel_table(freq, lags)
    fixed = [
        start_basis,
        jnp.asarray(table),
        jnp.asarray(ends),
        jnp.asarray(pick_matrix(pairs, seg, rank)),
        jnp.asarray(spread_matrix(pairs, seg, rank)),
    ]
    *staged, index = call(
        functools.partial(stage_kernel, groups, stations),
        [struct(one.shape, one.dtype) for one in fixed] + [struct(rows.shape, jnp.int32)],
        [SMEM, VMEM] + [HBM] * (len(fixed) + 1),
        [VMEM] * (len(fixed) + 1),
        [
            pltpu.VMEM(start_basis.shape, F32),
            pltpu.VMEM(rows.shape, jnp.int32),
            pltpu.SemaphoreType.DMA((len(fixed) + 1,)),
        ],
        moved=parts * freq * lags,
    )(place, to_next[0], far(rows), *[far(one) for one in fixed])
    core = jnp.mod(hour, 2).reshape(1).astype(jnp.int32)
    chip = (hour // 2).reshape(1).astype(jnp.int32)
    height = -(-(rank + 1) * pairs // 16) * 16
    total_windows = windows * slices
    partial, stacks = None, []
    for w in range(windows):
        last = w == windows - 1
        sizes = (pairs, seg, rank, lags, freq, total_windows, slices, w == 0)
        scratch = [
            pltpu.VMEM((stations + 2 * NEAR, parts * seg, freq), BF16),
            pltpu.VMEM((pairs * seg, parts * freq), BF16),
            pltpu.VMEM((HEAD, lags), F32),
            pltpu.VMEM((HEAD, lags), BF16),
            pltpu.VMEM((HEAD, lags), BF16),
        ]
        args = [index, whitened[w], lows[w], highs[w], *staged]
        specs = [VMEM] * len(args)
        outs = [struct((pairs, lags))]
        if w == 0:
            outs.append(struct((height, lags)))
        else:
            args += [core, partial]
            specs += [SMEM, VMEM]
            outs += [struct((chips, height, width), BF16), struct((chips, height, width))]
        result = call(
            functools.partial(window_kernel, sizes),
            outs,
            specs,
            [VMEM] * len(outs),
            scratch,
            flops=pairs * seg * parts * freq * lags,
            moved=parts * freq * lags,
        )(*args)
        stacks.append(result[0])
        if w == 0:
            partial = result[1]
        else:
            send, keep = result[1:]
    window_stacks = jnp.stack(stacks, 1)
    swap = lambda value, step: lax.ppermute(value, "hours", [(k, k ^ step) for k in range(slices)])
    got = swap(send, 1)
    top = rank * pairs
    message = struct((chips * top + height - top, width), BF16)
    mine, *sends = call(
        functools.partial(add_kernel, top),
        [struct(keep.shape)] + [message] * (chips - 1),
        [SMEM, VMEM, VMEM],
        [VMEM] * chips,
    )(chip, keep, got)
    arrived = [swap(one, 2 * (step + 1)) for step, one in reversed(list(enumerate(sends)))]
    total, gram = call(
        functools.partial(gram_kernel, pairs, rank),
        [struct((height, width)), struct((pairs, 128))],
        [SMEM] + [VMEM] * chips,
        [VMEM] * 2,
        [pltpu.VMEM((chips, top, width), F32)],
    )(chip, mine, *arrived)
    stack, basis = call(
        functools.partial(finish_kernel, pairs, rank, lags),
        [struct((pairs, width)), struct((pairs, rank, width))],
        [VMEM] * 3,
        [VMEM] * 2,
    )(total, gram, swap(gram, 1))
    return (window_stacks, stack, basis)


def solution(mesh):
    in_specs = (
        P("pairs", "hours", None, None, None),
        P("pairs", "hours", None),
        P("pairs", None),
        P(),
    )
    out_specs = (P("pairs", "hours", None), P("pairs", "hours"), P("pairs", None, "hours"))
    return jax.shard_map(
        on_device, mesh=mesh, in_specs=in_specs, out_specs=out_specs, check_vma=False
    )
```

```python
import functools
import math

import jax
import jax.numpy as jnp
import numpy as np
from jax import lax
from jax.experimental import pallas as pl
from jax.experimental.pallas import tpu as pltpu
from jax.sharding import PartitionSpec as P

BAND = 64
TURNS = 2
NEAR = 4
F32 = jnp.float32
BF16 = jnp.bfloat16
VMEM = pl.BlockSpec(memory_space=pltpu.VMEM)
SMEM = pl.BlockSpec(memory_space=pltpu.SMEM)
HBM = pl.BlockSpec(memory_space=pltpu.HBM)
HEAD = 128
LANE = 16


def kernel_table(freq, lags):
    nfft = 2 * lags
    bins = np.arange(1, freq + 1, dtype=np.int64)[:, None]
    shifts = np.append(np.arange(lags // 2, dtype=np.int64), -(lags // 2))[None, :]
    phase = np.mod(bins * shifts, nfft).astype(np.float64) * (2.0 * math.pi / nfft)
    scale = freq ** (-0.5)
    both = np.concatenate([np.cos(phase) * scale, -np.sin(phase) * scale], 0)
    both = both.astype(np.float32).astype(jnp.bfloat16)
    ends = both[:, -1].astype(np.float32).reshape(2, freq)
    return both[:, :-1], ends


def pick_matrix(pairs, seg, rank):
    pick = np.zeros((HEAD, 2 * HEAD), np.float32)
    side = (seg + rank) * LANE
    for pair in range(pairs):
        for part in range(seg):
            pick[pair * seg + part, part * LANE + pair] = 1
            pick[pair * seg + part, side + pair] = 1
    for row in range(rank):
        pick[pairs * seg + row, (seg + row) * LANE : (seg + row + 1) * LANE] = 1
    return pick.astype(jnp.bfloat16)


def spread_matrix(pairs, seg, rank):
    spread = np.zeros((HEAD, (rank + 1) * HEAD), np.float32)
    for row in range(rank + 1):
        for part in range(seg):
            for pair in range(pairs):
                spread[row * LANE + part, row * HEAD + pair * seg + part] = 1
        for other in range(rank):
            spread[row * LANE + seg + other, row * HEAD + pairs * seg + other] = 1
    return spread.astype(jnp.bfloat16)


def two_parts(values):
    high = values.astype(BF16)
    return high, (values - high.astype(F32)).astype(BF16)


def dot(left, right):
    return jnp.dot(left, right, preferred_element_type=F32)


def dot_rows(left, right):
    return lax.dot_general(left, right, (((1,), (1,)), ((), ())), preferred_element_type=F32)


def lower_factor(gram, rank):
    lower = [[None] * rank for _ in range(rank)]
    inverse = [None] * rank
    for row in range(rank):
        for col in range(row + 1):
            total = gram[row][col]
            for inner in range(col):
                total = total - lower[row][inner] * lower[col][inner]
            if row == col:
                inverse[row] = lax.rsqrt(total)
                lower[row][row] = total * inverse[row]
            else:
                lower[row][col] = total * inverse[col]
    return lower, inverse


def solve_rows(rows, lower, inverse):
    result = []
    for row, current in enumerate(rows):
        for inner in range(row):
            current = current - lower[row][inner] * result[inner]
        result.append(current * inverse[row])
    return result


def used_stations(second, low, stations):
    number = lax.broadcasted_iota(jnp.int32, (stations, second.shape[1]), 0)
    return jnp.max(jnp.where(second == low + number, 1.0, 0.0), 1, keepdims=True)


def flip(values):
    rows, width = values.shape
    back = 127 - lax.broadcasted_iota(jnp.int32, (rows, 128), 1)
    turned = []
    for at in range(width - 128, -1, -128):
        turned.append(jnp.take_along_axis(values[:, at : at + 128], back, axis=1))
    return jnp.concatenate(turned, 1)


def first_lane(values, first, other):
    lane = lax.broadcasted_iota(jnp.int32, values, 1)
    return jnp.where(lane == 0, first, other)


def unfold(even, odd):
    shape = even.shape
    root = math.sqrt(2.0)
    right = first_lane(shape, even * root, even + odd)
    left = first_lane(shape, odd * root, even - odd)
    return flip(pltpu.roll(left, shape[1] - 1, 1)), right


def stage_kernel(groups, stations, place, early, far_rows, *refs):
    *refs, index, natural, rows, sems = refs
    count = len(refs) // 2
    sources, targets = refs[:count], refs[count:]
    copies = [
        pltpu.make_async_copy(source, target, sems.at[number])
        for number, (source, target) in enumerate(zip(sources, (natural, *targets[1:])))
    ]
    for copy in copies:
        copy.start()
    known = pltpu.make_async_copy(far_rows, rows, sems.at[count])
    known.start()
    known.wait()
    before = lax.rem(place[0] + groups - 1, groups) * stations
    after = lax.rem(place[0] + 1, groups) * stations
    own = place[0] * stations
    second = rows[1:2]
    in_before = jnp.logical_and(second >= before, second < before + stations)
    in_own = jnp.logical_and(second >= own, second < own + stations)
    local = second - jnp.where(in_before, before, jnp.where(in_own, own, after))
    below = lax.broadcasted_iota(jnp.int32, (stations, second.shape[1]), 0) < local
    slots = [
        jnp.sum(jnp.where(below, used_stations(second, low, stations), 0.0), 0, keepdims=True)
        for low in (before, after)
    ]
    spot = jnp.where(in_own, NEAR + local, NEAR + stations + slots[1].astype(jnp.int32))
    index[0:1] = rows[0:1] - own
    index[1:2] = jnp.where(in_before, slots[0].astype(jnp.int32), spot)
    copies[0].wait()
    values = natural[...]
    half = values.shape[1] // 2
    right = values[:, half:]
    left = pltpu.roll(flip(values[:, :half]), 1, 1)
    shape = right.shape
    root = math.sqrt(0.5)
    targets[0][:, :half] = first_lane(shape, right * root, (right + left) * 0.5)
    targets[0][:, half:] = first_lane(shape, left * root, (right - left) * 0.5)
    for copy in copies[1:]:
        copy.wait()


def whiten_kernel(far_spectra, far_masks, *refs):
    whitened, (spectra, masks, sems) = refs[:-3], refs[-3:]
    stations, windows, seg, _, freq = spectra.shape
    small = [pltpu.make_async_copy(far_masks, masks, sems.at[0])]
    large = [pltpu.make_async_copy(far_spectra, spectra, sems.at[1])]
    for copy in small + large:
        copy.start()
    tile = (128, 128)
    same = lax.broadcasted_iota(jnp.int32, tile, 0) // BAND == lax.broadcasted_iota(jnp.int32, tile, 1) // BAND
    bands = jnp.where(same, 1.0, 0.0).astype(BF16)
    for copy in small:
        copy.wait()
    eye = lax.broadcasted_iota(jnp.int32, (seg, seg), 0) == lax.broadcasted_iota(jnp.int32, (seg, seg), 1)
    open_rows = []
    for station in range(stations):
        for window in range(windows):
            mask = masks[station, window : window + 1].astype(F32)
            mask = jnp.where(eye, jnp.broadcast_to(mask, (seg, seg)), 0.0)
            open_rows.append(jnp.sum(mask, 1, keepdims=True))
    large[0].wait()
    values, squares = [], []
    for station in range(stations):
        for window in range(windows):
            block = spectra[station, window].astype(F32)
            real, imag = block[:, 0], block[:, 1]
            values.append((real, imag))
            squares.append(real * real + imag * imag)
    height = len(values) * seg
    squares = jnp.concatenate(squares, 0)
    here = jnp.concatenate(open_rows, 0)
    scales = []
    for at in range(0, freq, 128):
        power = dot(jnp.concatenate(two_parts(squares[:, at : at + 128]), 1), jnp.concatenate([bands, bands], 0))
        scales.append(lax.rsqrt(power * (1.0 / (2 * BAND)) + 1e-06) * here)
    scale = jnp.concatenate(scales, 1)
    for number, (real, imag) in enumerate(values):
        here = scale[number * seg : (number + 1) * seg]
        block = jnp.concatenate([real * here, imag * here], 0).astype(BF16)
        whitened[number % windows][number // windows] = block


def select_kernel(stations, place, early, rows, *refs):
    windows = len(refs) // 2
    used = used_stations(rows[1:2], place[0] * stations, stations)
    weight = jnp.left_shift(1, lax.broadcasted_iota(jnp.int32, (stations, 1), 0)).astype(F32)
    needed = jnp.sum(used * weight).astype(jnp.int32)
    for slot in range(NEAR):
        lowest = jnp.bitwise_and(needed, -needed)
        station = jnp.int32(0)
        for number in range(1, stations):
            station = station + jnp.where(lowest >= (1 << number), 1, 0)
        for source, target in zip(refs[:windows], refs[windows:]):
            target[slot] = source[station]
        needed = needed - lowest


def window_kernel(sizes, index, own, low, high, start, table, ends, pick, spread, *refs):
    pairs, seg, rank, lags, freq, total_windows, slices, first_window = sizes
    rows = pairs * seg
    if first_window:
        win_out, merged_out, near, cross, vectors, high_part, low_part = refs
    else:
        (core, partial, win_out, send_out, keep_out, near, cross, vectors, high_part, low_part) = refs
    stations = own.shape[0]
    half = lags // 2
    picked = index[...]
    near[0:NEAR] = low[...]
    near[NEAR : NEAR + stations] = own[...]
    near[NEAR + stations :] = high[...]
    edges = []
    for pair in range(0, pairs, 2):
        real, imag = [], []
        for one in (pair, pair + 1):
            a = own[picked[0, one]].astype(F32)
            b = near[picked[1, one]].astype(F32)
            a_re, a_im, b_re, b_im = a[:seg], a[seg:], b[:seg], b[seg:]
            real.append(a_re * b_re + a_im * b_im)
            imag.append(a_im * b_re - a_re * b_im)
        block = pl.ds(pair * seg, 2 * seg)
        real = jnp.concatenate(real, 0).astype(BF16)
        imag = jnp.concatenate(imag, 0).astype(BF16)
        cross[block, 0:freq] = real
        cross[block, freq:] = imag
        last = real.astype(F32) * ends[0:1] + imag.astype(F32) * ends[1:2]
        edges.append(jnp.sum(last, 1, keepdims=True))
    vectors[rows : rows + rank] = start[...]
    vectors[rows + rank :] = jnp.zeros((HEAD - rows - rank, lags), F32)
    step = 512
    for at in range(0, half, step):
        for part in (0, 1):
            block = cross[:, part * freq : (part + 1) * freq]
            block = jnp.concatenate([block, block[0 : HEAD - rows]], 0)
            block = dot(block, table[part * freq : (part + 1) * freq, at : at + step])
            vectors[0:rows, part * half + at : part * half + at + step] = block[0:rows]
    shape = (rows, 128)
    root = math.sqrt(0.5)
    column = vectors[0:rows, 0:128]
    vectors[0:rows, 0:128] = first_lane(shape, column * root, column)
    edge = jnp.broadcast_to(jnp.concatenate(edges, 0) * root, shape)
    vectors[0:rows, half : half + 128] = first_lane(shape, edge, vectors[0:rows, half : half + 128])
    every = vectors[...]
    high_part[...] = every.astype(BF16)
    low_part[...] = (every - high_part[...].astype(F32)).astype(BF16)
    gram = dot_rows(high_part[...], high_part[...])
    side = dot_rows(low_part[...], high_part[...])
    gram = 2.0 * (gram + side + side.T)
    lane = lax.broadcasted_iota(jnp.int32, (seg, HEAD), 1)
    sub = lax.broadcasted_iota(jnp.int32, (seg, HEAD), 0)
    blocks = jnp.zeros((seg, HEAD), F32)
    for pair in range(pairs):
        blocks = blocks + jnp.where(lane // seg == pair, gram[pair * seg : (pair + 1) * seg], 0.0)
    basis_rows = gram[rows : rows + 8]
    turned = [
        jnp.where(lane % seg == sub, jnp.broadcast_to(basis_rows[row : row + 1], (seg, HEAD)), 0.0)
        for row in range(rank)
    ]
    stacked = jnp.concatenate([blocks, basis_rows] + turned, 0)
    count = stacked.shape[0]
    moved = dot(jnp.concatenate(two_parts(stacked), 0), pick[...])
    moved = moved[0:count] + moved[count:]
    products = [moved[0:16, k * LANE : (k + 1) * LANE] for k in range(seg)]
    side_at = (seg + rank) * LANE
    for row in range(rank):
        upper = moved[16 + row * seg : 16 + (row + 1) * seg, side_at : side_at + LANE]
        under = moved[8:16, (seg + row) * LANE : (seg + row + 1) * LANE]
        products.append(jnp.concatenate([upper, under], 0))
    level = lax.broadcasted_iota(jnp.int32, (16, LANE), 0)
    of_corr = level < seg
    known = [jnp.where(level == seg + row, 1.0, 0.0) for row in range(rank)]
    reach = [jnp.where(of_corr, products[seg + row], 0.0) for row in range(rank)]
    for turn in range(TURNS):
        known = [known[r] + reach[r] * (1.0 / lags) for r in range(rank)]
        images = []
        for r in range(rank):
            image = known[r][0:1] * products[0]
            for k in range(1, seg + rank):
                image = image + known[r][k : k + 1] * products[k]
            images.append(image)
        inner = [
            [jnp.sum(images[r] * known[s], 0, keepdims=True) for s in range(r + 1)] for r in range(rank)
        ]
        lower, inverse = lower_factor(inner, rank)
        known = solve_rows(known, lower, inverse)
        reach = [jnp.where(of_corr, v, 0.0) for v in solve_rows(images, lower, inverse)]
    outs = [reach[r] + float(lags) * known[r] for r in range(rank)]
    window = jnp.zeros_like(known[0])
    for r in range(rank):
        window = window + jnp.sum(reach[r], 0, keepdims=True) * known[r]
    outs.append(window * (1.0 / math.sqrt(seg)))
    coefs = jnp.concatenate(outs + [jnp.zeros((HEAD - (rank + 1) * 16, LANE), F32)], 0)
    coefs = jnp.concatenate([coefs, jnp.zeros((HEAD, HEAD - LANE), F32)], 1).T[0:LANE]
    wide = dot(jnp.concatenate(two_parts(coefs), 0), spread[...])
    wide = wide[0:LANE] + wide[LANE:]
    row_of = lax.broadcasted_iota(jnp.int32, (LANE, HEAD), 0)
    lane_of = lax.broadcasted_iota(jnp.int32, (LANE, HEAD), 1)
    mine = jnp.logical_or(lane_of // seg == row_of, lane_of >= rows)
    weights = [
        jnp.where(mine, wide[:, r * HEAD : (r + 1) * HEAD], 0.0)[0:pairs] for r in range(rank + 1)
    ]
    filled = (rank + 1) * pairs
    height = -(-filled // 16) * 16
    weights = jnp.concatenate(weights + [jnp.zeros((height - filled, HEAD), F32)], 0)
    w_high, w_low = two_parts(weights)
    both = jnp.concatenate([w_high, w_low], 0)
    scale = 1.0 / math.sqrt(total_windows)
    width = lags // slices
    top = rank * pairs

    def combined(at):
        part = dot(both, high_part[:, at : at + step])
        return part[0:height] + part[height:] + dot(w_high, low_part[:, at : at + step])

    result = [jnp.concatenate([combined(side + at) for at in range(0, half, step)], 1) for side in (0, half)]
    left, right = unfold(*[one[top:] for one in result])
    win_out[:, 0:half] = left[0:pairs]
    win_out[:, half:] = right[0:pairs]
    result = [jnp.concatenate([one[0:top], one[top:] * scale], 0) for one in result]
    if first_window:
        merged_out[:, 0:half] = result[0]
        merged_out[:, half:] = result[1]
    else:
        left, right = unfold(result[0] + partial[:, 0:half], result[1] + partial[:, half:])
        swapped = core[0] == 1
        for piece in range(slices // 2):
            side, at = (left, right)[piece // (slices // 4)], 2 * piece * width % half
            one, two = side[:, at : at + width], side[:, at + width : at + 2 * width]
            send_out[piece] = jnp.where(swapped, one, two).astype(BF16)
            keep_out[piece] = jnp.where(swapped, two, one)


def add_kernel(top, chip, keep, got, mine_out, *sends):
    chips, height, _ = keep.shape
    for part in range(chips):
        both = keep[part] + got[part].astype(F32)
        mine_out[part] = both
        short = both[0:top].astype(BF16)
        for out in sends:
            out[part * top : (part + 1) * top] = short
    for step, out in enumerate(sends):
        other = jnp.bitwise_xor(chip[0], step + 1)
        out[chips * top :] = mine_out[other, top:height].astype(BF16)


def gram_kernel(pairs, rank, chip, mine, *refs):
    got, (total_out, gram_out, parts) = refs[:-3], refs[-3:]
    chips, height, width = mine.shape
    top = rank * pairs
    sums = [[jnp.zeros((pairs, width), F32) for _ in range(r + 1)] for r in range(rank)]
    for part in range(chips):
        block = mine[part, 0:top].astype(BF16).astype(F32)
        for one in got:
            block = block + one[part * top : (part + 1) * top].astype(F32)
        parts[part] = block
        rows = [block[r * pairs : (r + 1) * pairs] for r in range(rank)]
        sums = [[sums[r][s] + rows[r] * rows[s] for s in range(r + 1)] for r in range(rank)]
    stack = mine[chip[0], top:height]
    for one in got:
        stack = stack + one[chips * top :].astype(F32)
    total_out[0:top] = parts[chip[0]]
    total_out[top:] = stack
    lane = lax.broadcasted_iota(jnp.int32, (pairs, 128), 1)
    gram = jnp.zeros((pairs, 128), F32)
    for r in range(rank):
        for s in range(r + 1):
            value = jnp.sum(sums[r][s], 1, keepdims=True)
            gram = jnp.where(lane == r * rank + s, value, gram)
    gram_out[...] = gram


def finish_kernel(pairs, rank, lags, total, mine, got, stack_out, basis_out):
    gram = mine[...] + got[...]
    shape = (pairs, total.shape[1])
    entries = [
        [jnp.broadcast_to(gram[:, r * rank + s : r * rank + s + 1], shape) for s in range(r + 1)]
        for r in range(rank)
    ]
    lower, inverse = lower_factor(entries, rank)
    rows = [total[r * pairs : (r + 1) * pairs] for r in range(rank)]
    for r, row in enumerate(solve_rows(rows, lower, inverse)):
        basis_out[:, r, :] = row * math.sqrt(lags)
    stack_out[...] = total[rank * pairs : (rank + 1) * pairs]


def call(kernel, out_shape, in_specs, out_specs, scratch=(), flops=0, moved=0):
    return pl.pallas_call(
        kernel,
        out_shape=out_shape,
        in_specs=in_specs,
        out_specs=out_specs,
        scratch_shapes=list(scratch),
        compiler_params=pltpu.CompilerParams(vmem_limit_bytes=12 * 1024 * 1024),
        cost_estimate=pl.CostEstimate(flops=flops, bytes_accessed=moved, transcendentals=0),
    )


def far(value):
    return pltpu.with_memory_space_constraint(value, pltpu.HBM)


def struct(shape, dtype=F32):
    return jax.ShapeDtypeStruct(shape, dtype)


def on_device(spectra, masks, pair_rows, start_basis):
    stations, windows, seg, parts, freq = spectra.shape
    rank, lags = start_basis.shape
    pairs = pair_rows.shape[0]
    groups = lax.axis_size("pairs")
    group_index = lax.axis_index("pairs")
    slices = lax.axis_size("hours")
    hour = lax.axis_index("hours")
    width = lags // slices
    chips = slices // 2
    forward = [(i, (i + 1) % groups) for i in range(groups)]
    backward = [(target, source) for source, target in forward]
    rows = pair_rows.T
    before = lax.ppermute(rows, "pairs", forward)
    after = lax.ppermute(rows, "pairs", backward)
    place = group_index.reshape(1).astype(jnp.int32)
    whitened = call(
        whiten_kernel,
        [struct((stations, parts * seg, freq), BF16)] * windows,
        [HBM] * 2,
        [VMEM] * windows,
        [
            pltpu.VMEM(spectra.shape, BF16),
            pltpu.VMEM(masks.shape, jnp.int32),
            pltpu.SemaphoreType.DMA((2,)),
        ],
    )(far(spectra), far(masks))
    block = struct((NEAR, parts * seg, freq), BF16)
    def select(wanted, early):
        return call(
            functools.partial(select_kernel, stations),
            [block] * windows,
            [SMEM] + [VMEM] * (2 + windows),
            [VMEM] * windows,
        )(place, early, wanted, *whitened)

    to_next = select(after, whitened[0])
    to_last = select(before, to_next[0])
    lows = [lax.ppermute(one, "pairs", forward) for one in to_next]
    highs = [lax.ppermute(one, "pairs", backward) for one in to_last]
    table, ends = kernel_table(freq, lags)
    fixed = [
        start_basis,
        jnp.asarray(table),
        jnp.asarray(ends),
        jnp.asarray(pick_matrix(pairs, seg, rank)),
        jnp.asarray(spread_matrix(pairs, seg, rank)),
    ]
    *staged, index = call(
        functools.partial(stage_kernel, groups, stations),
        [struct(one.shape, one.dtype) for one in fixed] + [struct(rows.shape, jnp.int32)],
        [SMEM, VMEM] + [HBM] * (len(fixed) + 1),
        [VMEM] * (len(fixed) + 1),
        [
            pltpu.VMEM(start_basis.shape, F32),
            pltpu.VMEM(rows.shape, jnp.int32),
            pltpu.SemaphoreType.DMA((len(fixed) + 1,)),
        ],
        moved=parts * freq * lags,
    )(place, to_next[0], far(rows), *[far(one) for one in fixed])
    core = jnp.mod(hour, 2).reshape(1).astype(jnp.int32)
    chip = (hour // 2).reshape(1).astype(jnp.int32)
    height = -(-(rank + 1) * pairs // 16) * 16
    total_windows = windows * slices
    partial, stacks = None, []
    for w in range(windows):
        last = w == windows - 1
        sizes = (pairs, seg, rank, lags, freq, total_windows, slices, w == 0)
        scratch = [
            pltpu.VMEM((stations + 2 * NEAR, parts * seg, freq), BF16),
            pltpu.VMEM((pairs * seg, parts * freq), BF16),
            pltpu.VMEM((HEAD, lags), F32),
            pltpu.VMEM((HEAD, lags), BF16),
            pltpu.VMEM((HEAD, lags), BF16),
        ]
        args = [index, whitened[w], lows[w], highs[w], *staged]
        specs = [VMEM] * len(args)
        outs = [struct((pairs, lags))]
        if w == 0:
            outs.append(struct((height, lags)))
        else:
            args += [core, partial]
            specs += [SMEM, VMEM]
            outs += [struct((chips, height, width), BF16), struct((chips, height, width))]
        result = call(
            functools.partial(window_kernel, sizes),
            outs,
            specs,
            [VMEM] * len(outs),
            scratch,
            flops=pairs * seg * parts * freq * lags,
            moved=parts * freq * lags,
        )(*args)
        stacks.append(result[0])
        if w == 0:
            partial = result[1]
        else:
            send, keep = result[1:]
    window_stacks = jnp.stack(stacks, 1)
    swap = lambda value, step: lax.ppermute(value, "hours", [(k, k ^ step) for k in range(slices)])
    got = swap(send, 1)
    top = rank * pairs
    message = struct((chips * top + height - top, width), BF16)
    mine, *sends = call(
        functools.partial(add_kernel, top),
        [struct(keep.shape)] + [message] * (chips - 1),
        [SMEM, VMEM, VMEM],
        [VMEM] * chips,
    )(chip, keep, got)
    arrived = [swap(one, 2 * (step + 1)) for step, one in reversed(list(enumerate(sends)))]
    total, gram = call(
        functools.partial(gram_kernel, pairs, rank),
        [struct((height, width)), struct((pairs, 128))],
        [SMEM] + [VMEM] * chips,
        [VMEM] * 2,
        [pltpu.VMEM((chips, top, width), F32)],
    )(chip, mine, *arrived)
    stack, basis = call(
        functools.partial(finish_kernel, pairs, rank, lags),
        [struct((pairs, width)), struct((pairs, rank, width))],
        [VMEM] * 3,
        [VMEM] * 2,
    )(total, gram, swap(gram, 1))
    return (window_stacks, stack, basis)


def solution(mesh):
    in_specs = (
        P("pairs", "hours", None, None, None),
        P("pairs", "hours", None),
        P("pairs", None),
        P(),
    )
    out_specs = (P("pairs", "hours", None), P("pairs", "hours"), P("pairs", None, "hours"))
    return jax.shard_map(
        on_device, mesh=mesh, in_specs=in_specs, out_specs=out_specs, check_vma=False
    )
```
